512 devices in a mesh: tm: 64 (over z, x, y_hi), head: 8 (over y_lo, core).
Axes of the slice: x: 4, y: 8 (y_hi: 2, y_lo: 4; y = y_hi * 4 + y_lo), z: 8, core: 2. Of those that a mesh axis runs over, the one named last changes fastest.
Arguments:
- queries: bfloat16 [8192, 8192], P(('tm', 'head')), may hold values from -160 to 160
- vis_keys: bfloat16 [16384, 1024], P('tm', 'head'), may hold values from -15 to 15
- vis_values: bfloat16 [16384, 1024], P('tm', 'head'), may hold values from -6 to 6
- span_start: int32 [8192], P('tm'), may hold values from 0 to 63, as said below
- span_end: int32 [8192], P('tm'), may hold values from 0 to 63, as said below
Outputs:
- context: bfloat16 [8192, 8192], P(('tm', 'head'))
The draws below stay inside these ranges and needn't reach their ends.
Inputs may be any that keep to these rules, and one draw needn't show every extreme that they name: Row r's span [span_start[r], span_end[r]] holds 1 to 6 shards and contains the row's own shard r // 128; some row reaches 6 shards. span_end[r] >= span_start[r], as described for span_start.
All inputs are finite; a program needn't handle non-finite values.
Results may differ from the reference program's by a relative error of at most 0.004.
Values may be sent and summed in bfloat16 or wider, within the bound.
A program may use at most 64 MiB of HBM per device.

```python
import math
import jax
import jax.numpy as jnp
from jax import lax

HEADS = 64
KV_HEADS = 8
HEAD_DIM = 128
VIS_DEV = 256
SPAN = 6
ROWS_TM = 128
ROWS = 8192
VIS = 16384


def key_base(key):
    raw = jax.random.normal(jax.random.fold_in(key, 11), (VIS, KV_HEADS, HEAD_DIM), jnp.float32) * 2.5
    return jnp.clip(raw, -15.0, 15.0)


def span_pair(key):
    group_count = ROWS // ROWS_TM
    split_keys = jax.random.split(jax.random.fold_in(key, 13), 4)
    caps = jax.random.randint(split_keys[0], (group_count,), 1, SPAN + 1)
    chosen = jax.random.randint(split_keys[1], (), 0, group_count)
    caps = jnp.where(jnp.arange(group_count) == chosen, SPAN, caps).astype(jnp.int32)
    row_ids = jnp.arange(ROWS, dtype=jnp.int32)
    group_of = row_ids // ROWS_TM
    slot_of = row_ids % ROWS_TM
    cap_row = caps[group_of]
    length = jax.random.randint(split_keys[2], (ROWS,), 0, 720) % cap_row + 1
    place = jax.random.randint(split_keys[3], (ROWS,), 0, 720) % length
    length = jnp.where(slot_of < 2, cap_row, length)
    place = jnp.where(slot_of == 0, length - 1, jnp.where(slot_of == 1, 0, place))
    start = jnp.clip(group_of - place, 0, group_count - length)
    finish = start + length - 1
    return (start.astype(jnp.int32), finish.astype(jnp.int32))


def draw_queries(key, part):
    key = jax.random.fold_in(key, 5)
    raw = jnp.clip(jax.random.normal(key, (ROWS, HEADS, HEAD_DIM), jnp.float32), -6.0, 6.0)
    return raw.reshape(ROWS, HEADS * HEAD_DIM).astype(jnp.bfloat16)


def draw_vis_keys(key, part):
    base = key_base(key)
    return base.reshape(VIS, KV_HEADS * HEAD_DIM).astype(jnp.bfloat16)


def draw_span_start(key, part):
    pair = span_pair(key)
    return pair[0]


def draw_span_end(key, part):
    pair = span_pair(key)
    return pair[1]


def block_scale(stream_key, extent, cuts, least, top_value):
    level = 1.0
    for position, parts in cuts:
        steps = jax.random.uniform(jax.random.fold_in(jax.random.fold_in(stream_key, 6), position), (parts,), jnp.float32, least / len(cuts), top_value / len(cuts))
        level = level * jnp.repeat(jnp.exp(steps), extent[position] // parts).reshape((-1,) + (1,) * (len(extent) - 1 - position))
    return level


def gaussian(key, dims, deviation, reach, cuts=(), kind=jnp.bfloat16):
    level = block_scale(key, dims, cuts, -0.22, 0.18) if cuts else 1.0
    values = jax.random.normal(key, dims, jnp.float32) * deviation * level
    return jnp.minimum(jnp.maximum(values, -reach), reach).astype(kind)


def setup_inputs(seed: int = 0) -> dict:
    keys = jax.random.split(jax.random.key(seed), 6)
    return {
        "queries": draw_queries(jax.random.fold_in(keys[5], 71), 0),
        "vis_keys": draw_vis_keys(jax.random.fold_in(keys[5], 71), 0),
        "vis_values": gaussian(keys[2], (VIS, KV_HEADS * HEAD_DIM), 1.0, 6.0, ((0, 64), (1, 8))),
        "span_start": draw_span_start(jax.random.fold_in(keys[5], 71), 0),
        "span_end": draw_span_end(jax.random.fold_in(keys[5], 71), 0),
    }


def reference(queries, vis_keys, vis_values, span_start, span_end):
    group_size = HEADS // KV_HEADS
    max_offset = SPAN - 1
    group_count = ROWS // ROWS_TM
    window_len = (2 * max_offset + 1) * VIS_DEV
    padding = jnp.zeros((max_offset * VIS_DEV, KV_HEADS * HEAD_DIM), vis_keys.dtype)
    padded_keys = jnp.concatenate([padding, vis_keys, padding], axis=0)
    padded_values = jnp.concatenate([padding, vis_values, padding], axis=0)

    def per_group(group_index):
        group_index = group_index.astype(jnp.int32)
        row_first = (group_index * ROWS_TM).astype(jnp.int32)
        token_first = (group_index * VIS_DEV).astype(jnp.int32)
        query_block = lax.dynamic_slice_in_dim(queries, row_first, ROWS_TM, 0).astype(jnp.float32)
        query_block = query_block.reshape(ROWS_TM, KV_HEADS, group_size, HEAD_DIM)
        key_block = lax.dynamic_slice_in_dim(padded_keys, token_first, window_len, 0).astype(jnp.float32)
        key_block = key_block.reshape(window_len, KV_HEADS, HEAD_DIM)
        value_block = lax.dynamic_slice_in_dim(padded_values, token_first, window_len, 0).astype(jnp.float32)
        value_block = value_block.reshape(window_len, KV_HEADS, HEAD_DIM)
        starts = lax.dynamic_slice_in_dim(span_start, row_first, ROWS_TM, 0)
        finishes = lax.dynamic_slice_in_dim(span_end, row_first, ROWS_TM, 0)
        shard_index = group_index - max_offset + jnp.arange(window_len, dtype=jnp.int32) // VIS_DEV
        in_span = (starts[:, None] <= shard_index[None, :]) & (shard_index[None, :] <= finishes[:, None])
        in_span = in_span[:, None, None, :]
        scores = jnp.einsum('rjgd,kjd->rjgk', query_block, key_block) / math.sqrt(HEAD_DIM)
        scores = jnp.where(in_span, scores, -jnp.inf)
        row_max = lax.optimization_barrier(jnp.max(scores, axis=-1, keepdims=True))
        weights = jnp.where(in_span, jnp.exp(scores - row_max), 0.0)
        denominator = lax.optimization_barrier(jnp.sum(weights, axis=-1))
        rounded = weights.astype(jnp.bfloat16).astype(jnp.float32)
        context = jnp.einsum('rjgk,kjd->rjgd', rounded, value_block) / denominator[..., None]
        return context.reshape(ROWS_TM, HEADS * HEAD_DIM).astype(jnp.bfloat16)
    blocks = lax.map(per_group, jnp.arange(group_count, dtype=jnp.int32))
    return blocks.reshape(ROWS, HEADS * HEAD_DIM)
```

```python
import functools
import math

import jax
import jax.numpy as jnp
from jax import lax
from jax.experimental import pallas as pl
from jax.experimental.pallas import tpu as pltpu
from jax.sharding import PartitionSpec as P

HEADS = 64
KV_HEADS = 8
HEAD_DIM = 128
MESH = pl.DeviceIdType.MESH
GROUP = HEADS // KV_HEADS
RATE = math.log2(math.e) / math.sqrt(HEAD_DIM)
FAR = 1e30

OWN = {0: 0, -1: 1, 1: 2, -2: 3, 2: 4}
PAIR = {0: 5, -1: 6, 1: 7, -2: 8, 2: 9}
EDGE, SLOTS = 10, 11


class Move:
    def __init__(self, copies, arrives):
        self.copies, self.arrives = copies, arrives

    def start(self):
        for sends, copy in self.copies:
            pl.when(sends)(copy.start)

    def wait_recv(self):
        pl.when(self.arrives)(self.copies[0][1].wait_recv)

    def wait_send(self):
        for sends, copy in self.copies:
            pl.when(sends)(copy.wait_send)


def kernel(
    groups, q_hbm, k_hbm, v_hbm, first_hbm, last_hbm, out_ref, first_ref, last_ref,
    q_buf, k_buf, v_buf, v_rows, total, peak, first, last, ready,
    local_sem, q_send, q_recv, k_send, k_recv, v_send, v_recv, o_send, o_recv,
):
    t = lax.axis_index("tm")
    h = lax.axis_index("head")
    pair, parity = t // 2, t % 2
    side = 1 - 2 * parity
    x, z = pair % 4, pair // 4
    chip, core = h // 2, h % 2
    rows, width = q_buf.shape[1:]
    tokens = k_buf.shape[1]

    opposite_x = {"tm": 8 * z + 2 * ((x + 2) % 4) + parity, "head": h}

    def at_pair(distance):
        return {"tm": (t + groups + 2 * distance) % groups, "head": h}

    def flip(value):
        return value + 1 - 2 * (value % 2)

    def chunk_of(ring):
        start = chip if ring < 2 else (chip + 2) % 4
        return start if ring % 2 == 0 else flip(start)

    def columns(head):
        return pl.ds(pl.multiple_of(head * width, width), width)

    def remote(source, target, send, recv, device):
        return pltpu.make_async_remote_copy(
            source, target, send, recv, device_id=device, device_id_type=MESH
        )

    def head_of(ring, other):
        return 2 * chunk_of(ring) + (core if other == 0 else 1 - core)

    near = [(1, 0), (1, 1), (0, 1)]
    distant = [(2, 0), (2, 1), (3, 0), (3, 1)]
    mates = distant + near

    def q_copy(ring, other):
        target = head_of(ring, other)
        index = 2 * ring + other
        return remote(
            q_hbm.at[:, columns(target)], q_buf.at[h], q_send.at[index], q_recv.at[index],
            {"tm": t, "head": target},
        )

    def k_copy(source, target, role, device):
        return remote(source, target, k_send.at[role], k_recv.at[role], device)

    def v_copy(source, target, role, device):
        return remote(source, target, v_send.at[role], v_recv.at[role], device)

    k_load = pltpu.make_async_copy(k_hbm, k_buf.at[OWN[0]], local_sem.at[0])
    v_load = pltpu.make_async_copy(v_hbm, v_rows, local_sem.at[1])
    q_load = pltpu.make_async_copy(q_hbm.at[:, columns(h)], q_buf.at[h], local_sem.at[2])
    span_loads = [
        pltpu.make_async_copy(first_hbm, first_ref, local_sem.at[4]),
        pltpu.make_async_copy(last_hbm, last_ref, local_sem.at[5]),
    ]
    pairs = groups // 2
    at_start, at_end = z == 0, z == pairs // 4 - 1

    def has(distance):
        return (pair >= -distance) if distance < 0 else (pair < pairs - distance)

    barrier = pltpu.get_barrier_semaphore()
    everywhere = [{"tm": t + side, "head": h}, opposite_x]
    everywhere += [{"tm": t, "head": head_of(*mate)} for mate in mates]
    for partner in everywhere:
        pl.semaphore_signal(barrier, inc=1, device_id=partner, device_id_type=MESH)
    answers = len(everywhere)
    corner = jnp.where(parity == 0, pair == 0, pair == pairs - 1)
    cornered = jnp.where(parity == 0, pair == 3, pair == pairs - 4)
    others = [(has(distance), at_pair(distance)) for distance in (1, -1, 4, -4)]
    others += [(corner, at_pair(3 * side)), (cornered, at_pair(-3 * side))]
    for present, partner in others:
        answers = answers + jnp.where(present, 1, 0)

        @pl.when(present)
        def _(partner=partner):
            pl.semaphore_signal(barrier, inc=1, device_id=partner, device_id_type=MESH)

    for load in (v_load, k_load, *span_loads, q_load):
        load.start()

    low = x < 2
    to_next, to_last = jnp.logical_not(at_end), jnp.logical_not(at_start)

    def pick(base, condition, distance):
        return jnp.where(condition, base[distance], base[-distance])

    def spread(copy, buf, base, role, source):
        moves = {
            e: Move(
                [(has(e), copy(source, buf.at[base[-e]], role + i, at_pair(e)))],
                has(-e),
            )
            for i, e in enumerate((1, -1))
        }
        moves["x"] = copy(source, buf.at[pick(base, low, -2)], role + 2, opposite_x)
        along = copy(
            buf.at[pick(base, low, 2)], buf.at[pick(base, low, -2)], role + 3,
            at_pair(jnp.where(low, 4, -4)),
        )
        moves["z"] = Move(
            [(jnp.where(low, to_next, to_last), along)], jnp.where(low, to_last, to_next)
        )
        return moves

    def edge(copy, buf):
        up = parity == 0
        along = copy(
            buf.at[pick(PAIR, up, 1)], buf.at[EDGE], 9, at_pair(4 * side)
        )
        direct = copy(buf.at[PAIR[0]], buf.at[EDGE], 9, at_pair(3 * side))
        return Move(
            [(jnp.where(up, to_next, to_last), along), (corner, direct)],
            jnp.where(up, to_last | (x == 3), to_next | (x == 0)),
        )

    across = {"tm": t + side, "head": h}
    k_pair = k_copy(k_hbm, k_buf.at[PAIR[0]], 0, across)
    v_pair = v_copy(v_buf.at[OWN[0]], v_buf.at[PAIR[0]], 0, across)
    k_own = spread(k_copy, k_buf, OWN, 1, k_hbm)
    v_own = spread(v_copy, v_buf, OWN, 1, v_buf.at[OWN[0]])
    k_other = spread(k_copy, k_buf, PAIR, 5, k_buf.at[PAIR[0]])
    v_other = spread(v_copy, v_buf, PAIR, 5, v_buf.at[PAIR[0]])
    k_edge, v_edge = edge(k_copy, k_buf), edge(v_copy, v_buf)
    q_moves = {mate: q_copy(*mate) for mate in mates}

    pl.semaphore_wait(barrier, answers)

    first_steps = (1, -1, "x")
    k_pair.start()
    for step in first_steps:
        k_own[step].start()
    q_moves[0, 1].start()
    v_load.wait()
    v_buf[OWN[0]] = v_rows[...].T
    k_pair.wait_send()
    v_pair.start()
    for step in first_steps:
        v_own[step].start()

    unused = [(base[d], jnp.logical_not(has(d))) for base in (OWN, PAIR) for d in (1, -1, 2, -2)]
    unused.append((EDGE, jnp.logical_not(jnp.where(parity == 0, has(-3), has(3)))))
    for slot, empty in unused:
        @pl.when(empty)
        def _(slot=slot):
            k_buf[slot] = jnp.zeros(k_buf.shape[1:], k_buf.dtype)
            v_buf[slot] = jnp.zeros(v_buf.shape[1:], v_buf.dtype)

    for load in span_loads:
        load.wait()
    lane = lax.broadcasted_iota(jnp.int32, (128, 256), 1)
    row = lax.broadcasted_iota(jnp.int32, (128, 256), 0)
    for c in range(4):
        wanted = c * 32 + (lane // 128) * 16 + lane % 16
        chosen = jnp.where(row == wanted, 1.0, 0.0).astype(jnp.bfloat16)
        for ref, held in ((first_ref, first), (last_ref, last)):
            offset_row = (ref[...] - t).astype(jnp.float32)
            offset_row = jnp.broadcast_to(offset_row, (16, 128)).astype(jnp.bfloat16)
            placed = jnp.dot(offset_row, chosen, preferred_element_type=jnp.float32)
            held[c] = placed[0:1]

    def offset(slot):
        for base, shift in ((OWN, 0), (PAIR, side)):
            for distance, index in base.items():
                if index == slot:
                    return 2 * distance + shift
        return -5 * side

    def absorb(c, start, stop, fresh):
        queries = jnp.concatenate(
            [
                q_buf[2 * c + b, :, g * HEAD_DIM:(g + 1) * HEAD_DIM]
                for b in range(2)
                for g in range(GROUP)
            ],
            axis=0,
        )
        begin, finish = first[c], last[c]
        keys = k_buf[start:stop].reshape((stop - start) * tokens, HEAD_DIM)
        scores = lax.dot_general(
            keys, queries, (((1,), (1,)), ((), ())), preferred_element_type=jnp.float32
        )
        scores = [scores[i * tokens:(i + 1) * tokens] for i in range(stop - start)]
        inside, best = [], []
        for slot, score in zip(range(start, stop), scores):
            place = jnp.asarray(offset(slot), jnp.int32).astype(jnp.float32)
            within = (begin <= place) & (place <= finish)
            inside.append(within)
            best.append(jnp.where(within, jnp.max(score, axis=0, keepdims=True), -FAR))
        top = functools.reduce(jnp.maximum, best)
        if not fresh:
            before = peak[c]
            top = jnp.maximum(before, top)
        peak[c] = top
        weights = [
            jnp.exp2((score - jnp.where(within, top, FAR)) * RATE).astype(jnp.bfloat16)
            for score, within in zip(scores, inside)
        ]
        weights = jnp.concatenate(weights, axis=0)
        left = jnp.concatenate([v_buf[slot] for slot in range(start, stop)], axis=1)
        ones = jnp.ones((16, left.shape[1]), jnp.bfloat16)
        left = jnp.concatenate([left, ones], axis=0)
        gained = jnp.dot(left, weights, preferred_element_type=jnp.float32)
        if not fresh:
            gained = gained + total[c] * jnp.exp2((before - top) * RATE)
        return gained

    def visit(rings, start, stop, fresh):
        for ring in rings:
            c = chunk_of(ring)
            total[c] = absorb(c, start, stop, fresh)

    def visit_all(begin, count, start, stop, fresh):
        def body(i, carry):
            c = (begin + 2 * (i // 2)) % 4
            c = c + (i % 2) * (1 - 2 * (c % 2))
            total[c] = absorb(c, start, stop, fresh)
            return carry

        lax.fori_loop(0, count, body, 0)

    k_own["x"].wait_recv()
    k_own["z"].start()
    k_pair.wait_recv()
    for step in ("x", 1, -1):
        k_other[step].start()
    v_pair.wait_send()
    for mate in ((1, 0), (1, 1), (2, 0), (2, 1)):
        q_moves[mate].start()
    v_own["x"].wait_recv()
    v_own["z"].start()
    v_pair.wait_recv()
    for step in ("x", 1, -1):
        v_other[step].start()
    for mate in distant[2:]:
        q_moves[mate].start()
    k_load.wait()
    q_load.wait()
    for step in (1, -1, "z"):
        k_own[step].wait_recv()
        v_own[step].wait_recv()
    q_moves[0, 1].wait_recv()
    visit((0,), 0, 6, True)

    k_other["x"].wait_recv()
    k_other["z"].start()
    k_other[1].wait_recv()
    k_other[-1].wait_recv()
    k_edge.start()
    q_moves[1, 0].wait_recv()
    q_moves[1, 1].wait_recv()
    visit((1,), 0, 6, True)

    v_other["x"].wait_recv()
    v_other["z"].start()
    v_other[1].wait_recv()
    v_other[-1].wait_recv()
    v_edge.start()
    for mate in distant[:2]:
        q_moves[mate].wait_recv()
    visit((2,), 0, 6, True)
    for mate in distant[2:]:
        q_moves[mate].wait_recv()
    visit((3,), 0, 6, True)
    visit_all(chip, 4, 6, 8, False)

    for move in (k_other["z"], v_other["z"], k_edge, v_edge):
        move.wait_recv()

    own_out = pltpu.make_async_copy(ready.at[h], out_ref.at[:, columns(h)], local_sem.at[3])

    def o_copy(ring, other):
        target = head_of(ring, other)
        index = 2 * ring + other
        return remote(
            ready.at[target], out_ref.at[:, columns(h)], o_send.at[index], o_recv.at[index],
            {"tm": t, "head": target},
        )

    o_moves = {mate: o_copy(*mate) for mate in mates}
    for ring in (3, 2, 1, 0):
        c = chunk_of(ring)
        done = absorb(c, 8, 11, False)
        mean = done[:HEAD_DIM] / done[HEAD_DIM:HEAD_DIM + 1]
        turned = mean.T.astype(jnp.bfloat16)
        for b in range(2):
            for g in range(GROUP):
                begin = (b * GROUP + g) * rows
                ready[2 * c + b, :, g * HEAD_DIM:(g + 1) * HEAD_DIM] = turned[begin:begin + rows]
        for mate in mates:
            if mate[0] == ring:
                o_moves[mate].start()
        if ring == 0:
            own_out.start()

    for moves in (k_own, v_own, k_other, v_other):
        for move in moves.values():
            move.wait_send()
    k_edge.wait_send()
    v_edge.wait_send()
    for move in q_moves.values():
        move.wait_send()
    own_out.wait()
    for move in o_moves.values():
        move.wait_recv()
        move.wait_send()


def shards(groups, queries, vis_keys, vis_values, span_start, span_end):
    rows, width = queries.shape
    tokens = vis_keys.shape[0]
    part = width // KV_HEADS
    dma = pltpu.SemaphoreType.DMA
    spans = [span.reshape(1, -1) for span in (span_start, span_end)]
    operands = [queries, vis_keys, vis_values, *spans]
    flops = 4 * rows * width * tokens * SLOTS
    return pl.pallas_call(
        functools.partial(kernel, groups),
        out_shape=pltpu.VMEM((rows, width), jnp.bfloat16),
        in_specs=[pl.BlockSpec(memory_space=pltpu.HBM)] * 5,
        out_specs=pl.BlockSpec(memory_space=pl.ANY),
        scratch_shapes=[
            pltpu.VMEM(spans[0].shape, jnp.int32),
            pltpu.VMEM(spans[1].shape, jnp.int32),
            pltpu.VMEM((KV_HEADS, rows, part), jnp.bfloat16),
            pltpu.VMEM((SLOTS, tokens, HEAD_DIM), jnp.bfloat16),
            pltpu.VMEM((SLOTS, HEAD_DIM, tokens), jnp.bfloat16),
            pltpu.VMEM((tokens, HEAD_DIM), jnp.bfloat16),
            pltpu.VMEM((4, HEAD_DIM + 16, 256), jnp.float32),
            pltpu.VMEM((4, 1, 256), jnp.float32),
            pltpu.VMEM((4, 1, 256), jnp.float32),
            pltpu.VMEM((4, 1, 256), jnp.float32),
            pltpu.VMEM((KV_HEADS, rows, part), jnp.bfloat16),
            dma((6,)),
            dma((8,)),
            dma((8,)),
            dma((10,)),
            dma((10,)),
            dma((10,)),
            dma((10,)),
            dma((8,)),
            dma((8,)),
        ],
        cost_estimate=pl.CostEstimate(
            flops=flops, bytes_accessed=8 * rows * width, transcendentals=flops // 512
        ),
        compiler_params=pltpu.CompilerParams(
            collective_id=0, has_side_effects=True, vmem_limit_bytes=40 * 1024 * 1024
        ),
    )(*[pltpu.with_memory_space_constraint(value, pltpu.HBM) for value in operands])


def solution(mesh):
    return jax.shard_map(
        functools.partial(shards, mesh.shape["tm"]),
        mesh=mesh,
        in_specs=(P(("tm", "head"), None), P("tm", "head"), P("tm", "head"), P("tm"), P("tm")),
        out_specs=P(("tm", "head"), None),
        check_vma=False,
    )
```

```python
import functools
import math

import jax
import jax.numpy as jnp
from jax import lax
from jax.experimental import pallas as pl
from jax.experimental.pallas import tpu as pltpu
from jax.sharding import PartitionSpec as P

HEADS = 64
KV_HEADS = 8
HEAD_DIM = 128
MESH = pl.DeviceIdType.MESH
GROUP = HEADS // KV_HEADS
RATE = math.log2(math.e) / math.sqrt(HEAD_DIM)
FAR = 1e30

OWN = {0: 0, -1: 1, 1: 2, -2: 3, 2: 4}
PAIR = {0: 5, -1: 6, 1: 7, -2: 8, 2: 9}
EDGE, SLOTS = 10, 11


class Move:
    def __init__(self, copies, arrives):
        self.copies, self.arrives = copies, arrives

    def start(self):
        for sends, copy in self.copies:
            pl.when(sends)(copy.start)

    def wait_recv(self):
        pl.when(self.arrives)(self.copies[0][1].wait_recv)

    def wait_send(self):
        for sends, copy in self.copies:
            pl.when(sends)(copy.wait_send)


def kernel(
    groups, q_hbm, k_hbm, v_hbm, first_hbm, last_hbm, out_ref, first_ref, last_ref,
    q_buf, k_buf, v_buf, k_relay, v_relay, v_rows, total, peak, first, last, ready,
    local_sem, q_send, q_recv, k_send, k_recv, v_send, v_recv, o_send, o_recv,
):
    t = lax.axis_index("tm")
    h = lax.axis_index("head")
    pair, parity = t // 2, t % 2
    side = 1 - 2 * parity
    x, z = pair % 4, pair // 4
    chip, core = h // 2, h % 2
    rows, width = q_buf.shape[1:]
    tokens = k_buf.shape[1]

    opposite_x = {"tm": 8 * z + 2 * ((x + 2) % 4) + parity, "head": h}

    def at_pair(distance):
        return {"tm": (t + groups + 2 * distance) % groups, "head": h}

    def along_y(distance):
        there = (4 * parity + chip + 8 + distance) % 8
        return {"tm": 2 * pair + there // 4, "head": 2 * (there % 4) + core}

    def flip(value):
        return value + 1 - 2 * (value % 2)

    def chunk_of(ring):
        start = chip if ring < 2 else (chip + 2) % 4
        return start if ring % 2 == 0 else flip(start)

    def columns(head):
        return pl.ds(pl.multiple_of(head * width, width), width)

    def remote(source, target, send, recv, device):
        return pltpu.make_async_remote_copy(
            source, target, send, recv, device_id=device, device_id_type=MESH
        )

    def head_of(ring, other):
        return 2 * chunk_of(ring) + (core if other == 0 else 1 - core)

    near = [(1, 0), (1, 1), (0, 1)]
    distant = [(2, 0), (2, 1), (3, 0), (3, 1)]
    mates = distant + near

    def q_copy(ring, other):
        target = head_of(ring, other)
        index = 2 * ring + other
        return remote(
            q_hbm.at[:, columns(target)], q_buf.at[h], q_send.at[index], q_recv.at[index],
            {"tm": t, "head": target},
        )

    def k_copy(source, target, role, device):
        return remote(source, target, k_send.at[role], k_recv.at[role], device)

    def v_copy(source, target, role, device):
        return remote(source, target, v_send.at[role], v_recv.at[role], device)

    k_load = pltpu.make_async_copy(k_hbm, k_buf.at[OWN[0]], local_sem.at[0])
    v_load = pltpu.make_async_copy(v_hbm, v_rows, local_sem.at[1])
    q_load = pltpu.make_async_copy(q_hbm.at[:, columns(h)], q_buf.at[h], local_sem.at[2])
    span_loads = [
        pltpu.make_async_copy(first_hbm, first_ref, local_sem.at[4]),
        pltpu.make_async_copy(last_hbm, last_ref, local_sem.at[5]),
    ]
    pairs = groups // 2
    at_start, at_end = z == 0, z == pairs // 4 - 1

    def has(distance):
        return (pair >= -distance) if distance < 0 else (pair < pairs - distance)

    barrier = pltpu.get_barrier_semaphore()
    everywhere = [along_y(2), along_y(-2), opposite_x]
    everywhere += [{"tm": t, "head": head_of(*mate)} for mate in mates]
    for partner in everywhere:
        pl.semaphore_signal(barrier, inc=1, device_id=partner, device_id_type=MESH)
    answers = len(everywhere)
    corner = jnp.where(parity == 0, pair == 0, pair == pairs - 1)
    cornered = jnp.where(parity == 0, pair == 3, pair == pairs - 4)
    others = [(has(distance), at_pair(distance)) for distance in (1, -1, 4, -4)]
    others += [(corner, at_pair(3 * side)), (cornered, at_pair(-3 * side))]
    for present, partner in others:
        answers = answers + jnp.where(present, 1, 0)

        @pl.when(present)
        def _(partner=partner):
            pl.semaphore_signal(barrier, inc=1, device_id=partner, device_id_type=MESH)

    for load in (v_load, k_load, *span_loads, q_load):
        load.start()

    low = x < 2
    to_next, to_last = jnp.logical_not(at_end), jnp.logical_not(at_start)

    def pick(base, condition, distance):
        return jnp.where(condition, base[distance], base[-distance])

    def spread(copy, buf, base, role, source):
        moves = {
            e: Move(
                [(has(e), copy(source, buf.at[base[-e]], role + i, at_pair(e)))],
                has(-e),
            )
            for i, e in enumerate((1, -1))
        }
        moves["x"] = copy(source, buf.at[pick(base, low, -2)], role + 2, opposite_x)
        along = copy(
            buf.at[pick(base, low, 2)], buf.at[pick(base, low, -2)], role + 3,
            at_pair(jnp.where(low, 4, -4)),
        )
        moves["z"] = Move(
            [(jnp.where(low, to_next, to_last), along)], jnp.where(low, to_last, to_next)
        )
        return moves

    def edge(copy, buf):
        up = parity == 0
        along = copy(
            buf.at[pick(PAIR, up, 1)], buf.at[EDGE], 9, at_pair(4 * side)
        )
        direct = copy(buf.at[PAIR[0]], buf.at[EDGE], 9, at_pair(3 * side))
        return Move(
            [(jnp.where(up, to_next, to_last), along), (corner, direct)],
            jnp.where(up, to_last | (x == 3), to_next | (x == 0)),
        )

    def legs(copy, buf, source, passing):
        half = passing.shape[0] // 2
        parts = ((pl.ds(0, half), 2, 0, 11), (pl.ds(half, half), -2, 10, 12))
        return [
            [
                copy(source.at[part], passing.at[part], role, along_y(way))
                for part, way, role, _ in parts
            ],
            [
                copy(passing.at[part], buf.at[PAIR[0], part], role, along_y(way))
                for part, way, _, role in parts
            ],
        ]

    k_leg = legs(k_copy, k_buf, k_hbm, k_relay)
    v_leg = legs(v_copy, v_buf, v_buf.at[OWN[0]], v_relay)
    k_own = spread(k_copy, k_buf, OWN, 1, k_hbm)
    v_own = spread(v_copy, v_buf, OWN, 1, v_buf.at[OWN[0]])
    k_other = spread(k_copy, k_buf, PAIR, 5, k_buf.at[PAIR[0]])
    v_other = spread(v_copy, v_buf, PAIR, 5, v_buf.at[PAIR[0]])
    k_edge, v_edge = edge(k_copy, k_buf), edge(v_copy, v_buf)
    q_moves = {mate: q_copy(*mate) for mate in mates}

    pl.semaphore_wait(barrier, answers)

    first_steps = (1, -1, "x")
    for move in k_leg[0]:
        move.start()
    for step in first_steps:
        k_own[step].start()
    q_moves[0, 1].start()
    v_load.wait()
    v_buf[OWN[0]] = v_rows[...].T
    for move in k_leg[0]:
        move.wait_send()
    for move in v_leg[0]:
        move.start()
    for step in first_steps:
        v_own[step].start()
    for mate in ((1, 0), (1, 1)):
        q_moves[mate].start()

    unused = [(base[d], jnp.logical_not(has(d))) for base in (OWN, PAIR) for d in (1, -1, 2, -2)]
    unused.append((EDGE, jnp.logical_not(jnp.where(parity == 0, has(-3), has(3)))))
    for slot, empty in unused:
        @pl.when(empty)
        def _(slot=slot):
            k_buf[slot] = jnp.zeros(k_buf.shape[1:], k_buf.dtype)
            v_buf[slot] = jnp.zeros(v_buf.shape[1:], v_buf.dtype)

    for load in span_loads:
        load.wait()
    lane = lax.broadcasted_iota(jnp.int32, (128, 256), 1)
    row = lax.broadcasted_iota(jnp.int32, (128, 256), 0)
    for c in range(4):
        wanted = c * 32 + (lane // 128) * 16 + lane % 16
        chosen = jnp.where(row == wanted, 1.0, 0.0).astype(jnp.bfloat16)
        for ref, held in ((first_ref, first), (last_ref, last)):
            offset_row = (ref[...] - t).astype(jnp.float32)
            offset_row = jnp.broadcast_to(offset_row, (16, 128)).astype(jnp.bfloat16)
            placed = jnp.dot(offset_row, chosen, preferred_element_type=jnp.float32)
            held[c] = placed[0:1]

    def offset(slot):
        for base, shift in ((OWN, 0), (PAIR, side)):
            for distance, index in base.items():
                if index == slot:
                    return 2 * distance + shift
        return -5 * side

    def absorb(c, start, stop, fresh):
        queries = jnp.concatenate(
            [
                q_buf[2 * c + b, :, g * HEAD_DIM:(g + 1) * HEAD_DIM]
                for b in range(2)
                for g in range(GROUP)
            ],
            axis=0,
        )
        begin, finish = first[c], last[c]
        keys = k_buf[start:stop].reshape((stop - start) * tokens, HEAD_DIM)
        scores = lax.dot_general(
            keys, queries, (((1,), (1,)), ((), ())), preferred_element_type=jnp.float32
        )
        scores = [scores[i * tokens:(i + 1) * tokens] for i in range(stop - start)]
        inside, best = [], []
        for slot, score in zip(range(start, stop), scores):
            place = jnp.asarray(offset(slot), jnp.int32).astype(jnp.float32)
            within = (begin <= place) & (place <= finish)
            inside.append(within)
            best.append(jnp.where(within, jnp.max(score, axis=0, keepdims=True), -FAR))
        top = functools.reduce(jnp.maximum, best)
        if not fresh:
            before = peak[c]
            top = jnp.maximum(before, top)
        peak[c] = top
        weights = [
            jnp.exp2((score - jnp.where(within, top, FAR)) * RATE).astype(jnp.bfloat16)
            for score, within in zip(scores, inside)
        ]
        weights = jnp.concatenate(weights, axis=0)
        left = jnp.concatenate([v_buf[slot] for slot in range(start, stop)], axis=1)
        ones = jnp.ones((16, left.shape[1]), jnp.bfloat16)
        left = jnp.concatenate([left, ones], axis=0)
        gained = jnp.dot(left, weights, preferred_element_type=jnp.float32)
        if not fresh:
            gained = gained + total[c] * jnp.exp2((before - top) * RATE)
        return gained

    def visit(rings, start, stop, fresh):
        for ring in rings:
            c = chunk_of(ring)
            total[c] = absorb(c, start, stop, fresh)

    def visit_all(begin, count, start, stop, fresh):
        def body(i, carry):
            c = (begin + 2 * (i // 2)) % 4
            c = c + (i % 2) * (1 - 2 * (c % 2))
            total[c] = absorb(c, start, stop, fresh)
            return carry

        lax.fori_loop(0, count, body, 0)

    for move, onward in zip(k_leg[0], k_leg[1]):
        move.wait_recv()
        onward.start()
    k_own["x"].wait_recv()
    k_own["z"].start()
    for move, onward in zip(v_leg[0], v_leg[1]):
        move.wait_recv()
        onward.start()
    for mate in distant[:2]:
        q_moves[mate].start()
    for move in k_leg[1]:
        move.wait_recv()
    for step in ("x", 1, -1):
        k_other[step].start()
    v_own["x"].wait_recv()
    v_own["z"].start()
    k_load.wait()
    q_load.wait()
    for step in (1, -1):
        k_own[step].wait_recv()
        v_own[step].wait_recv()
    for mate in near:
        q_moves[mate].wait_recv()
    visit_all(chip, 2, 0, 3, True)

    for move in v_leg[1]:
        move.wait_recv()
    for step in ("x", 1, -1):
        v_other[step].start()
    for mate in distant[2:]:
        q_moves[mate].start()
    k_own["z"].wait_recv()
    v_own["z"].wait_recv()
    visit_all(chip, 2, 3, 6, False)

    k_other["x"].wait_recv()
    k_other["z"].start()
    k_other[1].wait_recv()
    k_other[-1].wait_recv()
    k_edge.start()
    for mate in distant[:2]:
        q_moves[mate].wait_recv()
    visit((2,), 0, 6, True)

    v_other["x"].wait_recv()
    v_other["z"].start()
    v_other[1].wait_recv()
    v_other[-1].wait_recv()
    v_edge.start()
    for mate in distant[2:]:
        q_moves[mate].wait_recv()
    visit((3,), 0, 6, True)
    visit_all(chip, 4, 6, 8, False)

    for move in (k_other["z"], v_other["z"], k_edge, v_edge):
        move.wait_recv()

    own_out = pltpu.make_async_copy(ready.at[h], out_ref.at[:, columns(h)], local_sem.at[3])

    def o_copy(ring, other):
        target = head_of(ring, other)
        index = 2 * ring + other
        return remote(
            ready.at[target], out_ref.at[:, columns(h)], o_send.at[index], o_recv.at[index],
            {"tm": t, "head": target},
        )

    o_moves = {mate: o_copy(*mate) for mate in mates}
    for ring in (3, 2, 1, 0):
        c = chunk_of(ring)
        done = absorb(c, 8, 11, False)
        mean = done[:HEAD_DIM] / done[HEAD_DIM:HEAD_DIM + 1]
        turned = mean.T.astype(jnp.bfloat16)
        for b in range(2):
            for g in range(GROUP):
                begin = (b * GROUP + g) * rows
                ready[2 * c + b, :, g * HEAD_DIM:(g + 1) * HEAD_DIM] = turned[begin:begin + rows]
        for mate in mates:
            if mate[0] == ring:
                o_moves[mate].start()
        if ring == 0:
            own_out.start()

    for moves in (k_own, v_own, k_other, v_other):
        for move in moves.values():
            move.wait_send()
    for move in (k_edge, v_edge, *k_leg[1], *v_leg[0], *v_leg[1]):
        move.wait_send()
    for move in q_moves.values():
        move.wait_send()
    own_out.wait()
    for move in o_moves.values():
        move.wait_recv()
        move.wait_send()


def shards(groups, queries, vis_keys, vis_values, span_start, span_end):
    rows, width = queries.shape
    tokens = vis_keys.shape[0]
    part = width // KV_HEADS
    dma = pltpu.SemaphoreType.DMA
    spans = [span.reshape(1, -1) for span in (span_start, span_end)]
    operands = [queries, vis_keys, vis_values, *spans]
    flops = 4 * rows * width * tokens * SLOTS
    return pl.pallas_call(
        functools.partial(kernel, groups),
        out_shape=pltpu.VMEM((rows, width), jnp.bfloat16),
        in_specs=[pl.BlockSpec(memory_space=pltpu.HBM)] * 5,
        out_specs=pl.BlockSpec(memory_space=pl.ANY),
        scratch_shapes=[
            pltpu.VMEM(spans[0].shape, jnp.int32),
            pltpu.VMEM(spans[1].shape, jnp.int32),
            pltpu.VMEM((KV_HEADS, rows, part), jnp.bfloat16),
            pltpu.VMEM((SLOTS, tokens, HEAD_DIM), jnp.bfloat16),
            pltpu.VMEM((SLOTS, HEAD_DIM, tokens), jnp.bfloat16),
            pltpu.VMEM((tokens, HEAD_DIM), jnp.bfloat16),
            pltpu.VMEM((HEAD_DIM, tokens), jnp.bfloat16),
            pltpu.VMEM((tokens, HEAD_DIM), jnp.bfloat16),
            pltpu.VMEM((4, HEAD_DIM + 16, 256), jnp.float32),
            pltpu.VMEM((4, 1, 256), jnp.float32),
            pltpu.VMEM((4, 1, 256), jnp.float32),
            pltpu.VMEM((4, 1, 256), jnp.float32),
            pltpu.VMEM((KV_HEADS, rows, part), jnp.bfloat16),
            dma((6,)),
            dma((8,)),
            dma((8,)),
            dma((13,)),
            dma((13,)),
            dma((13,)),
            dma((13,)),
            dma((8,)),
            dma((8,)),
        ],
        cost_estimate=pl.CostEstimate(
            flops=flops, bytes_accessed=8 * rows * width, transcendentals=flops // 512
        ),
        compiler_params=pltpu.CompilerParams(
            collective_id=0, has_side_effects=True, vmem_limit_bytes=40 * 1024 * 1024
        ),
    )(*[pltpu.with_memory_space_constraint(value, pltpu.HBM) for value in operands])


def solution(mesh):
    return jax.shard_map(
        functools.partial(shards, mesh.shape["tm"]),
        mesh=mesh,
        in_specs=(P(("tm", "head"), None), P("tm", "head"), P("tm", "head"), P("tm"), P("tm")),
        out_specs=P(("tm", "head"), None),
        check_vma=False,
    )
```

```python
import functools
import math

import jax
import jax.numpy as jnp
from jax import lax
from jax.experimental import pallas as pl
from jax.experimental.pallas import tpu as pltpu
from jax.sharding import PartitionSpec as P

HEADS = 64
KV_HEADS = 8
HEAD_DIM = 128
MESH = pl.DeviceIdType.MESH
GROUP = HEADS // KV_HEADS
RATE = math.log2(math.e) / math.sqrt(HEAD_DIM)
FAR = 1e30

OWN = {0: 0, -1: 1, 1: 2, -2: 3, 2: 4}
PAIR = {0: 5, -1: 6, 1: 7, -2: 8, 2: 9}
EDGE, SLOTS = 10, 11


class Move:
    def __init__(self, copies, arrives):
        self.copies, self.arrives = copies, arrives

    def start(self):
        for sends, copy in self.copies:
            pl.when(sends)(copy.start)

    def wait_recv(self):
        pl.when(self.arrives)(self.copies[0][1].wait_recv)

    def wait_send(self):
        for sends, copy in self.copies:
            pl.when(sends)(copy.wait_send)


def kernel(
    groups, q_hbm, k_hbm, v_hbm, first_hbm, last_hbm, out_ref, first_ref, last_ref,
    q_buf, k_buf, v_buf, k_relay, v_relay, v_rows, total, peak, first, last, ready,
    local_sem, q_send, q_recv, k_send, k_recv, v_send, v_recv, o_send, o_recv,
):
    t = lax.axis_index("tm")
    h = lax.axis_index("head")
    pair, parity = t // 2, t % 2
    side = 1 - 2 * parity
    x, z = pair % 4, pair // 4
    chip, core = h // 2, h % 2
    rows, width = q_buf.shape[1:]
    tokens = k_buf.shape[1]

    opposite_x = {"tm": 8 * z + 2 * ((x + 2) % 4) + parity, "head": h}

    def at_pair(distance):
        return {"tm": (t + groups + 2 * distance) % groups, "head": h}

    def along_y(distance):
        there = (4 * parity + chip + 8 + distance) % 8
        return {"tm": 2 * pair + there // 4, "head": 2 * (there % 4) + core}

    def flip(value):
        return value + 1 - 2 * (value % 2)

    def chunk_of(ring):
        start = chip if ring < 2 else (chip + 2) % 4
        return start if ring % 2 == 0 else flip(start)

    def columns(head):
        return pl.ds(pl.multiple_of(head * width, width), width)

    def remote(source, target, send, recv, device):
        return pltpu.make_async_remote_copy(
            source, target, send, recv, device_id=device, device_id_type=MESH
        )

    def head_of(ring, other):
        return 2 * chunk_of(ring) + (core if other == 0 else 1 - core)

    near = [(1, 0), (1, 1), (0, 1)]
    distant = [(2, 0), (2, 1), (3, 0), (3, 1)]
    mates = distant + near

    def q_copy(ring, other):
        target = head_of(ring, other)
        index = 2 * ring + other
        return remote(
            q_hbm.at[:, columns(target)], q_buf.at[h], q_send.at[index], q_recv.at[index],
            {"tm": t, "head": target},
        )

    def k_copy(source, target, role, device):
        return remote(source, target, k_send.at[role], k_recv.at[role], device)

    def v_copy(source, target, role, device):
        return remote(source, target, v_send.at[role], v_recv.at[role], device)

    k_load = pltpu.make_async_copy(k_hbm, k_buf.at[OWN[0]], local_sem.at[0])
    v_load = pltpu.make_async_copy(v_hbm, v_rows, local_sem.at[1])
    q_load = pltpu.make_async_copy(q_hbm.at[:, columns(h)], q_buf.at[h], local_sem.at[2])
    span_loads = [
        pltpu.make_async_copy(first_hbm, first_ref, local_sem.at[4]),
        pltpu.make_async_copy(last_hbm, last_ref, local_sem.at[5]),
    ]
    pairs = groups // 2
    at_start, at_end = z == 0, z == pairs // 4 - 1

    def has(distance):
        return (pair >= -distance) if distance < 0 else (pair < pairs - distance)

    barrier = pltpu.get_barrier_semaphore()
    everywhere = [along_y(2), along_y(-2), opposite_x]
    everywhere += [{"tm": t, "head": head_of(*mate)} for mate in mates]
    for partner in everywhere:
        pl.semaphore_signal(barrier, inc=1, device_id=partner, device_id_type=MESH)
    answers = len(everywhere)
    corner = jnp.where(parity == 0, pair == 0, pair == pairs - 1)
    cornered = jnp.where(parity == 0, pair == 3, pair == pairs - 4)
    others = [(has(distance), at_pair(distance)) for distance in (1, -1, 4, -4)]
    others += [(corner, at_pair(3 * side)), (cornered, at_pair(-3 * side))]
    for present, partner in others:
        answers = answers + jnp.where(present, 1, 0)

        @pl.when(present)
        def _(partner=partner):
            pl.semaphore_signal(barrier, inc=1, device_id=partner, device_id_type=MESH)

    for load in (v_load, k_load, *span_loads, q_load):
        load.start()

    low = x < 2
    to_next, to_last = jnp.logical_not(at_end), jnp.logical_not(at_start)

    def pick(base, condition, distance):
        return jnp.where(condition, base[distance], base[-distance])

    def spread(copy, buf, base, role, source):
        moves = {
            e: Move(
                [(has(e), copy(source, buf.at[base[-e]], role + i, at_pair(e)))],
                has(-e),
            )
            for i, e in enumerate((1, -1))
        }
        moves["x"] = copy(source, buf.at[pick(base, low, -2)], role + 2, opposite_x)
        along = copy(
            buf.at[pick(base, low, 2)], buf.at[pick(base, low, -2)], role + 3,
            at_pair(jnp.where(low, 4, -4)),
        )
        moves["z"] = Move(
            [(jnp.where(low, to_next, to_last), along)], jnp.where(low, to_last, to_next)
        )
        return moves

    def edge(copy, buf):
        up = parity == 0
        along = copy(
            buf.at[pick(PAIR, up, 1)], buf.at[EDGE], 9, at_pair(4 * side)
        )
        direct = copy(buf.at[PAIR[0]], buf.at[EDGE], 9, at_pair(3 * side))
        return Move(
            [(jnp.where(up, to_next, to_last), along), (corner, direct)],
            jnp.where(up, to_last | (x == 3), to_next | (x == 0)),
        )

    def legs(copy, buf, source, passing):
        half = passing.shape[0] // 2
        parts = ((pl.ds(0, half), 2, 0, 11), (pl.ds(half, half), -2, 10, 12))
        return [
            [
                copy(source.at[part], passing.at[part], role, along_y(way))
                for part, way, role, _ in parts
            ],
            [
                copy(passing.at[part], buf.at[PAIR[0], part], role, along_y(way))
                for part, way, _, role in parts
            ],
        ]

    k_leg = legs(k_copy, k_buf, k_hbm, k_relay)
    v_leg = legs(v_copy, v_buf, v_buf.at[OWN[0]], v_relay)
    k_own = spread(k_copy, k_buf, OWN, 1, k_hbm)
    v_own = spread(v_copy, v_buf, OWN, 1, v_buf.at[OWN[0]])
    k_other = spread(k_copy, k_buf, PAIR, 5, k_buf.at[PAIR[0]])
    v_other = spread(v_copy, v_buf, PAIR, 5, v_buf.at[PAIR[0]])
    k_edge, v_edge = edge(k_copy, k_buf), edge(v_copy, v_buf)
    q_moves = {mate: q_copy(*mate) for mate in mates}

    pl.semaphore_wait(barrier, answers)

    first_steps = (1, -1, "x")
    for move in k_leg[0]:
        move.start()
    for step in first_steps:
        k_own[step].start()
    q_moves[0, 1].start()
    v_load.wait()
    v_buf[OWN[0]] = v_rows[...].T
    for move in k_leg[0]:
        move.wait_send()
    for move in v_leg[0]:
        move.start()
    for step in first_steps:
        v_own[step].start()
    for mate in ((1, 0), (1, 1)):
        q_moves[mate].start()

    unused = [(base[d], jnp.logical_not(has(d))) for base in (OWN, PAIR) for d in (1, -1, 2, -2)]
    unused.append((EDGE, jnp.logical_not(jnp.where(parity == 0, has(-3), has(3)))))
    for slot, empty in unused:
        @pl.when(empty)
        def _(slot=slot):
            k_buf[slot] = jnp.zeros(k_buf.shape[1:], k_buf.dtype)
            v_buf[slot] = jnp.zeros(v_buf.shape[1:], v_buf.dtype)

    for load in span_loads:
        load.wait()
    lane = lax.broadcasted_iota(jnp.int32, (128, 256), 1)
    row = lax.broadcasted_iota(jnp.int32, (128, 256), 0)
    for ring in range(4):
        wanted = chunk_of(ring) * 32 + (lane // 128) * 16 + lane % 16
        chosen = jnp.where(row == wanted, 1.0, 0.0).astype(jnp.bfloat16)
        for ref, held in ((first_ref, first), (last_ref, last)):
            offset_row = (ref[...] - t).astype(jnp.float32)
            offset_row = jnp.broadcast_to(offset_row, (16, 128)).astype(jnp.bfloat16)
            placed = jnp.dot(offset_row, chosen, preferred_element_type=jnp.float32)
            held[ring] = placed[0:1]

    def offset(slot):
        for base, shift in ((OWN, 0), (PAIR, side)):
            for distance, index in base.items():
                if index == slot:
                    return 2 * distance + shift
        return -5 * side

    def score(ring, slot):
        queries = jnp.concatenate(
            [
                q_buf[2 * chunk_of(ring) + b, :, g * HEAD_DIM:(g + 1) * HEAD_DIM]
                for b in range(2)
                for g in range(GROUP)
            ],
            axis=0,
        )
        return lax.dot_general(
            k_buf[slot], queries, (((1,), (1,)), ((), ())), preferred_element_type=jnp.float32
        )

    def visit(units, fresh=False, finish=None):
        scores = [score(units[0][0], slot) for slot in units[0][1]]
        ones = jnp.ones((16, tokens), jnp.bfloat16)
        for at, (ring, slots) in enumerate(units):
            following = units[at + 1] if at + 1 < len(units) else (ring, ())
            renew = fresh and all(ring != earlier for earlier, _ in units[:at])
            begin, end = first[ring], last[ring]
            inside, best = [], []
            for slot, part in zip(slots, scores):
                place = jnp.asarray(offset(slot), jnp.int32).astype(jnp.float32)
                within = (begin <= place) & (place <= end)
                inside.append(within)
                best.append(jnp.where(within, jnp.max(part, axis=0, keepdims=True), -FAR))
            top = functools.reduce(jnp.maximum, best)
            if renew:
                gained = jnp.zeros(total.shape[1:], jnp.float32)
            else:
                before = peak[ring]
                top = jnp.maximum(before, top)
                gained = total[ring] * jnp.exp2((before - top) * RATE)
            ahead = []
            for i, slot in enumerate(slots):
                if i < len(following[1]):
                    ahead.append(score(following[0], following[1][i]))
                level = jnp.where(inside[i], top, FAR)
                weights = jnp.exp2((scores[i] - level) * RATE).astype(jnp.bfloat16)
                left = jnp.concatenate([v_buf[slot], ones], axis=0)
                gained = gained + jnp.dot(left, weights, preferred_element_type=jnp.float32)
            for slot in following[1][len(slots):]:
                ahead.append(score(following[0], slot))
            if finish is None:
                peak[ring] = top
                total[ring] = gained
            else:
                finish(ring, gained)
            scores = ahead

    for move, onward in zip(k_leg[0], k_leg[1]):
        move.wait_recv()
        onward.start()
    k_own["x"].wait_recv()
    k_own["z"].start()
    for move, onward in zip(v_leg[0], v_leg[1]):
        move.wait_recv()
        onward.start()
    for mate in distant[:2]:
        q_moves[mate].start()
    for move in k_leg[1]:
        move.wait_recv()
    for step in ("x", 1, -1):
        k_other[step].start()
    v_own["x"].wait_recv()
    v_own["z"].start()
    k_load.wait()
    q_load.wait()
    for step in (1, -1):
        k_own[step].wait_recv()
        v_own[step].wait_recv()
    for mate in near:
        q_moves[mate].wait_recv()
    visit([(0, (0, 1, 2)), (1, (0, 1, 2))], fresh=True)

    for move in v_leg[1]:
        move.wait_recv()
    for step in ("x", 1, -1):
        v_other[step].start()
    for mate in distant[2:]:
        q_moves[mate].start()
    k_own["z"].wait_recv()
    v_own["z"].wait_recv()
    visit([(0, (3, 4, 5)), (1, (3, 4, 5))])

    k_other["x"].wait_recv()
    k_other["z"].start()
    k_other[1].wait_recv()
    k_other[-1].wait_recv()
    k_edge.start()
    for mate in distant[:2]:
        q_moves[mate].wait_recv()
    visit([(2, (0, 1, 2)), (2, (3, 4, 5))], fresh=True)

    v_other["x"].wait_recv()
    v_other["z"].start()
    v_other[1].wait_recv()
    v_other[-1].wait_recv()
    v_edge.start()
    visit([(ring, (6, 7)) for ring in range(3)])
    for mate in distant[2:]:
        q_moves[mate].wait_recv()
    visit([(3, (0, 1, 2)), (3, (3, 4, 5)), (3, (6, 7))], fresh=True)

    for move in (k_other["z"], v_other["z"], k_edge, v_edge):
        move.wait_recv()

    own_out = pltpu.make_async_copy(ready.at[h], out_ref.at[:, columns(h)], local_sem.at[3])

    def o_copy(ring, other):
        target = head_of(ring, other)
        index = 2 * ring + other
        return remote(
            ready.at[target], out_ref.at[:, columns(h)], o_send.at[index], o_recv.at[index],
            {"tm": t, "head": target},
        )

    o_moves = {mate: o_copy(*mate) for mate in mates}
    def send(ring, done):
        mean = done[:HEAD_DIM] / done[HEAD_DIM:HEAD_DIM + 1]
        turned = mean.T.astype(jnp.bfloat16)
        for b in range(2):
            for g in range(GROUP):
                begin = (b * GROUP + g) * rows
                ready[2 * chunk_of(ring) + b, :, g * HEAD_DIM:(g + 1) * HEAD_DIM] = turned[
                    begin:begin + rows
                ]
        for mate in mates:
            if mate[0] == ring:
                o_moves[mate].start()
        if ring == 0:
            own_out.start()

    visit([(ring, (8, 9, 10)) for ring in (3, 2, 1, 0)], finish=send)

    for moves in (k_own, v_own, k_other, v_other):
        for move in moves.values():
            move.wait_send()
    for move in (k_edge, v_edge, *k_leg[1], *v_leg[0], *v_leg[1]):
        move.wait_send()
    for move in q_moves.values():
        move.wait_send()
    own_out.wait()
    for move in o_moves.values():
        move.wait_recv()
        move.wait_send()


def shards(groups, queries, vis_keys, vis_values, span_start, span_end):
    rows, width = queries.shape
    tokens = vis_keys.shape[0]
    part = width // KV_HEADS
    dma = pltpu.SemaphoreType.DMA
    spans = [span.reshape(1, -1) for span in (span_start, span_end)]
    operands = [queries, vis_keys, vis_values, *spans]
    flops = 4 * rows * width * tokens * SLOTS
    return pl.pallas_call(
        functools.partial(kernel, groups),
        out_shape=pltpu.VMEM((rows, width), jnp.bfloat16),
        in_specs=[pl.BlockSpec(memory_space=pltpu.HBM)] * 5,
        out_specs=pl.BlockSpec(memory_space=pl.ANY),
        scratch_shapes=[
            pltpu.VMEM(spans[0].shape, jnp.int32),
            pltpu.VMEM(spans[1].shape, jnp.int32),
            pltpu.VMEM((KV_HEADS, rows, part), jnp.bfloat16),
            pltpu.VMEM((SLOTS, tokens, HEAD_DIM), jnp.bfloat16),
            pltpu.VMEM((SLOTS, HEAD_DIM, tokens), jnp.bfloat16),
            pltpu.VMEM((tokens, HEAD_DIM), jnp.bfloat16),
            pltpu.VMEM((HEAD_DIM, tokens), jnp.bfloat16),
            pltpu.VMEM((tokens, HEAD_DIM), jnp.bfloat16),
            pltpu.VMEM((4, HEAD_DIM + 16, 256), jnp.float32),
            pltpu.VMEM((4, 1, 256), jnp.float32),
            pltpu.VMEM((4, 1, 256), jnp.float32),
            pltpu.VMEM((4, 1, 256), jnp.float32),
            pltpu.VMEM((KV_HEADS, rows, part), jnp.bfloat16),
            dma((6,)),
            dma((8,)),
            dma((8,)),
            dma((13,)),
            dma((13,)),
            dma((13,)),
            dma((13,)),
            dma((8,)),
            dma((8,)),
        ],
        cost_estimate=pl.CostEstimate(
            flops=flops, bytes_accessed=8 * rows * width, transcendentals=flops // 512
        ),
        compiler_params=pltpu.CompilerParams(
            collective_id=0, has_side_effects=True, vmem_limit_bytes=40 * 1024 * 1024
        ),
    )(*[pltpu.with_memory_space_constraint(value, pltpu.HBM) for value in operands])


def solution(mesh):
    return jax.shard_map(
        functools.partial(shards, mesh.shape["tm"]),
        mesh=mesh,
        in_specs=(P(("tm", "head"), None), P("tm", "head"), P("tm", "head"), P("tm"), P("tm")),
        out_specs=P(("tm", "head"), None),
        check_vma=False,
    )
```

```python
import functools
import math

import jax
import jax.numpy as jnp
from jax import lax
from jax.experimental import pallas as pl
from jax.experimental.pallas import tpu as pltpu
from jax.sharding import PartitionSpec as P

HEADS = 64
KV_HEADS = 8
HEAD_DIM = 128
MESH = pl.DeviceIdType.MESH
GROUP = HEADS // KV_HEADS
RATE = math.log2(math.e) / math.sqrt(HEAD_DIM)
FAR = 1e30

OWN = {0: 0, -1: 1, 1: 2, "x": 3, "z": 4}
PAIR = {0: 5, -1: 6, 1: 7, "x": 8, "z": 9}
EDGE, SLOTS = 10, 11


class Move:
    def __init__(self, copies, arrives):
        self.copies, self.arrives = copies, arrives

    def start(self):
        for sends, copy in self.copies:
            pl.when(sends)(copy.start)

    def wait_recv(self):
        pl.when(self.arrives)(self.copies[0][1].wait_recv)

    def wait_send(self):
        for sends, copy in self.copies:
            pl.when(sends)(copy.wait_send)


def kernel(
    groups, q_hbm, k_hbm, v_hbm, first_hbm, last_hbm, out_ref, first_ref, last_ref,
    q_buf, k_buf, v_buf, k_relay, v_relay, v_rows, total, peak, first, last, ready,
    local_sem, q_send, q_recv, k_send, k_recv, v_send, v_recv, o_send, o_recv,
):
    t = lax.axis_index("tm")
    h = lax.axis_index("head")
    pair, parity = t // 2, t % 2
    side = 1 - 2 * parity
    x, z = pair % 4, pair // 4
    chip, core = h // 2, h % 2
    rows, width = q_buf.shape[1:]
    tokens = k_buf.shape[1]

    opposite_x = {"tm": 8 * z + 2 * ((x + 2) % 4) + parity, "head": h}

    def at_pair(distance):
        return {"tm": (t + groups + 2 * distance) % groups, "head": h}

    def along_y(distance):
        there = (4 * parity + chip + 8 + distance) % 8
        return {"tm": 2 * pair + there // 4, "head": 2 * (there % 4) + core}

    def flip(value):
        return value + 1 - 2 * (value % 2)

    def chunk_of(ring):
        start = chip if ring < 2 else (chip + 2) % 4
        return start if ring % 2 == 0 else flip(start)

    def columns(head):
        return pl.ds(pl.multiple_of(head * width, width), width)

    def remote(source, target, send, recv, device):
        return pltpu.make_async_remote_copy(
            source, target, send, recv, device_id=device, device_id_type=MESH
        )

    def head_of(ring, other):
        return 2 * chunk_of(ring) + (core if other == 0 else 1 - core)

    near = [(1, 0), (1, 1), (0, 1)]
    distant = [(2, 0), (2, 1), (3, 0), (3, 1)]
    mates = distant + near

    def q_copy(ring, other):
        target = head_of(ring, other)
        index = 2 * ring + other
        return remote(
            q_hbm.at[:, columns(target)], q_buf.at[h], q_send.at[index], q_recv.at[index],
            {"tm": t, "head": target},
        )

    def k_copy(source, target, role, device):
        return remote(source, target, k_send.at[role], k_recv.at[role], device)

    def v_copy(source, target, role, device):
        return remote(source, target, v_send.at[role], v_recv.at[role], device)

    k_load = pltpu.make_async_copy(k_hbm, k_buf.at[OWN[0]], local_sem.at[0])
    v_load = pltpu.make_async_copy(v_hbm, v_rows, local_sem.at[1])
    q_load = pltpu.make_async_copy(q_hbm.at[:, columns(h)], q_buf.at[h], local_sem.at[2])
    span_loads = [
        pltpu.make_async_copy(first_hbm, first_ref, local_sem.at[4]),
        pltpu.make_async_copy(last_hbm, last_ref, local_sem.at[5]),
    ]
    pairs = groups // 2
    at_start, at_end = z == 0, z == pairs // 4 - 1

    def has(distance):
        return (pair >= -distance) if distance < 0 else (pair < pairs - distance)

    barrier = pltpu.get_barrier_semaphore()
    everywhere = [along_y(2), along_y(-2), opposite_x]
    everywhere += [{"tm": t, "head": head_of(*mate)} for mate in mates]
    for partner in everywhere:
        pl.semaphore_signal(barrier, inc=1, device_id=partner, device_id_type=MESH)
    answers = len(everywhere)
    corner = jnp.where(parity == 0, pair == 0, pair == pairs - 1)
    cornered = jnp.where(parity == 0, pair == 3, pair == pairs - 4)
    others = [(has(distance), at_pair(distance)) for distance in (1, -1, 4, -4)]
    others += [(corner, at_pair(3 * side)), (cornered, at_pair(-3 * side))]
    for present, partner in others:
        answers = answers + jnp.where(present, 1, 0)

        @pl.when(present)
        def _(partner=partner):
            pl.semaphore_signal(barrier, inc=1, device_id=partner, device_id_type=MESH)

    for load in (v_load, k_load, *span_loads, q_load):
        load.start()

    low = x < 2
    to_next, to_last = jnp.logical_not(at_end), jnp.logical_not(at_start)

    def spread(copy, buf, base, role, source):
        moves = {
            e: Move(
                [(has(e), copy(source, buf.at[base[-e]], role + i, at_pair(e)))],
                has(-e),
            )
            for i, e in enumerate((1, -1))
        }
        moves["x"] = copy(source, buf.at[base["x"]], role + 2, opposite_x)
        along = copy(
            buf.at[base["x"]], buf.at[base["z"]], role + 3, at_pair(jnp.where(low, 4, -4))
        )
        moves["z"] = Move(
            [(jnp.where(low, to_next, to_last), along)], jnp.where(low, to_last, to_next)
        )
        return moves

    def edge(copy, buf):
        up = parity == 0
        beside = jnp.where(up, PAIR[1], PAIR[-1])
        along = copy(buf.at[beside], buf.at[EDGE], 9, at_pair(4 * side))
        direct = copy(buf.at[PAIR[0]], buf.at[EDGE], 9, at_pair(3 * side))
        return Move(
            [(jnp.where(up, to_next, to_last), along), (corner, direct)],
            jnp.where(up, to_last | (x == 3), to_next | (x == 0)),
        )

    def legs(copy, buf, source, passing):
        half = passing.shape[0] // 2
        parts = ((pl.ds(0, half), 2, 0, 11), (pl.ds(half, half), -2, 10, 12))
        return [
            [
                copy(source.at[part], passing.at[part], role, along_y(way))
                for part, way, role, _ in parts
            ],
            [
                copy(passing.at[part], buf.at[PAIR[0], part], role, along_y(way))
                for part, way, _, role in parts
            ],
        ]

    k_leg = legs(k_copy, k_buf, k_hbm, k_relay)
    v_leg = legs(v_copy, v_buf, v_buf.at[OWN[0]], v_relay)
    k_own = spread(k_copy, k_buf, OWN, 1, k_hbm)
    v_own = spread(v_copy, v_buf, OWN, 1, v_buf.at[OWN[0]])
    k_other = spread(k_copy, k_buf, PAIR, 5, k_buf.at[PAIR[0]])
    v_other = spread(v_copy, v_buf, PAIR, 5, v_buf.at[PAIR[0]])
    k_edge, v_edge = edge(k_copy, k_buf), edge(v_copy, v_buf)
    q_moves = {mate: q_copy(*mate) for mate in mates}

    pl.semaphore_wait(barrier, answers)

    first_steps = (1, -1, "x")
    for move in k_leg[0]:
        move.start()
    for step in first_steps:
        k_own[step].start()
    q_moves[0, 1].start()
    v_load.wait()
    v_buf[OWN[0]] = v_rows[...].T
    for move in k_leg[0]:
        move.wait_send()
    for move in v_leg[0]:
        move.start()
    for step in first_steps:
        v_own[step].start()
    for mate in ((1, 0), (1, 1)):
        q_moves[mate].start()

    unused = [(base[d], jnp.logical_not(has(d))) for base in (OWN, PAIR) for d in (1, -1)]
    unused += [(base["z"], jnp.where(low, at_start, at_end)) for base in (OWN, PAIR)]
    unused.append((EDGE, jnp.logical_not(jnp.where(parity == 0, has(-3), has(3)))))
    for slot, empty in unused:
        @pl.when(empty)
        def _(slot=slot):
            k_buf[slot] = jnp.zeros(k_buf.shape[1:], k_buf.dtype)
            v_buf[slot] = jnp.zeros(v_buf.shape[1:], v_buf.dtype)

    for load in span_loads:
        load.wait()
    lane = lax.broadcasted_iota(jnp.int32, (128, 256), 1)
    row = lax.broadcasted_iota(jnp.int32, (128, 256), 0)
    for ring in range(4):
        wanted = chunk_of(ring) * 32 + (lane // 128) * 16 + lane % 16
        chosen = jnp.where(row == wanted, 1.0, 0.0).astype(jnp.bfloat16)
        for ref, held in ((first_ref, first), (last_ref, last)):
            offset_row = (ref[...] - t).astype(jnp.float32)
            offset_row = jnp.broadcast_to(offset_row, (16, 128)).astype(jnp.bfloat16)
            placed = jnp.dot(offset_row, chosen, preferred_element_type=jnp.float32)
            held[ring] = placed[0:1]

    def offset(slot):
        places = {"x": jnp.where(low, 2, -2), "z": jnp.where(low, -2, 2)}
        for base, shift in ((OWN, 0), (PAIR, side)):
            for distance, index in base.items():
                if index == slot:
                    return 2 * places.get(distance, distance) + shift
        return -5 * side

    def score(ring, slot):
        queries = jnp.concatenate(
            [
                q_buf[2 * chunk_of(ring) + b, :, g * HEAD_DIM:(g + 1) * HEAD_DIM]
                for b in range(2)
                for g in range(GROUP)
            ],
            axis=0,
        )
        return lax.dot_general(
            k_buf[slot], queries, (((1,), (1,)), ((), ())), preferred_element_type=jnp.float32
        )

    def visit(units, fresh=False, finish=None):
        scores = [score(units[0][0], slot) for slot in units[0][1]]
        ones = jnp.ones((16, tokens), jnp.bfloat16)
        for at, (ring, slots) in enumerate(units):
            following = units[at + 1] if at + 1 < len(units) else (ring, ())
            renew = fresh and all(ring != earlier for earlier, _ in units[:at])
            begin, end = first[ring], last[ring]
            inside, best = [], []
            for slot, part in zip(slots, scores):
                place = jnp.asarray(offset(slot), jnp.int32).astype(jnp.float32)
                within = (begin <= place) & (place <= end)
                inside.append(within)
                best.append(jnp.where(within, jnp.max(part, axis=0, keepdims=True), -FAR))
            top = functools.reduce(jnp.maximum, best)
            if renew:
                gained = jnp.zeros(total.shape[1:], jnp.float32)
            else:
                before = peak[ring]
                top = jnp.maximum(before, top)
                gained = total[ring] * jnp.exp2((before - top) * RATE)
            ahead = []
            for i, slot in enumerate(slots):
                if i < len(following[1]):
                    ahead.append(score(following[0], following[1][i]))
                level = jnp.where(inside[i], top, FAR)
                weights = jnp.exp2((scores[i] - level) * RATE).astype(jnp.bfloat16)
                left = jnp.concatenate([v_buf[slot], ones], axis=0)
                gained = gained + jnp.dot(left, weights, preferred_element_type=jnp.float32)
            for slot in following[1][len(slots):]:
                ahead.append(score(following[0], slot))
            if finish is None:
                peak[ring] = top
                total[ring] = gained
            else:
                finish(ring, gained)
            scores = ahead

    for move, onward in zip(k_leg[0], k_leg[1]):
        move.wait_recv()
        onward.start()
    k_own["x"].wait_recv()
    k_own["z"].start()
    for move, onward in zip(v_leg[0], v_leg[1]):
        move.wait_recv()
        onward.start()
    for mate in distant[:2]:
        q_moves[mate].start()
    for move in k_leg[1]:
        move.wait_recv()
    for step in ("x", 1, -1):
        k_other[step].start()
    v_own["x"].wait_recv()
    v_own["z"].start()
    k_load.wait()
    q_load.wait()
    for step in (1, -1):
        k_own[step].wait_recv()
        v_own[step].wait_recv()
    for mate in near:
        q_moves[mate].wait_recv()
    visit([(0, (0, 1, 2, 3)), (1, (0, 1, 2, 3))], fresh=True)

    for move in v_leg[1]:
        move.wait_recv()
    for step in ("x", 1, -1):
        v_other[step].start()
    for mate in distant[2:]:
        q_moves[mate].start()
    k_own["z"].wait_recv()
    v_own["z"].wait_recv()
    visit([(0, (4, 5)), (1, (4, 5))])

    k_other["x"].wait_recv()
    k_other["z"].start()
    k_other[1].wait_recv()
    k_other[-1].wait_recv()
    k_edge.start()
    for mate in distant[:2]:
        q_moves[mate].wait_recv()
    visit([(2, (0, 1, 2)), (2, (3, 4, 5))], fresh=True)

    v_other["x"].wait_recv()
    v_other["z"].start()
    v_other[1].wait_recv()
    v_other[-1].wait_recv()
    v_edge.start()
    visit([(ring, (6, 7, 8)) for ring in range(3)])
    for mate in distant[2:]:
        q_moves[mate].wait_recv()
    visit([(3, (0, 1, 2)), (3, (3, 4, 5)), (3, (6, 7, 8))], fresh=True)

    for move in (k_other["z"], v_other["z"], k_edge, v_edge):
        move.wait_recv()

    own_out = pltpu.make_async_copy(ready.at[h], out_ref.at[:, columns(h)], local_sem.at[3])

    def o_copy(ring, other):
        target = head_of(ring, other)
        index = 2 * ring + other
        return remote(
            ready.at[target], out_ref.at[:, columns(h)], o_send.at[index], o_recv.at[index],
            {"tm": t, "head": target},
        )

    o_moves = {mate: o_copy(*mate) for mate in mates}
    def send(ring, done):
        mean = done[:HEAD_DIM] / done[HEAD_DIM:HEAD_DIM + 1]
        turned = mean.T.astype(jnp.bfloat16)
        for b in range(2):
            for g in range(GROUP):
                begin = (b * GROUP + g) * rows
                ready[2 * chunk_of(ring) + b, :, g * HEAD_DIM:(g + 1) * HEAD_DIM] = turned[
                    begin:begin + rows
                ]
        for mate in mates:
            if mate[0] == ring:
                o_moves[mate].start()
        if ring == 0:
            own_out.start()

    visit([(ring, (9, 10)) for ring in (3, 2, 1, 0)], finish=send)

    for moves in (k_own, v_own, k_other, v_other):
        for move in moves.values():
            move.wait_send()
    for move in (k_edge, v_edge, *k_leg[1], *v_leg[0], *v_leg[1]):
        move.wait_send()
    for move in q_moves.values():
        move.wait_send()
    own_out.wait()
    for move in o_moves.values():
        move.wait_recv()
        move.wait_send()


def shards(groups, queries, vis_keys, vis_values, span_start, span_end):
    rows, width = queries.shape
    tokens = vis_keys.shape[0]
    part = width // KV_HEADS
    dma = pltpu.SemaphoreType.DMA
    spans = [span.reshape(1, -1) for span in (span_start, span_end)]
    operands = [queries, vis_keys, vis_values, *spans]
    flops = 4 * rows * width * tokens * SLOTS
    return pl.pallas_call(
        functools.partial(kernel, groups),
        out_shape=pltpu.VMEM((rows, width), jnp.bfloat16),
        in_specs=[pl.BlockSpec(memory_space=pltpu.HBM)] * 5,
        out_specs=pl.BlockSpec(memory_space=pl.ANY),
        scratch_shapes=[
            pltpu.VMEM(spans[0].shape, jnp.int32),
            pltpu.VMEM(spans[1].shape, jnp.int32),
            pltpu.VMEM((KV_HEADS, rows, part), jnp.bfloat16),
            pltpu.VMEM((SLOTS, tokens, HEAD_DIM), jnp.bfloat16),
            pltpu.VMEM((SLOTS, HEAD_DIM, tokens), jnp.bfloat16),
            pltpu.VMEM((tokens, HEAD_DIM), jnp.bfloat16),
            pltpu.VMEM((HEAD_DIM, tokens), jnp.bfloat16),
            pltpu.VMEM((tokens, HEAD_DIM), jnp.bfloat16),
            pltpu.VMEM((4, HEAD_DIM + 16, 256), jnp.float32),
            pltpu.VMEM((4, 1, 256), jnp.float32),
            pltpu.VMEM((4, 1, 256), jnp.float32),
            pltpu.VMEM((4, 1, 256), jnp.float32),
            pltpu.VMEM((KV_HEADS, rows, part), jnp.bfloat16),
            dma((6,)),
            dma((8,)),
            dma((8,)),
            dma((13,)),
            dma((13,)),
            dma((13,)),
            dma((13,)),
            dma((8,)),
            dma((8,)),
        ],
        cost_estimate=pl.CostEstimate(
            flops=flops, bytes_accessed=8 * rows * width, transcendentals=flops // 512
        ),
        compiler_params=pltpu.CompilerParams(
            collective_id=0, has_side_effects=True, vmem_limit_bytes=40 * 1024 * 1024
        ),
    )(*[pltpu.with_memory_space_constraint(value, pltpu.HBM) for value in operands])


def solution(mesh):
    return jax.shard_map(
        functools.partial(shards, mesh.shape["tm"]),
        mesh=mesh,
        in_specs=(P(("tm", "head"), None), P("tm", "head"), P("tm", "head"), P("tm"), P("tm")),
        out_specs=P(("tm", "head"), None),
        check_vma=False,
    )
```

```python
import functools
import math

import jax
import jax.numpy as jnp
from jax import lax
from jax.experimental import pallas as pl
from jax.experimental.pallas import tpu as pltpu
from jax.sharding import PartitionSpec as P

HEADS = 64
KV_HEADS = 8
HEAD_DIM = 128
MESH = pl.DeviceIdType.MESH
GROUP = HEADS // KV_HEADS
RATE = math.log2(math.e) / math.sqrt(HEAD_DIM)
FAR = 1e30

OWN = {0: 0, -1: 1, 1: 2, "x": 3, "z": 4}
PAIR = {0: 5, -1: 6, 1: 7, "x": 8, "z": 9}
EDGE, SLOTS = 10, 11


class Move:
    def __init__(self, copies, arrives):
        self.copies, self.arrives = copies, arrives

    def start(self):
        for sends, copy in self.copies:
            pl.when(sends)(copy.start)

    def wait_recv(self):
        pl.when(self.arrives)(self.copies[0][1].wait_recv)

    def wait_send(self):
        for sends, copy in self.copies:
            pl.when(sends)(copy.wait_send)


def kernel(
    groups, q_hbm, k_hbm, v_hbm, first_hbm, last_hbm, out_ref, first_ref, last_ref,
    q_buf, k_buf, v_buf, k_relay, v_relay, v_rows, total, peak, first, last, ready,
    local_sem, q_send, q_recv, k_send, k_recv, v_send, v_recv, o_send, o_recv,
):
    t = lax.axis_index("tm")
    h = lax.axis_index("head")
    pair, parity = t // 2, t % 2
    side = 1 - 2 * parity
    x, z = pair % 4, pair // 4
    chip, core = h // 2, h % 2
    rows, width = q_buf.shape[1:]
    tokens = k_buf.shape[1]

    opposite_x = {"tm": 8 * z + 2 * ((x + 2) % 4) + parity, "head": h}

    def at_pair(distance):
        return {"tm": (t + groups + 2 * distance) % groups, "head": h}

    def along_y(distance):
        there = (4 * parity + chip + 8 + distance) % 8
        return {"tm": 2 * pair + there // 4, "head": 2 * (there % 4) + core}

    def flip(value):
        return value + 1 - 2 * (value % 2)

    def chunk_of(ring):
        start = chip if ring < 2 else 3 - chip
        return start if ring % 2 == 0 else flip(start)

    def columns(head):
        return pl.ds(pl.multiple_of(head * width, width), width)

    def remote(source, target, send, recv, device):
        return pltpu.make_async_remote_copy(
            source, target, send, recv, device_id=device, device_id_type=MESH
        )

    def head_of(ring, other):
        return 2 * chunk_of(ring) + (core if other == 0 else 1 - core)

    near = [(1, 0), (1, 1), (0, 1)]
    distant = [(2, 0), (2, 1), (3, 0), (3, 1)]
    mates = distant + near

    def q_copy(ring, other):
        target = head_of(ring, other)
        index = 2 * ring + other
        return remote(
            q_hbm.at[:, columns(target)], q_buf.at[h], q_send.at[index], q_recv.at[index],
            {"tm": t, "head": target},
        )

    def k_copy(source, target, role, device):
        return remote(source, target, k_send.at[role], k_recv.at[role], device)

    def v_copy(source, target, role, device):
        return remote(source, target, v_send.at[role], v_recv.at[role], device)

    k_load = pltpu.make_async_copy(k_hbm, k_buf.at[OWN[0]], local_sem.at[0])
    v_load = pltpu.make_async_copy(v_hbm, v_rows, local_sem.at[1])
    q_load = pltpu.make_async_copy(q_hbm.at[:, columns(h)], q_buf.at[h], local_sem.at[2])
    span_loads = [
        pltpu.make_async_copy(first_hbm, first_ref, local_sem.at[4]),
        pltpu.make_async_copy(last_hbm, last_ref, local_sem.at[5]),
    ]
    pairs = groups // 2
    at_start, at_end = z == 0, z == pairs // 4 - 1

    def has(distance):
        return (pair >= -distance) if distance < 0 else (pair < pairs - distance)

    barrier = pltpu.get_barrier_semaphore()
    everywhere = [along_y(2), along_y(-2), opposite_x]
    everywhere += [{"tm": t, "head": head_of(*mate)} for mate in mates]
    for partner in everywhere:
        pl.semaphore_signal(barrier, inc=1, device_id=partner, device_id_type=MESH)
    answers = len(everywhere)
    corner = jnp.where(parity == 0, pair == 0, pair == pairs - 1)
    cornered = jnp.where(parity == 0, pair == 3, pair == pairs - 4)
    others = [(has(distance), at_pair(distance)) for distance in (1, -1, 4, -4)]
    others += [(corner, at_pair(3 * side)), (cornered, at_pair(-3 * side))]
    for present, partner in others:
        answers = answers + jnp.where(present, 1, 0)

        @pl.when(present)
        def _(partner=partner):
            pl.semaphore_signal(barrier, inc=1, device_id=partner, device_id_type=MESH)

    for load in (v_load, k_load, *span_loads, q_load):
        load.start()

    low = x < 2
    to_next, to_last = jnp.logical_not(at_end), jnp.logical_not(at_start)

    def spread(copy, buf, base, role, source):
        moves = {
            e: Move(
                [(has(e), copy(source, buf.at[base[-e]], role + i, at_pair(e)))],
                has(-e),
            )
            for i, e in enumerate((1, -1))
        }
        moves["x"] = copy(source, buf.at[base["x"]], role + 2, opposite_x)
        along = copy(
            buf.at[base["x"]], buf.at[base["z"]], role + 3, at_pair(jnp.where(low, 4, -4))
        )
        moves["z"] = Move(
            [(jnp.where(low, to_next, to_last), along)], jnp.where(low, to_last, to_next)
        )
        return moves

    def edge(copy, buf):
        up = parity == 0
        beside = jnp.where(up, PAIR[1], PAIR[-1])
        along = copy(buf.at[beside], buf.at[EDGE], 9, at_pair(4 * side))
        direct = copy(buf.at[PAIR[0]], buf.at[EDGE], 9, at_pair(3 * side))
        return Move(
            [(jnp.where(up, to_next, to_last), along), (corner, direct)],
            jnp.where(up, to_last | (x == 3), to_next | (x == 0)),
        )

    def legs(copy, buf, source, passing):
        half = passing.shape[0] // 2
        parts = ((pl.ds(0, half), 2, 0, 11), (pl.ds(half, half), -2, 10, 12))
        return [
            [
                copy(source.at[part], passing.at[part], role, along_y(way))
                for part, way, role, _ in parts
            ],
            [
                copy(passing.at[part], buf.at[PAIR[0], part], role, along_y(way))
                for part, way, _, role in parts
            ],
        ]

    k_leg = legs(k_copy, k_buf, k_hbm, k_relay)
    v_leg = legs(v_copy, v_buf, v_buf.at[OWN[0]], v_relay)
    k_own = spread(k_copy, k_buf, OWN, 1, k_hbm)
    v_own = spread(v_copy, v_buf, OWN, 1, v_buf.at[OWN[0]])
    k_other = spread(k_copy, k_buf, PAIR, 5, k_buf.at[PAIR[0]])
    v_other = spread(v_copy, v_buf, PAIR, 5, v_buf.at[PAIR[0]])
    k_edge, v_edge = edge(k_copy, k_buf), edge(v_copy, v_buf)
    q_moves = {mate: q_copy(*mate) for mate in mates}

    pl.semaphore_wait(barrier, answers)

    first_steps = (1, -1, "x")
    for move in k_leg[0]:
        move.start()
    for step in first_steps:
        k_own[step].start()
    q_moves[0, 1].start()
    v_load.wait()
    v_buf[OWN[0]] = v_rows[...].T
    for move in k_leg[0]:
        move.wait_send()
    for move in v_leg[0]:
        move.start()
    for step in first_steps:
        v_own[step].start()
    for mate in ((1, 0), (1, 1)):
        q_moves[mate].start()

    unused = [(base[d], jnp.logical_not(has(d))) for base in (OWN, PAIR) for d in (1, -1)]
    unused += [(base["z"], jnp.where(low, at_start, at_end)) for base in (OWN, PAIR)]
    unused.append((EDGE, jnp.logical_not(jnp.where(parity == 0, has(-3), has(3)))))
    for slot, empty in unused:
        @pl.when(empty)
        def _(slot=slot):
            k_buf[slot] = jnp.zeros(k_buf.shape[1:], k_buf.dtype)
            v_buf[slot] = jnp.zeros(v_buf.shape[1:], v_buf.dtype)

    for load in span_loads:
        load.wait()
    lane = lax.broadcasted_iota(jnp.int32, (128, 256), 1)
    row = lax.broadcasted_iota(jnp.int32, (128, 256), 0)
    for ring in range(4):
        wanted = chunk_of(ring) * 32 + (lane // 128) * 16 + lane % 16
        chosen = jnp.where(row == wanted, 1.0, 0.0).astype(jnp.bfloat16)
        for ref, held in ((first_ref, first), (last_ref, last)):
            offset_row = (ref[...] - t).astype(jnp.float32)
            offset_row = jnp.broadcast_to(offset_row, (16, 128)).astype(jnp.bfloat16)
            placed = jnp.dot(offset_row, chosen, preferred_element_type=jnp.float32)
            held[ring] = placed[0:1]

    def offset(slot):
        places = {"x": jnp.where(low, 2, -2), "z": jnp.where(low, -2, 2)}
        for base, shift in ((OWN, 0), (PAIR, side)):
            for distance, index in base.items():
                if index == slot:
                    return 2 * places.get(distance, distance) + shift
        return -5 * side

    def score(ring, slot):
        queries = jnp.concatenate(
            [
                q_buf[2 * chunk_of(ring) + b, :, g * HEAD_DIM:(g + 1) * HEAD_DIM]
                for b in range(2)
                for g in range(GROUP)
            ],
            axis=0,
        )
        return lax.dot_general(
            k_buf[slot], queries, (((1,), (1,)), ((), ())), preferred_element_type=jnp.float32
        )

    def visit(units, fresh=False, finish=None):
        scores = [score(units[0][0], slot) for slot in units[0][1]]
        ones = jnp.ones((16, tokens), jnp.bfloat16)
        for at, (ring, slots) in enumerate(units):
            following = units[at + 1] if at + 1 < len(units) else (ring, ())
            renew = fresh and all(ring != earlier for earlier, _ in units[:at])
            begin, end = first[ring], last[ring]
            inside, best = [], []
            for slot, part in zip(slots, scores):
                place = jnp.asarray(offset(slot), jnp.int32).astype(jnp.float32)
                within = (begin <= place) & (place <= end)
                inside.append(within)
                best.append(jnp.where(within, jnp.max(part, axis=0, keepdims=True), -FAR))
            top = functools.reduce(jnp.maximum, best)
            if renew:
                gained = jnp.zeros(total.shape[1:], jnp.float32)
            else:
                before = peak[ring]
                top = jnp.maximum(before, top)
                gained = total[ring] * jnp.exp2((before - top) * RATE)
            ahead = []
            for i, slot in enumerate(slots):
                if i < len(following[1]):
                    ahead.append(score(following[0], following[1][i]))
                level = jnp.where(inside[i], top, FAR)
                weights = jnp.exp2((scores[i] - level) * RATE).astype(jnp.bfloat16)
                left = jnp.concatenate([v_buf[slot], ones], axis=0)
                gained = gained + jnp.dot(left, weights, preferred_element_type=jnp.float32)
            for slot in following[1][len(slots):]:
                ahead.append(score(following[0], slot))
            if finish is None:
                peak[ring] = top
                total[ring] = gained
            else:
                finish(ring, gained)
            scores = ahead

    for move, onward in zip(k_leg[0], k_leg[1]):
        move.wait_recv()
        onward.start()
    for mate in distant[:2]:
        q_moves[mate].start()
    k_own["x"].wait_recv()
    k_own["z"].start()
    for move, onward in zip(v_leg[0], v_leg[1]):
        move.wait_recv()
        onward.start()
    for move in k_leg[1]:
        move.wait_recv()
    for step in ("x", 1, -1):
        k_other[step].start()
    for mate in distant[2:]:
        q_moves[mate].start()
    v_own["x"].wait_recv()
    v_own["z"].start()
    k_load.wait()
    q_load.wait()
    for step in (1, -1):
        k_own[step].wait_recv()
        v_own[step].wait_recv()
    for mate in near:
        q_moves[mate].wait_recv()
    visit([(0, (0, 1, 2, 3)), (1, (0, 1, 2, 3))], fresh=True)

    for move in v_leg[1]:
        move.wait_recv()
    for step in ("x", 1, -1):
        v_other[step].start()
    k_own["z"].wait_recv()
    v_own["z"].wait_recv()
    visit([(0, (4, 5)), (1, (4, 5))])

    k_other["x"].wait_recv()
    k_other["z"].start()
    k_other[1].wait_recv()
    k_other[-1].wait_recv()
    k_edge.start()
    for mate in distant[:2]:
        q_moves[mate].wait_recv()
    visit([(2, (0, 1, 2)), (2, (3, 4, 5))], fresh=True)

    v_other["x"].wait_recv()
    v_other["z"].start()
    v_other[1].wait_recv()
    v_other[-1].wait_recv()
    v_edge.start()
    visit([(ring, (6, 7, 8)) for ring in range(3)])
    for mate in distant[2:]:
        q_moves[mate].wait_recv()
    visit([(3, (0, 1, 2)), (3, (3, 4, 5)), (3, (6, 7, 8))], fresh=True)

    for move in (k_other["z"], v_other["z"], k_edge, v_edge):
        move.wait_recv()

    own_out = pltpu.make_async_copy(ready.at[h], out_ref.at[:, columns(h)], local_sem.at[3])

    def o_copy(ring, other):
        target = head_of(ring, other)
        index = 2 * ring + other
        return remote(
            ready.at[target], out_ref.at[:, columns(h)], o_send.at[index], o_recv.at[index],
            {"tm": t, "head": target},
        )

    o_moves = {mate: o_copy(*mate) for mate in mates}
    def send(ring, done):
        mean = done[:HEAD_DIM] / done[HEAD_DIM:HEAD_DIM + 1]
        turned = mean.T.astype(jnp.bfloat16)
        for b in range(2):
            for g in range(GROUP):
                begin = (b * GROUP + g) * rows
                ready[2 * chunk_of(ring) + b, :, g * HEAD_DIM:(g + 1) * HEAD_DIM] = turned[
                    begin:begin + rows
                ]
        for mate in mates:
            if mate[0] == ring:
                o_moves[mate].start()
        if ring == 0:
            own_out.start()

    visit([(ring, (9, 10)) for ring in (2, 3, 1, 0)], finish=send)

    for moves in (k_own, v_own, k_other, v_other):
        for move in moves.values():
            move.wait_send()
    for move in (k_edge, v_edge, *k_leg[1], *v_leg[0], *v_leg[1]):
        move.wait_send()
    for move in q_moves.values():
        move.wait_send()
    own_out.wait()
    for move in o_moves.values():
        move.wait_recv()
        move.wait_send()


def shards(groups, queries, vis_keys, vis_values, span_start, span_end):
    rows, width = queries.shape
    tokens = vis_keys.shape[0]
    part = width // KV_HEADS
    dma = pltpu.SemaphoreType.DMA
    spans = [span.reshape(1, -1) for span in (span_start, span_end)]
    operands = [queries, vis_keys, vis_values, *spans]
    flops = 4 * rows * width * tokens * SLOTS
    return pl.pallas_call(
        functools.partial(kernel, groups),
        out_shape=pltpu.VMEM((rows, width), jnp.bfloat16),
        in_specs=[pl.BlockSpec(memory_space=pltpu.HBM)] * 5,
        out_specs=pl.BlockSpec(memory_space=pl.ANY),
        scratch_shapes=[
            pltpu.VMEM(spans[0].shape, jnp.int32),
            pltpu.VMEM(spans[1].shape, jnp.int32),
            pltpu.VMEM((KV_HEADS, rows, part), jnp.bfloat16),
            pltpu.VMEM((SLOTS, tokens, HEAD_DIM), jnp.bfloat16),
            pltpu.VMEM((SLOTS, HEAD_DIM, tokens), jnp.bfloat16),
            pltpu.VMEM((tokens, HEAD_DIM), jnp.bfloat16),
            pltpu.VMEM((HEAD_DIM, tokens), jnp.bfloat16),
            pltpu.VMEM((tokens, HEAD_DIM), jnp.bfloat16),
            pltpu.VMEM((4, HEAD_DIM + 16, 256), jnp.float32),
            pltpu.VMEM((4, 1, 256), jnp.float32),
            pltpu.VMEM((4, 1, 256), jnp.float32),
            pltpu.VMEM((4, 1, 256), jnp.float32),
            pltpu.VMEM((KV_HEADS, rows, part), jnp.bfloat16),
            dma((6,)),
            dma((8,)),
            dma((8,)),
            dma((13,)),
            dma((13,)),
            dma((13,)),
            dma((13,)),
            dma((8,)),
            dma((8,)),
        ],
        cost_estimate=pl.CostEstimate(
            flops=flops, bytes_accessed=8 * rows * width, transcendentals=flops // 512
        ),
        compiler_params=pltpu.CompilerParams(
            collective_id=0, has_side_effects=True, vmem_limit_bytes=40 * 1024 * 1024
        ),
    )(*[pltpu.with_memory_space_constraint(value, pltpu.HBM) for value in operands])


def solution(mesh):
    return jax.shard_map(
        functools.partial(shards, mesh.shape["tm"]),
        mesh=mesh,
        in_specs=(P(("tm", "head"), None), P("tm", "head"), P("tm", "head"), P("tm"), P("tm")),
        out_specs=P(("tm", "head"), None),
        check_vma=False,
    )
```

```python
import functools
import math

import jax
import jax.numpy as jnp
from jax import lax
from jax.experimental import pallas as pl
from jax.experimental.pallas import tpu as pltpu
from jax.sharding import PartitionSpec as P

HEADS = 64
KV_HEADS = 8
HEAD_DIM = 128
MESH = pl.DeviceIdType.MESH
GROUP = HEADS // KV_HEADS
RATE = math.log2(math.e) / math.sqrt(HEAD_DIM)
FAR = 1e30

OWN = {0: 0, -1: 1, 1: 2, "x": 3, "z": 4}
PAIR = {0: 5, -1: 6, 1: 7, "x": 8, "z": 9}
EDGE, SLOTS = 10, 11


class Move:
    def __init__(self, copies, arrives):
        self.copies, self.arrives = copies, arrives

    def start(self):
        for sends, copy in self.copies:
            pl.when(sends)(copy.start)

    def wait_recv(self):
        pl.when(self.arrives)(self.copies[0][1].wait_recv)

    def wait_send(self):
        for sends, copy in self.copies:
            pl.when(sends)(copy.wait_send)


def kernel(
    groups, q_hbm, k_hbm, v_hbm, first_hbm, last_hbm, out_ref, first_ref, last_ref,
    q_buf, q_turned, k_buf, v_buf, k_relay, v_relay, v_rows, total, peak, first, last, ready,
    local_sem, q_send, q_recv, k_send, k_recv, v_send, v_recv, o_send, o_recv,
):
    t = lax.axis_index("tm")
    h = lax.axis_index("head")
    pair, parity = t // 2, t % 2
    side = 1 - 2 * parity
    x, z = pair % 4, pair // 4
    chip, core = h // 2, h % 2
    rows, width = q_buf.shape[1:]
    tokens = k_buf.shape[1]

    opposite_x = {"tm": 8 * z + 2 * ((x + 2) % 4) + parity, "head": h}

    def at_pair(distance):
        return {"tm": (t + groups + 2 * distance) % groups, "head": h}

    def along_y(distance):
        there = (4 * parity + chip + 8 + distance) % 8
        return {"tm": 2 * pair + there // 4, "head": 2 * (there % 4) + core}

    def flip(value):
        return value + 1 - 2 * (value % 2)

    def chunk_of(ring):
        start = chip if ring < 2 else (chip + 2) % 4
        return start if ring % 2 == 0 else flip(start)

    def columns(head):
        return pl.ds(pl.multiple_of(head * width, width), width)

    def remote(source, target, send, recv, device):
        return pltpu.make_async_remote_copy(
            source, target, send, recv, device_id=device, device_id_type=MESH
        )

    def head_of(ring, other):
        return 2 * chunk_of(ring) + (core if other == 0 else 1 - core)

    near = [(1, 0), (1, 1), (0, 1)]
    distant = [(2, 0), (2, 1), (3, 0), (3, 1)]
    mates = distant + near

    def q_copy(ring, other):
        target = head_of(ring, other)
        index = 2 * ring + other
        return remote(
            q_hbm.at[:, columns(target)], q_buf.at[h], q_send.at[index], q_recv.at[index],
            {"tm": t, "head": target},
        )

    def k_copy(source, target, role, device):
        return remote(source, target, k_send.at[role], k_recv.at[role], device)

    def v_copy(source, target, role, device):
        return remote(source, target, v_send.at[role], v_recv.at[role], device)

    k_load = pltpu.make_async_copy(k_hbm, k_buf.at[OWN[0]], local_sem.at[0])
    v_load = pltpu.make_async_copy(v_hbm, v_rows, local_sem.at[1])
    q_load = pltpu.make_async_copy(q_hbm.at[:, columns(h)], q_buf.at[h], local_sem.at[2])
    span_loads = [
        pltpu.make_async_copy(first_hbm, first_ref, local_sem.at[4]),
        pltpu.make_async_copy(last_hbm, last_ref, local_sem.at[5]),
    ]
    pairs = groups // 2
    at_start, at_end = z == 0, z == pairs // 4 - 1

    def has(distance):
        return (pair >= -distance) if distance < 0 else (pair < pairs - distance)

    barrier = pltpu.get_barrier_semaphore()
    everywhere = [along_y(2), along_y(-2), opposite_x]
    everywhere += [{"tm": t, "head": head_of(*mate)} for mate in mates]
    for partner in everywhere:
        pl.semaphore_signal(barrier, inc=1, device_id=partner, device_id_type=MESH)
    answers = len(everywhere)
    corner = jnp.where(parity == 0, pair == 0, pair == pairs - 1)
    cornered = jnp.where(parity == 0, pair == 3, pair == pairs - 4)
    others = [(has(distance), at_pair(distance)) for distance in (1, -1, 4, -4)]
    others += [(corner, at_pair(3 * side)), (cornered, at_pair(-3 * side))]
    for present, partner in others:
        answers = answers + jnp.where(present, 1, 0)

        @pl.when(present)
        def _(partner=partner):
            pl.semaphore_signal(barrier, inc=1, device_id=partner, device_id_type=MESH)

    for load in (v_load, k_load, *span_loads, q_load):
        load.start()

    low = x < 2
    to_next, to_last = jnp.logical_not(at_end), jnp.logical_not(at_start)

    def spread(copy, buf, base, role, source):
        moves = {
            e: Move(
                [(has(e), copy(source, buf.at[base[-e]], role + i, at_pair(e)))],
                has(-e),
            )
            for i, e in enumerate((1, -1))
        }
        moves["x"] = copy(source, buf.at[base["x"]], role + 2, opposite_x)
        along = copy(
            buf.at[base["x"]], buf.at[base["z"]], role + 3, at_pair(jnp.where(low, 4, -4))
        )
        moves["z"] = Move(
            [(jnp.where(low, to_next, to_last), along)], jnp.where(low, to_last, to_next)
        )
        return moves

    def edge(copy, buf):
        up = parity == 0
        beside = jnp.where(up, PAIR[1], PAIR[-1])
        along = copy(buf.at[beside], buf.at[EDGE], 9, at_pair(4 * side))
        direct = copy(buf.at[PAIR[0]], buf.at[EDGE], 9, at_pair(3 * side))
        return Move(
            [(jnp.where(up, to_next, to_last), along), (corner, direct)],
            jnp.where(up, to_last | (x == 3), to_next | (x == 0)),
        )

    def legs(copy, buf, source, passing):
        half = passing.shape[0] // 2
        parts = ((pl.ds(0, half), 2, 0, 11), (pl.ds(half, half), -2, 10, 12))
        return [
            [
                copy(source.at[part], passing.at[part], role, along_y(way))
                for part, way, role, _ in parts
            ],
            [
                copy(passing.at[part], buf.at[PAIR[0], part], role, along_y(way))
                for part, way, _, role in parts
            ],
        ]

    k_leg = legs(k_copy, k_buf, k_hbm, k_relay)
    v_leg = legs(v_copy, v_buf, v_buf.at[OWN[0]], v_relay)
    k_own = spread(k_copy, k_buf, OWN, 1, k_hbm)
    v_own = spread(v_copy, v_buf, OWN, 1, v_buf.at[OWN[0]])
    k_other = spread(k_copy, k_buf, PAIR, 5, k_buf.at[PAIR[0]])
    v_other = spread(v_copy, v_buf, PAIR, 5, v_buf.at[PAIR[0]])
    k_edge, v_edge = edge(k_copy, k_buf), edge(v_copy, v_buf)
    q_moves = {mate: q_copy(*mate) for mate in mates}

    pl.semaphore_wait(barrier, answers)

    first_steps = (1, -1, "x")
    for move in k_leg[0]:
        move.start()
    for step in first_steps:
        k_own[step].start()
    q_moves[0, 1].start()
    v_load.wait()
    v_buf[OWN[0]] = v_rows[...].T
    for move in k_leg[0]:
        move.wait_send()
    for move in v_leg[0]:
        move.start()
    for step in first_steps:
        v_own[step].start()
    for mate in ((1, 0), (1, 1)):
        q_moves[mate].start()

    unused = [(base[d], jnp.logical_not(has(d))) for base in (OWN, PAIR) for d in (1, -1)]
    unused += [(base["z"], jnp.where(low, at_start, at_end)) for base in (OWN, PAIR)]
    unused.append((EDGE, jnp.logical_not(jnp.where(parity == 0, has(-3), has(3)))))
    for slot, empty in unused:
        @pl.when(empty)
        def _(slot=slot):
            k_buf[slot] = jnp.zeros(k_buf.shape[1:], k_buf.dtype)
            v_buf[slot] = jnp.zeros(v_buf.shape[1:], v_buf.dtype)

    for load in span_loads:
        load.wait()
    lane = lax.broadcasted_iota(jnp.int32, (128, 256), 1)
    row = lax.broadcasted_iota(jnp.int32, (128, 256), 0)
    for ring in range(4):
        wanted = chunk_of(ring) * 32 + (lane // 128) * 16 + lane % 16
        chosen = jnp.where(row == wanted, 1.0, 0.0).astype(jnp.bfloat16)
        for ref, held in ((first_ref, first), (last_ref, last)):
            offset_row = (ref[...] - t).astype(jnp.float32)
            offset_row = jnp.broadcast_to(offset_row, (16, 128)).astype(jnp.bfloat16)
            placed = jnp.dot(offset_row, chosen, preferred_element_type=jnp.float32)
            held[ring] = placed[0:1]

    def offset(slot):
        places = {"x": jnp.where(low, 2, -2), "z": jnp.where(low, -2, 2)}
        for base, shift in ((OWN, 0), (PAIR, side)):
            for distance, index in base.items():
                if index == slot:
                    return 2 * places.get(distance, distance) + shift
        return -5 * side

    def turn_queries(ring):
        queries = [
            q_buf[2 * chunk_of(ring) + b, :, g * HEAD_DIM:(g + 1) * HEAD_DIM]
            for b in range(2)
            for g in range(GROUP)
        ]
        q_turned[ring] = jnp.concatenate(queries, axis=0).T

    def score(ring, slot):
        return jnp.dot(k_buf[slot], q_turned[ring], preferred_element_type=jnp.float32)

    def visit(units, fresh=False, finish=None):
        scores = [score(units[0][0], slot) for slot in units[0][1]]
        ones = jnp.ones((16, tokens), jnp.bfloat16)
        for at, (ring, slots) in enumerate(units):
            following = units[at + 1] if at + 1 < len(units) else (ring, ())
            renew = fresh and all(ring != earlier for earlier, _ in units[:at])
            begin, end = first[ring], last[ring]
            inside, best = [], []
            for slot, part in zip(slots, scores):
                place = jnp.asarray(offset(slot), jnp.int32).astype(jnp.float32)
                within = (begin <= place) & (place <= end)
                inside.append(within)
                best.append(jnp.where(within, jnp.max(part, axis=0, keepdims=True), -FAR))
            top = functools.reduce(jnp.maximum, best)
            if renew:
                gained = jnp.zeros(total.shape[1:], jnp.float32)
            else:
                before = peak[ring]
                top = jnp.maximum(before, top)
                gained = total[ring] * jnp.exp2((before - top) * RATE)
            ahead = []
            for i, slot in enumerate(slots):
                if i < len(following[1]):
                    ahead.append(score(following[0], following[1][i]))
                level = jnp.where(inside[i], top, FAR)
                weights = jnp.exp2((scores[i] - level) * RATE).astype(jnp.bfloat16)
                left = jnp.concatenate([v_buf[slot], ones], axis=0)
                gained = gained + jnp.dot(left, weights, preferred_element_type=jnp.float32)
            for slot in following[1][len(slots):]:
                ahead.append(score(following[0], slot))
            if finish is None:
                peak[ring] = top
                total[ring] = gained
            else:
                finish(ring, gained)
            scores = ahead

    for move, onward in zip(k_leg[0], k_leg[1]):
        move.wait_recv()
        onward.start()
    k_own["x"].wait_recv()
    k_own["z"].start()
    for move, onward in zip(v_leg[0], v_leg[1]):
        move.wait_recv()
        onward.start()
    for mate in distant[:2]:
        q_moves[mate].start()
    for move in k_leg[1]:
        move.wait_recv()
    for step in ("x", 1, -1):
        k_other[step].start()
    v_own["x"].wait_recv()
    v_own["z"].start()
    k_load.wait()
    q_load.wait()
    for step in (1, -1):
        k_own[step].wait_recv()
        v_own[step].wait_recv()
    for mate in near:
        q_moves[mate].wait_recv()
    turn_queries(0)
    turn_queries(1)
    visit([(0, (0, 1, 2, 3)), (1, (0, 1, 2, 3))], fresh=True)

    for move in v_leg[1]:
        move.wait_recv()
    for step in ("x", 1, -1):
        v_other[step].start()
    for mate in distant[2:]:
        q_moves[mate].start()
    k_own["z"].wait_recv()
    v_own["z"].wait_recv()
    visit([(0, (4, 5)), (1, (4, 5))])

    k_other["x"].wait_recv()
    k_other["z"].start()
    k_other[1].wait_recv()
    k_other[-1].wait_recv()
    k_edge.start()
    for mate in distant[:2]:
        q_moves[mate].wait_recv()
    turn_queries(2)
    visit([(2, (0, 1, 2)), (2, (3, 4, 5))], fresh=True)

    v_other["x"].wait_recv()
    v_other["z"].start()
    v_other[1].wait_recv()
    v_other[-1].wait_recv()
    v_edge.start()
    visit([(ring, (6, 7, 8)) for ring in range(3)])
    for mate in distant[2:]:
        q_moves[mate].wait_recv()
    turn_queries(3)
    visit([(3, (0, 1, 2)), (3, (3, 4, 5)), (3, (6, 7, 8))], fresh=True)

    for move in (k_other["z"], v_other["z"], k_edge, v_edge):
        move.wait_recv()

    own_out = pltpu.make_async_copy(ready.at[h], out_ref.at[:, columns(h)], local_sem.at[3])

    def o_copy(ring, other):
        target = head_of(ring, other)
        index = 2 * ring + other
        return remote(
            ready.at[target], out_ref.at[:, columns(h)], o_send.at[index], o_recv.at[index],
            {"tm": t, "head": target},
        )

    o_moves = {mate: o_copy(*mate) for mate in mates}
    def send(ring, done):
        mean = done[:HEAD_DIM] / done[HEAD_DIM:HEAD_DIM + 1]
        turned = mean.T.astype(jnp.bfloat16)
        for b in range(2):
            for g in range(GROUP):
                begin = (b * GROUP + g) * rows
                ready[2 * chunk_of(ring) + b, :, g * HEAD_DIM:(g + 1) * HEAD_DIM] = turned[
                    begin:begin + rows
                ]
        for mate in mates:
            if mate[0] == ring:
                o_moves[mate].start()
        if ring == 0:
            own_out.start()

    visit([(ring, (9, 10)) for ring in (3, 2, 1, 0)], finish=send)

    for moves in (k_own, v_own, k_other, v_other):
        for move in moves.values():
            move.wait_send()
    for move in (k_edge, v_edge, *k_leg[1], *v_leg[0], *v_leg[1]):
        move.wait_send()
    for move in q_moves.values():
        move.wait_send()
    own_out.wait()
    for move in o_moves.values():
        move.wait_recv()
        move.wait_send()


def shards(groups, queries, vis_keys, vis_values, span_start, span_end):
    rows, width = queries.shape
    tokens = vis_keys.shape[0]
    part = width // KV_HEADS
    dma = pltpu.SemaphoreType.DMA
    spans = [span.reshape(1, -1) for span in (span_start, span_end)]
    operands = [queries, vis_keys, vis_values, *spans]
    flops = 4 * rows * width * tokens * SLOTS
    return pl.pallas_call(
        functools.partial(kernel, groups),
        out_shape=pltpu.VMEM((rows, width), jnp.bfloat16),
        in_specs=[pl.BlockSpec(memory_space=pltpu.HBM)] * 5,
        out_specs=pl.BlockSpec(memory_space=pl.ANY),
        scratch_shapes=[
            pltpu.VMEM(spans[0].shape, jnp.int32),
            pltpu.VMEM(spans[1].shape, jnp.int32),
            pltpu.VMEM((KV_HEADS, rows, part), jnp.bfloat16),
            pltpu.VMEM((4, HEAD_DIM, 256), jnp.bfloat16),
            pltpu.VMEM((SLOTS, tokens, HEAD_DIM), jnp.bfloat16),
            pltpu.VMEM((SLOTS, HEAD_DIM, tokens), jnp.bfloat16),
            pltpu.VMEM((tokens, HEAD_DIM), jnp.bfloat16),
            pltpu.VMEM((HEAD_DIM, tokens), jnp.bfloat16),
            pltpu.VMEM((tokens, HEAD_DIM), jnp.bfloat16),
            pltpu.VMEM((4, HEAD_DIM + 16, 256), jnp.float32),
            pltpu.VMEM((4, 1, 256), jnp.float32),
            pltpu.VMEM((4, 1, 256), jnp.float32),
            pltpu.VMEM((4, 1, 256), jnp.float32),
            pltpu.VMEM((KV_HEADS, rows, part), jnp.bfloat16),
            dma((6,)),
            dma((8,)),
            dma((8,)),
            dma((13,)),
            dma((13,)),
            dma((13,)),
            dma((13,)),
            dma((8,)),
            dma((8,)),
        ],
        cost_estimate=pl.CostEstimate(
            flops=flops, bytes_accessed=8 * rows * width, transcendentals=flops // 512
        ),
        compiler_params=pltpu.CompilerParams(
            collective_id=0, has_side_effects=True, vmem_limit_bytes=40 * 1024 * 1024
        ),
    )(*[pltpu.with_memory_space_constraint(value, pltpu.HBM) for value in operands])


def solution(mesh):
    return jax.shard_map(
        functools.partial(shards, mesh.shape["tm"]),
        mesh=mesh,
        in_specs=(P(("tm", "head"), None), P("tm", "head"), P("tm", "head"), P("tm"), P("tm")),
        out_specs=P(("tm", "head"), None),
        check_vma=False,
    )
```

```python
import functools
import math

import jax
import jax.numpy as jnp
from jax import lax
from jax.experimental import pallas as pl
from jax.experimental.pallas import tpu as pltpu
from jax.sharding import PartitionSpec as P

HEADS = 64
KV_HEADS = 8
HEAD_DIM = 128
MESH = pl.DeviceIdType.MESH
GROUP = HEADS // KV_HEADS
RATE = math.log2(math.e) / math.sqrt(HEAD_DIM)
FAR = 1e30

OWN = {0: 0, -1: 1, 1: 2, "x": 3, "z": 4}
PAIR = {0: 5, -1: 6, 1: 7, "x": 8, "z": 9}
EDGE, SLOTS = 10, 11


class Move:
    def __init__(self, copies, arrives):
        self.copies, self.arrives = copies, arrives

    def start(self):
        for sends, copy in self.copies:
            pl.when(sends)(copy.start)

    def wait_recv(self):
        pl.when(self.arrives)(self.copies[0][1].wait_recv)

    def wait_send(self):
        for sends, copy in self.copies:
            pl.when(sends)(copy.wait_send)


def kernel(
    groups, q_hbm, k_hbm, v_hbm, first_hbm, last_hbm, out_ref, first_ref, last_ref,
    q_buf, q_turned, k_buf, v_buf, k_relay, v_relay, v_rows, total, peak, first, last, ready,
    local_sem, q_send, q_recv, k_send, k_recv, v_send, v_recv, o_send, o_recv,
):
    t = lax.axis_index("tm")
    h = lax.axis_index("head")
    pair, parity = t // 2, t % 2
    side = 1 - 2 * parity
    x, z = pair % 4, pair // 4
    chip, core = h // 2, h % 2
    rows, width = q_buf.shape[1:]
    tokens = k_buf.shape[1]

    opposite_x = {"tm": 8 * z + 2 * ((x + 2) % 4) + parity, "head": h}

    def at_pair(distance):
        return {"tm": (t + groups + 2 * distance) % groups, "head": h}

    def along_y(distance):
        there = (4 * parity + chip + 8 + distance) % 8
        return {"tm": 2 * pair + there // 4, "head": 2 * (there % 4) + core}

    def chunk_of(ring):
        start = (chip + 2 * (ring // 2)) % 4
        return start + (ring % 2) * (1 - 2 * (start % 2))

    def columns(head):
        return pl.ds(pl.multiple_of(head * width, width), width)

    def remote(source, target, send, recv, device):
        return pltpu.make_async_remote_copy(
            source, target, send, recv, device_id=device, device_id_type=MESH
        )

    def head_of(ring, other):
        return 2 * chunk_of(ring) + (core if other == 0 else 1 - core)

    near = [(1, 0), (1, 1), (0, 1)]
    distant = [(2, 0), (2, 1), (3, 0), (3, 1)]
    mates = distant + near

    def q_copy(ring, other):
        target = head_of(ring, other)
        index = 2 * ring + other
        return remote(
            q_hbm.at[:, columns(target)], q_buf.at[h], q_send.at[index], q_recv.at[index],
            {"tm": t, "head": target},
        )

    def k_copy(source, target, role, device):
        return remote(source, target, k_send.at[role], k_recv.at[role], device)

    def v_copy(source, target, role, device):
        return remote(source, target, v_send.at[role], v_recv.at[role], device)

    k_load = pltpu.make_async_copy(k_hbm, k_buf.at[OWN[0]], local_sem.at[0])
    v_load = pltpu.make_async_copy(v_hbm, v_rows, local_sem.at[1])
    q_load = pltpu.make_async_copy(q_hbm.at[:, columns(h)], q_buf.at[h], local_sem.at[2])
    span_loads = [
        pltpu.make_async_copy(first_hbm, first_ref, local_sem.at[4]),
        pltpu.make_async_copy(last_hbm, last_ref, local_sem.at[5]),
    ]
    pairs = groups // 2
    at_start, at_end = z == 0, z == pairs // 4 - 1

    def has(distance):
        return (pair >= -distance) if distance < 0 else (pair < pairs - distance)

    barrier = pltpu.get_barrier_semaphore()
    everywhere = [along_y(2), along_y(-2), opposite_x]
    everywhere += [{"tm": t, "head": head_of(*mate)} for mate in mates]
    for partner in everywhere:
        pl.semaphore_signal(barrier, inc=1, device_id=partner, device_id_type=MESH)
    answers = len(everywhere)
    corner = jnp.where(parity == 0, pair == 0, pair == pairs - 1)
    cornered = jnp.where(parity == 0, pair == 3, pair == pairs - 4)
    others = [(has(distance), at_pair(distance)) for distance in (1, -1, 4, -4)]
    others += [(corner, at_pair(3 * side)), (cornered, at_pair(-3 * side))]
    for present, partner in others:
        answers = answers + jnp.where(present, 1, 0)

        @pl.when(present)
        def _(partner=partner):
            pl.semaphore_signal(barrier, inc=1, device_id=partner, device_id_type=MESH)

    for load in (v_load, k_load, *span_loads, q_load):
        load.start()

    low = x < 2
    to_next, to_last = jnp.logical_not(at_end), jnp.logical_not(at_start)

    def spread(copy, buf, base, role, source):
        moves = {
            e: Move(
                [(has(e), copy(source, buf.at[base[-e]], role + i, at_pair(e)))],
                has(-e),
            )
            for i, e in enumerate((1, -1))
        }
        moves["x"] = copy(source, buf.at[base["x"]], role + 2, opposite_x)
        along = copy(
            buf.at[base["x"]], buf.at[base["z"]], role + 3, at_pair(jnp.where(low, 4, -4))
        )
        moves["z"] = Move(
            [(jnp.where(low, to_next, to_last), along)], jnp.where(low, to_last, to_next)
        )
        return moves

    def edge(copy, buf):
        up = parity == 0
        beside = jnp.where(up, PAIR[1], PAIR[-1])
        along = copy(buf.at[beside], buf.at[EDGE], 9, at_pair(4 * side))
        direct = copy(buf.at[PAIR[0]], buf.at[EDGE], 9, at_pair(3 * side))
        return Move(
            [(jnp.where(up, to_next, to_last), along), (corner, direct)],
            jnp.where(up, to_last | (x == 3), to_next | (x == 0)),
        )

    def legs(copy, buf, source, passing):
        half = passing.shape[0] // 2
        parts = ((pl.ds(0, half), 2, 0, 11), (pl.ds(half, half), -2, 10, 12))
        return [
            [
                copy(source.at[part], passing.at[part], role, along_y(way))
                for part, way, role, _ in parts
            ],
            [
                copy(passing.at[part], buf.at[PAIR[0], part], role, along_y(way))
                for part, way, _, role in parts
            ],
        ]

    k_leg = legs(k_copy, k_buf, k_hbm, k_relay)
    v_leg = legs(v_copy, v_buf, v_buf.at[OWN[0]], v_relay)
    k_own = spread(k_copy, k_buf, OWN, 1, k_hbm)
    v_own = spread(v_copy, v_buf, OWN, 1, v_buf.at[OWN[0]])
    k_other = spread(k_copy, k_buf, PAIR, 5, k_buf.at[PAIR[0]])
    v_other = spread(v_copy, v_buf, PAIR, 5, v_buf.at[PAIR[0]])
    k_edge, v_edge = edge(k_copy, k_buf), edge(v_copy, v_buf)
    q_moves = {mate: q_copy(*mate) for mate in mates}

    pl.semaphore_wait(barrier, answers)

    first_steps = (1, -1, "x")
    for move in k_leg[0]:
        move.start()
    for step in first_steps:
        k_own[step].start()
    q_moves[0, 1].start()
    v_load.wait()
    v_buf[OWN[0]] = v_rows[...].T
    for move in k_leg[0]:
        move.wait_send()
    for move in v_leg[0]:
        move.start()
    for step in first_steps:
        v_own[step].start()
    for mate in ((1, 0), (1, 1)):
        q_moves[mate].start()

    unused = [(base[d], jnp.logical_not(has(d))) for base in (OWN, PAIR) for d in (1, -1)]
    unused += [(base["z"], jnp.where(low, at_start, at_end)) for base in (OWN, PAIR)]
    unused.append((EDGE, jnp.logical_not(jnp.where(parity == 0, has(-3), has(3)))))
    for slot, empty in unused:
        @pl.when(empty)
        def _(slot=slot):
            k_buf[slot] = jnp.zeros(k_buf.shape[1:], k_buf.dtype)
            v_buf[slot] = jnp.zeros(v_buf.shape[1:], v_buf.dtype)

    for load in span_loads:
        load.wait()
    lane = lax.broadcasted_iota(jnp.int32, (128, 256), 1)
    row = lax.broadcasted_iota(jnp.int32, (128, 256), 0)
    for ring in range(4):
        wanted = chunk_of(ring) * 32 + (lane // 128) * 16 + lane % 16
        chosen = jnp.where(row == wanted, 1.0, 0.0).astype(jnp.bfloat16)
        for ref, held in ((first_ref, first), (last_ref, last)):
            offset_row = (ref[...] - t).astype(jnp.float32)
            offset_row = jnp.broadcast_to(offset_row, (16, 128)).astype(jnp.bfloat16)
            placed = jnp.dot(offset_row, chosen, preferred_element_type=jnp.float32)
            held[ring] = placed[0:1]

    def offset(slot):
        places = {"x": jnp.where(low, 2, -2), "z": jnp.where(low, -2, 2)}
        for base, shift in ((OWN, 0), (PAIR, side)):
            for distance, index in base.items():
                if index == slot:
                    return 2 * places.get(distance, distance) + shift
        return -5 * side

    def turn_queries(ring):
        queries = [
            q_buf[2 * chunk_of(ring) + b, :, g * HEAD_DIM:(g + 1) * HEAD_DIM]
            for b in range(2)
            for g in range(GROUP)
        ]
        q_turned[ring] = jnp.concatenate(queries, axis=0).T

    def score(ring, slot):
        return jnp.dot(k_buf[slot], q_turned[ring], preferred_element_type=jnp.float32)

    def visit(units, fresh=False, finish=None):
        scores = [score(units[0][0], slot) for slot in units[0][1]]
        ones = jnp.ones((16, tokens), jnp.bfloat16)
        for at, (ring, slots) in enumerate(units):
            following = units[at + 1] if at + 1 < len(units) else (ring, ())
            renew = fresh and at == 0
            begin, end = first[ring], last[ring]
            inside, best = [], []
            for slot, part in zip(slots, scores):
                place = jnp.asarray(offset(slot), jnp.int32).astype(jnp.float32)
                within = (begin <= place) & (place <= end)
                inside.append(within)
                best.append(jnp.where(within, jnp.max(part, axis=0, keepdims=True), -FAR))
            top = functools.reduce(jnp.maximum, best)
            if renew:
                gained = jnp.zeros(total.shape[1:], jnp.float32)
            else:
                before = peak[ring]
                top = jnp.maximum(before, top)
                gained = total[ring] * jnp.exp2((before - top) * RATE)
            ahead = []
            for i, slot in enumerate(slots):
                if i < len(following[1]):
                    ahead.append(score(following[0], following[1][i]))
                level = jnp.where(inside[i], top, FAR)
                weights = jnp.exp2((scores[i] - level) * RATE).astype(jnp.bfloat16)
                left = jnp.concatenate([v_buf[slot], ones], axis=0)
                gained = gained + jnp.dot(left, weights, preferred_element_type=jnp.float32)
            for slot in following[1][len(slots):]:
                ahead.append(score(following[0], slot))
            if finish is not None:
                finish(ring, gained)
            else:
                peak[ring] = top
                total[ring] = gained
            scores = ahead

    def over_rings(count, slots, fresh=False):
        def body(ring, carry):
            visit([(ring, slots)], fresh)
            return carry

        lax.fori_loop(0, count, body, 0)

    for move, onward in zip(k_leg[0], k_leg[1]):
        move.wait_recv()
        onward.start()
    k_own["x"].wait_recv()
    k_own["z"].start()
    for move, onward in zip(v_leg[0], v_leg[1]):
        move.wait_recv()
        onward.start()
    for mate in distant[:2]:
        q_moves[mate].start()
    for move in k_leg[1]:
        move.wait_recv()
    for step in ("x", 1, -1):
        k_other[step].start()
    v_own["x"].wait_recv()
    v_own["z"].start()
    k_load.wait()
    q_load.wait()
    for step in (1, -1):
        k_own[step].wait_recv()
        v_own[step].wait_recv()
    for mate in near:
        q_moves[mate].wait_recv()
    turn_queries(0)
    turn_queries(1)
    over_rings(2, (0, 1, 2, 3), fresh=True)

    for move in v_leg[1]:
        move.wait_recv()
    for step in ("x", 1, -1):
        v_other[step].start()
    for mate in distant[2:]:
        q_moves[mate].start()
    k_own["z"].wait_recv()
    v_own["z"].wait_recv()
    over_rings(2, (4, 5))

    k_other["x"].wait_recv()
    k_other["z"].start()
    k_other[1].wait_recv()
    k_other[-1].wait_recv()
    k_edge.start()
    for mate in distant[:2]:
        q_moves[mate].wait_recv()
    turn_queries(2)
    visit([(2, (0, 1, 2)), (2, (3, 4, 5))], fresh=True)

    v_other["x"].wait_recv()
    v_other["z"].start()
    v_other[1].wait_recv()
    v_other[-1].wait_recv()
    v_edge.start()
    over_rings(3, (6, 7, 8))
    for mate in distant[2:]:
        q_moves[mate].wait_recv()
    turn_queries(3)
    visit([(3, (0, 1, 2)), (3, (3, 4, 5)), (3, (6, 7, 8))], fresh=True)

    for move in (k_other["z"], v_other["z"], k_edge, v_edge):
        move.wait_recv()

    own_out = pltpu.make_async_copy(ready.at[h], out_ref.at[:, columns(h)], local_sem.at[3])

    def o_copy(ring, other):
        target = head_of(ring, other)
        index = 2 * ring + other
        return remote(
            ready.at[target], out_ref.at[:, columns(h)], o_send.at[index], o_recv.at[index],
            {"tm": t, "head": target},
        )

    def send(ring, done):
        mean = done[:HEAD_DIM] / done[HEAD_DIM:HEAD_DIM + 1]
        turned = mean.T.astype(jnp.bfloat16)
        for b in range(2):
            target = 2 * chunk_of(ring) + b
            for g in range(GROUP):
                begin = (b * GROUP + g) * rows
                ready[target, :, g * HEAD_DIM:(g + 1) * HEAD_DIM] = turned[begin:begin + rows]

    def last_stage(i, carry):
        ring = 3 - i
        visit([(ring, (9, 10))], finish=send)
        o_copy(ring, 1).start()

        @pl.when(ring > 0)
        def _():
            o_copy(ring, 0).start()

        @pl.when(ring == 0)
        def _():
            own_out.start()

        return carry

    lax.fori_loop(0, 4, last_stage, 0)
    o_moves = {mate: o_copy(*mate) for mate in mates}

    for moves in (k_own, v_own, k_other, v_other):
        for move in moves.values():
            move.wait_send()
    for move in (k_edge, v_edge, *k_leg[1], *v_leg[0], *v_leg[1]):
        move.wait_send()
    for move in q_moves.values():
        move.wait_send()
    own_out.wait()
    for move in o_moves.values():
        move.wait_recv()
        move.wait_send()


def shards(groups, queries, vis_keys, vis_values, span_start, span_end):
    rows, width = queries.shape
    tokens = vis_keys.shape[0]
    part = width // KV_HEADS
    dma = pltpu.SemaphoreType.DMA
    spans = [span.reshape(1, -1) for span in (span_start, span_end)]
    operands = [queries, vis_keys, vis_values, *spans]
    flops = 4 * rows * width * tokens * SLOTS
    return pl.pallas_call(
        functools.partial(kernel, groups),
        out_shape=pltpu.VMEM((rows, width), jnp.bfloat16),
        in_specs=[pl.BlockSpec(memory_space=pltpu.HBM)] * 5,
        out_specs=pl.BlockSpec(memory_space=pl.ANY),
        scratch_shapes=[
            pltpu.VMEM(spans[0].shape, jnp.int32),
            pltpu.VMEM(spans[1].shape, jnp.int32),
            pltpu.VMEM((KV_HEADS, rows, part), jnp.bfloat16),
            pltpu.VMEM((4, HEAD_DIM, 256), jnp.bfloat16),
            pltpu.VMEM((SLOTS, tokens, HEAD_DIM), jnp.bfloat16),
            pltpu.VMEM((SLOTS, HEAD_DIM, tokens), jnp.bfloat16),
            pltpu.VMEM((tokens, HEAD_DIM), jnp.bfloat16),
            pltpu.VMEM((HEAD_DIM, tokens), jnp.bfloat16),
            pltpu.VMEM((tokens, HEAD_DIM), jnp.bfloat16),
            pltpu.VMEM((4, HEAD_DIM + 16, 256), jnp.float32),
            pltpu.VMEM((4, 1, 256), jnp.float32),
            pltpu.VMEM((4, 1, 256), jnp.float32),
            pltpu.VMEM((4, 1, 256), jnp.float32),
            pltpu.VMEM((KV_HEADS, rows, part), jnp.bfloat16),
            dma((6,)),
            dma((8,)),
            dma((8,)),
            dma((13,)),
            dma((13,)),
            dma((13,)),
            dma((13,)),
            dma((8,)),
            dma((8,)),
        ],
        cost_estimate=pl.CostEstimate(
            flops=flops, bytes_accessed=8 * rows * width, transcendentals=flops // 512
        ),
        compiler_params=pltpu.CompilerParams(
            collective_id=0, has_side_effects=True, vmem_limit_bytes=40 * 1024 * 1024
        ),
    )(*[pltpu.with_memory_space_constraint(value, pltpu.HBM) for value in operands])


def solution(mesh):
    return jax.shard_map(
        functools.partial(shards, mesh.shape["tm"]),
        mesh=mesh,
        in_specs=(P(("tm", "head"), None), P("tm", "head"), P("tm", "head"), P("tm"), P("tm")),
        out_specs=P(("tm", "head"), None),
        check_vma=False,
    )
```

```python
import functools
import math

import jax
import jax.numpy as jnp
from jax import lax
from jax.experimental import pallas as pl
from jax.experimental.pallas import tpu as pltpu
from jax.sharding import PartitionSpec as P

HEADS = 64
KV_HEADS = 8
HEAD_DIM = 128
MESH = pl.DeviceIdType.MESH
GROUP = HEADS // KV_HEADS
RATE = math.log2(math.e) / math.sqrt(HEAD_DIM)
FAR = 1e30

OWN = {0: 0, -1: 1, 1: 2, "x": 3, "z": 4}
PAIR = {0: 5, -1: 6, 1: 7, "x": 8, "z": 9}
EDGE, SLOTS = 10, 11


class Move:
    def __init__(self, copies, arrives):
        self.copies, self.arrives = copies, arrives

    def start(self):
        for sends, copy in self.copies:
            pl.when(sends)(copy.start)

    def wait_recv(self):
        pl.when(self.arrives)(self.copies[0][1].wait_recv)

    def wait_send(self):
        for sends, copy in self.copies:
            pl.when(sends)(copy.wait_send)


def kernel(
    groups, q_hbm, k_hbm, v_hbm, first_hbm, last_hbm, out_ref, first_ref, last_ref,
    q_buf, q_turned, k_buf, v_buf, k_relay, v_relay, v_rows, total, peak, first, last, ready,
    local_sem, q_send, q_recv, k_send, k_recv, v_send, v_recv, o_send, o_recv,
):
    t = lax.axis_index("tm")
    h = lax.axis_index("head")
    pair, parity = t // 2, t % 2
    side = 1 - 2 * parity
    x, z = pair % 4, pair // 4
    chip, core = h // 2, h % 2
    rows, width = q_buf.shape[1:]
    tokens = k_buf.shape[1]

    opposite_x = {"tm": 8 * z + 2 * ((x + 2) % 4) + parity, "head": h}

    def at_pair(distance):
        return {"tm": (t + groups + 2 * distance) % groups, "head": h}

    def along_y(distance):
        there = (4 * parity + chip + 8 + distance) % 8
        return {"tm": 2 * pair + there // 4, "head": 2 * (there % 4) + core}

    def flip(value):
        return value + 1 - 2 * (value % 2)

    def chunk_of(ring):
        start = chip if ring < 2 else (chip + 2) % 4
        return start if ring % 2 == 0 else flip(start)

    def columns(head):
        return pl.ds(pl.multiple_of(head * width, width), width)

    def remote(source, target, send, recv, device):
        return pltpu.make_async_remote_copy(
            source, target, send, recv, device_id=device, device_id_type=MESH
        )

    def head_of(ring, other):
        return 2 * chunk_of(ring) + (core if other == 0 else 1 - core)

    near = [(1, 0), (1, 1), (0, 1)]
    distant = [(2, 0), (2, 1), (3, 0), (3, 1)]
    mates = distant + near

    def q_copy(ring, other):
        target = head_of(ring, other)
        index = 2 * ring + other
        return remote(
            q_hbm.at[:, columns(target)], q_buf.at[h], q_send.at[index], q_recv.at[index],
            {"tm": t, "head": target},
        )

    def k_copy(source, target, role, device):
        return remote(source, target, k_send.at[role], k_recv.at[role], device)

    def v_copy(source, target, role, device):
        return remote(source, target, v_send.at[role], v_recv.at[role], device)

    k_load = pltpu.make_async_copy(k_hbm, k_buf.at[OWN[0]], local_sem.at[0])
    v_load = pltpu.make_async_copy(v_hbm, v_rows, local_sem.at[1])
    q_load = pltpu.make_async_copy(q_hbm.at[:, columns(h)], q_buf.at[h], local_sem.at[2])
    span_loads = [
        pltpu.make_async_copy(first_hbm, first_ref, local_sem.at[4]),
        pltpu.make_async_copy(last_hbm, last_ref, local_sem.at[5]),
    ]
    pairs = groups // 2
    at_start, at_end = z == 0, z == pairs // 4 - 1

    def has(distance):
        return (pair >= -distance) if distance < 0 else (pair < pairs - distance)

    barrier = pltpu.get_barrier_semaphore()
    everywhere = [along_y(2), along_y(-2), opposite_x]
    everywhere += [{"tm": t, "head": head_of(*mate)} for mate in mates]
    for partner in everywhere:
        pl.semaphore_signal(barrier, inc=1, device_id=partner, device_id_type=MESH)
    answers = len(everywhere)
    corner = jnp.where(parity == 0, pair == 0, pair == pairs - 1)
    cornered = jnp.where(parity == 0, pair == 3, pair == pairs - 4)
    others = [(has(distance), at_pair(distance)) for distance in (1, -1, 4, -4)]
    others += [(corner, at_pair(3 * side)), (cornered, at_pair(-3 * side))]
    for present, partner in others:
        answers = answers + jnp.where(present, 1, 0)

        @pl.when(present)
        def _(partner=partner):
            pl.semaphore_signal(barrier, inc=1, device_id=partner, device_id_type=MESH)

    for load in (v_load, k_load, *span_loads, q_load):
        load.start()

    low = x < 2
    to_next, to_last = jnp.logical_not(at_end), jnp.logical_not(at_start)

    def spread(copy, buf, base, role, source):
        moves = {
            e: Move(
                [(has(e), copy(source, buf.at[base[-e]], role + i, at_pair(e)))],
                has(-e),
            )
            for i, e in enumerate((1, -1))
        }
        moves["x"] = copy(source, buf.at[base["x"]], role + 2, opposite_x)
        along = copy(
            buf.at[base["x"]], buf.at[base["z"]], role + 3, at_pair(jnp.where(low, 4, -4))
        )
        moves["z"] = Move(
            [(jnp.where(low, to_next, to_last), along)], jnp.where(low, to_last, to_next)
        )
        return moves

    def edge(copy, buf):
        up = parity == 0
        beside = jnp.where(up, PAIR[1], PAIR[-1])
        along = copy(buf.at[beside], buf.at[EDGE], 9, at_pair(4 * side))
        direct = copy(buf.at[PAIR[0]], buf.at[EDGE], 9, at_pair(3 * side))
        return Move(
            [(jnp.where(up, to_next, to_last), along), (corner, direct)],
            jnp.where(up, to_last | (x == 3), to_next | (x == 0)),
        )

    def legs(copy, buf, source, passing):
        half = passing.shape[0] // 2
        parts = ((pl.ds(0, half), 2, 0, 11), (pl.ds(half, half), -2, 10, 12))
        return [
            [
                copy(source.at[part], passing.at[part], role, along_y(way))
                for part, way, role, _ in parts
            ],
            [
                copy(passing.at[part], buf.at[PAIR[0], part], role, along_y(way))
                for part, way, _, role in parts
            ],
        ]

    k_leg = legs(k_copy, k_buf, k_hbm, k_relay)
    v_leg = legs(v_copy, v_buf, v_buf.at[OWN[0]], v_relay)
    k_own = spread(k_copy, k_buf, OWN, 1, k_hbm)
    v_own = spread(v_copy, v_buf, OWN, 1, v_buf.at[OWN[0]])
    k_other = spread(k_copy, k_buf, PAIR, 5, k_buf.at[PAIR[0]])
    v_other = spread(v_copy, v_buf, PAIR, 5, v_buf.at[PAIR[0]])
    k_edge, v_edge = edge(k_copy, k_buf), edge(v_copy, v_buf)
    q_moves = {mate: q_copy(*mate) for mate in mates}

    pl.semaphore_wait(barrier, answers)

    first_steps = (1, -1, "x")
    for move in k_leg[0]:
        move.start()
    for step in first_steps:
        k_own[step].start()
    q_moves[0, 1].start()
    v_load.wait()
    v_buf[OWN[0]] = v_rows[...].T
    for move in k_leg[0]:
        move.wait_send()
    for move in v_leg[0]:
        move.start()
    for step in first_steps:
        v_own[step].start()
    for mate in ((1, 0), (1, 1)):
        q_moves[mate].start()

    unused = [(base[d], jnp.logical_not(has(d))) for base in (OWN, PAIR) for d in (1, -1)]
    unused += [(base["z"], jnp.where(low, at_start, at_end)) for base in (OWN, PAIR)]
    unused.append((EDGE, jnp.logical_not(jnp.where(parity == 0, has(-3), has(3)))))
    for slot, empty in unused:
        @pl.when(empty)
        def _(slot=slot):
            k_buf[slot] = jnp.zeros(k_buf.shape[1:], k_buf.dtype)
            v_buf[slot] = jnp.zeros(v_buf.shape[1:], v_buf.dtype)

    for load in span_loads:
        load.wait()
    lane = lax.broadcasted_iota(jnp.int32, (128, 256), 1)
    row = lax.broadcasted_iota(jnp.int32, (128, 256), 0)
    for ring in range(4):
        wanted = chunk_of(ring) * 32 + (lane // 128) * 16 + lane % 16
        chosen = jnp.where(row == wanted, 1.0, 0.0).astype(jnp.bfloat16)
        for ref, held in ((first_ref, first), (last_ref, last)):
            offset_row = (ref[...] - t).astype(jnp.float32)
            offset_row = jnp.broadcast_to(offset_row, (16, 128)).astype(jnp.bfloat16)
            placed = jnp.dot(offset_row, chosen, preferred_element_type=jnp.float32)
            held[ring] = placed[0:1]

    def offset(slot):
        places = {"x": jnp.where(low, 2, -2), "z": jnp.where(low, -2, 2)}
        for base, shift in ((OWN, 0), (PAIR, side)):
            for distance, index in base.items():
                if index == slot:
                    return 2 * places.get(distance, distance) + shift
        return -5 * side

    def turn_queries(ring):
        queries = [
            q_buf[2 * chunk_of(ring) + b, :, g * HEAD_DIM:(g + 1) * HEAD_DIM]
            for b in range(2)
            for g in range(GROUP)
        ]
        q_turned[ring] = jnp.concatenate(queries, axis=0).T

    def score(ring, slot):
        return jnp.dot(k_buf[slot], q_turned[ring], preferred_element_type=jnp.float32)

    def visit(units, fresh=(), finish=None):
        scores = [score(units[0][0], slot) for slot in units[0][1]]
        ones = jnp.ones((16, tokens), jnp.bfloat16)
        for at, (ring, slots) in enumerate(units):
            following = units[at + 1] if at + 1 < len(units) else (ring, ())
            renew = ring in fresh and all(ring != earlier for earlier, _ in units[:at])
            begin, end = first[ring], last[ring]
            inside, best = [], []
            for slot, part in zip(slots, scores):
                place = jnp.asarray(offset(slot), jnp.int32).astype(jnp.float32)
                within = (begin <= place) & (place <= end)
                inside.append(within)
                best.append(jnp.where(within, jnp.max(part, axis=0, keepdims=True), -FAR))
            top = functools.reduce(jnp.maximum, best)
            if renew:
                gained = jnp.zeros(total.shape[1:], jnp.float32)
            else:
                before = peak[ring]
                top = jnp.maximum(before, top)
                gained = total[ring] * jnp.exp2((before - top) * RATE)
            ahead = []
            for i, slot in enumerate(slots):
                if i < len(following[1]):
                    ahead.append(score(following[0], following[1][i]))
                level = jnp.where(inside[i], top, FAR)
                weights = jnp.exp2((scores[i] - level) * RATE).astype(jnp.bfloat16)
                left = jnp.concatenate([v_buf[slot], ones], axis=0)
                gained = gained + jnp.dot(left, weights, preferred_element_type=jnp.float32)
            for slot in following[1][len(slots):]:
                ahead.append(score(following[0], slot))
            if finish is None:
                peak[ring] = top
                total[ring] = gained
            else:
                finish(ring, gained)
            scores = ahead

    for move, onward in zip(k_leg[0], k_leg[1]):
        move.wait_recv()
        onward.start()
    k_own["x"].wait_recv()
    k_own["z"].start()
    for move, onward in zip(v_leg[0], v_leg[1]):
        move.wait_recv()
        onward.start()
    for mate in distant[:2]:
        q_moves[mate].start()
    for move in k_leg[1]:
        move.wait_recv()
    for step in ("x", 1, -1):
        k_other[step].start()
    v_own["x"].wait_recv()
    v_own["z"].start()
    k_load.wait()
    q_load.wait()
    for step in (1, -1):
        k_own[step].wait_recv()
        v_own[step].wait_recv()
    for mate in near:
        q_moves[mate].wait_recv()
    turn_queries(0)
    turn_queries(1)
    visit([(0, (0, 1, 2, 3)), (1, (0, 1, 2, 3))], fresh=(0, 1))

    for move in v_leg[1]:
        move.wait_recv()
    for step in ("x", 1, -1):
        v_other[step].start()
    for mate in distant[2:]:
        q_moves[mate].start()
    k_own["z"].wait_recv()
    v_own["z"].wait_recv()
    k_other["x"].wait_recv()
    k_other["z"].start()
    k_other[1].wait_recv()
    k_other[-1].wait_recv()
    k_edge.start()
    for mate in distant[:2]:
        q_moves[mate].wait_recv()
    turn_queries(2)
    visit([(2, (0, 1, 2)), (0, (4, 5)), (2, (3, 4, 5)), (1, (4, 5))], fresh=(2,))

    v_other["x"].wait_recv()
    v_other["z"].start()
    v_other[1].wait_recv()
    v_other[-1].wait_recv()
    v_edge.start()
    for mate in distant[2:]:
        q_moves[mate].wait_recv()
    turn_queries(3)
    units = [(3, (0, 1, 2)), (0, (6, 7, 8)), (3, (3, 4, 5)), (1, (6, 7, 8)), (3, (6, 7, 8))]
    visit(units + [(2, (6, 7, 8))], fresh=(3,))

    for move in (k_other["z"], v_other["z"], k_edge, v_edge):
        move.wait_recv()

    own_out = pltpu.make_async_copy(ready.at[h], out_ref.at[:, columns(h)], local_sem.at[3])

    def o_copy(ring, other):
        target = head_of(ring, other)
        index = 2 * ring + other
        return remote(
            ready.at[target], out_ref.at[:, columns(h)], o_send.at[index], o_recv.at[index],
            {"tm": t, "head": target},
        )

    o_moves = {mate: o_copy(*mate) for mate in mates}
    def send(ring, done):
        mean = done[:HEAD_DIM] * (1.0 / done[HEAD_DIM:HEAD_DIM + 1])
        turned = mean.astype(jnp.bfloat16).T
        for b in range(2):
            for g in range(GROUP):
                begin = (b * GROUP + g) * rows
                ready[2 * chunk_of(ring) + b, :, g * HEAD_DIM:(g + 1) * HEAD_DIM] = turned[
                    begin:begin + rows
                ]
        for mate in mates:
            if mate[0] == ring:
                o_moves[mate].start()
        if ring == 0:
            own_out.start()

    visit([(ring, (9, 10)) for ring in (3, 2, 1, 0)], finish=send)

    for moves in (k_own, v_own, k_other, v_other):
        for move in moves.values():
            move.wait_send()
    for move in (k_edge, v_edge, *k_leg[1], *v_leg[0], *v_leg[1]):
        move.wait_send()
    for move in q_moves.values():
        move.wait_send()
    own_out.wait()
    for move in o_moves.values():
        move.wait_recv()
        move.wait_send()


def shards(groups, queries, vis_keys, vis_values, span_start, span_end):
    rows, width = queries.shape
    tokens = vis_keys.shape[0]
    part = width // KV_HEADS
    dma = pltpu.SemaphoreType.DMA
    spans = [span.reshape(1, -1) for span in (span_start, span_end)]
    operands = [queries, vis_keys, vis_values, *spans]
    flops = 4 * rows * width * tokens * SLOTS
    return pl.pallas_call(
        functools.partial(kernel, groups),
        out_shape=pltpu.VMEM((rows, width), jnp.bfloat16),
        in_specs=[pl.BlockSpec(memory_space=pltpu.HBM)] * 5,
        out_specs=pl.BlockSpec(memory_space=pl.ANY),
        scratch_shapes=[
            pltpu.VMEM(spans[0].shape, jnp.int32),
            pltpu.VMEM(spans[1].shape, jnp.int32),
            pltpu.VMEM((KV_HEADS, rows, part), jnp.bfloat16),
            pltpu.VMEM((4, HEAD_DIM, 256), jnp.bfloat16),
            pltpu.VMEM((SLOTS, tokens, HEAD_DIM), jnp.bfloat16),
            pltpu.VMEM((SLOTS, HEAD_DIM, tokens), jnp.bfloat16),
            pltpu.VMEM((tokens, HEAD_DIM), jnp.bfloat16),
            pltpu.VMEM((HEAD_DIM, tokens), jnp.bfloat16),
            pltpu.VMEM((tokens, HEAD_DIM), jnp.bfloat16),
            pltpu.VMEM((4, HEAD_DIM + 16, 256), jnp.float32),
            pltpu.VMEM((4, 1, 256), jnp.float32),
            pltpu.VMEM((4, 1, 256), jnp.float32),
            pltpu.VMEM((4, 1, 256), jnp.float32),
            pltpu.VMEM((KV_HEADS, rows, part), jnp.bfloat16),
            dma((6,)),
            dma((8,)),
            dma((8,)),
            dma((13,)),
            dma((13,)),
            dma((13,)),
            dma((13,)),
            dma((8,)),
            dma((8,)),
        ],
        cost_estimate=pl.CostEstimate(
            flops=flops, bytes_accessed=8 * rows * width, transcendentals=flops // 512
        ),
        compiler_params=pltpu.CompilerParams(
            collective_id=0, has_side_effects=True, vmem_limit_bytes=40 * 1024 * 1024
        ),
    )(*[pltpu.with_memory_space_constraint(value, pltpu.HBM) for value in operands])


def solution(mesh):
    return jax.shard_map(
        functools.partial(shards, mesh.shape["tm"]),
        mesh=mesh,
        in_specs=(P(("tm", "head"), None), P("tm", "head"), P("tm", "head"), P("tm"), P("tm")),
        out_specs=P(("tm", "head"), None),
        check_vma=False,
    )
```

```python
import functools
import math

import jax
import jax.numpy as jnp
from jax import lax
from jax.experimental import pallas as pl
from jax.experimental.pallas import tpu as pltpu
from jax.sharding import PartitionSpec as P

HEADS = 64
KV_HEADS = 8
HEAD_DIM = 128
MESH = pl.DeviceIdType.MESH
GROUP = HEADS // KV_HEADS
RATE = math.log2(math.e) / math.sqrt(HEAD_DIM)
FAR = 1e30

OWN = {0: 0, -1: 1, 1: 2, "x": 3, "z": 4}
PAIR = {0: 5, -1: 6, 1: 7, "x": 8, "z": 9}
EDGE, SLOTS = 10, 11


class Move:
    def __init__(self, copies, arrives):
        self.copies, self.arrives = copies, arrives

    def start(self):
        for sends, copy in self.copies:
            pl.when(sends)(copy.start)

    def wait_recv(self):
        pl.when(self.arrives)(self.copies[0][1].wait_recv)

    def wait_send(self):
        for sends, copy in self.copies:
            pl.when(sends)(copy.wait_send)


def kernel(
    groups, q_hbm, k_hbm, v_hbm, first_hbm, last_hbm, out_ref, first_ref, last_ref,
    q_buf, q_turned, k_buf, v_buf, k_relay, v_relay, v_rows, total, peak, first, last, ready,
    local_sem, q_send, q_recv, k_send, k_recv, v_send, v_recv, o_send, o_recv,
):
    t = lax.axis_index("tm")
    h = lax.axis_index("head")
    pair, parity = t // 2, t % 2
    side = 1 - 2 * parity
    x, z = pair % 4, pair // 4
    chip, core = h // 2, h % 2
    rows, width = q_buf.shape[1:]
    tokens = k_buf.shape[1]

    opposite_x = {"tm": 8 * z + 2 * ((x + 2) % 4) + parity, "head": h}

    def at_pair(distance):
        return {"tm": (t + groups + 2 * distance) % groups, "head": h}

    def along_y(distance):
        there = (4 * parity + chip + 8 + distance) % 8
        return {"tm": 2 * pair + there // 4, "head": 2 * (there % 4) + core}

    def flip(value):
        return value + 1 - 2 * (value % 2)

    def chunk_of(ring):
        start = chip if ring < 2 else (chip + 2) % 4
        return start if ring % 2 == 0 else flip(start)

    def columns(head):
        return pl.ds(pl.multiple_of(head * width, width), width)

    def remote(source, target, send, recv, device):
        return pltpu.make_async_remote_copy(
            source, target, send, recv, device_id=device, device_id_type=MESH
        )

    def head_of(ring, other):
        return 2 * chunk_of(ring) + (core if other == 0 else 1 - core)

    near = [(1, 0), (1, 1), (0, 1)]
    distant = [(2, 0), (2, 1), (3, 0), (3, 1)]
    mates = distant + near

    def q_copy(ring, other):
        target = head_of(ring, other)
        index = 2 * ring + other
        return remote(
            q_hbm.at[:, columns(target)], q_buf.at[h], q_send.at[index], q_recv.at[index],
            {"tm": t, "head": target},
        )

    def k_copy(source, target, role, device):
        return remote(source, target, k_send.at[role], k_recv.at[role], device)

    def v_copy(source, target, role, device):
        return remote(source, target, v_send.at[role], v_recv.at[role], device)

    k_load = pltpu.make_async_copy(k_hbm, k_buf.at[OWN[0]], local_sem.at[0])
    v_load = pltpu.make_async_copy(v_hbm, v_rows, local_sem.at[1])
    q_load = pltpu.make_async_copy(q_hbm.at[:, columns(h)], q_buf.at[h], local_sem.at[2])
    span_loads = [
        pltpu.make_async_copy(first_hbm, first_ref, local_sem.at[4]),
        pltpu.make_async_copy(last_hbm, last_ref, local_sem.at[5]),
    ]
    pairs = groups // 2
    at_start, at_end = z == 0, z == pairs // 4 - 1

    def has(distance):
        return (pair >= -distance) if distance < 0 else (pair < pairs - distance)

    barrier = pltpu.get_barrier_semaphore()
    everywhere = [along_y(2), along_y(-2), opposite_x]
    everywhere += [{"tm": t, "head": head_of(*mate)} for mate in mates]
    for partner in everywhere:
        pl.semaphore_signal(barrier, inc=1, device_id=partner, device_id_type=MESH)
    answers = len(everywhere)
    corner = jnp.where(parity == 0, pair == 0, pair == pairs - 1)
    cornered = jnp.where(parity == 0, pair == 3, pair == pairs - 4)
    others = [(has(distance), at_pair(distance)) for distance in (1, -1, 4, -4)]
    others += [(corner, at_pair(3 * side)), (cornered, at_pair(-3 * side))]
    for present, partner in others:
        answers = answers + jnp.where(present, 1, 0)

        @pl.when(present)
        def _(partner=partner):
            pl.semaphore_signal(barrier, inc=1, device_id=partner, device_id_type=MESH)

    for load in (v_load, k_load, *span_loads, q_load):
        load.start()

    low = x < 2
    to_next, to_last = jnp.logical_not(at_end), jnp.logical_not(at_start)

    def spread(copy, buf, base, role, source):
        moves = {
            e: Move(
                [(has(e), copy(source, buf.at[base[-e]], role + i, at_pair(e)))],
                has(-e),
            )
            for i, e in enumerate((1, -1))
        }
        moves["x"] = copy(source, buf.at[base["x"]], role + 2, opposite_x)
        along = copy(
            buf.at[base["x"]], buf.at[base["z"]], role + 3, at_pair(jnp.where(low, 4, -4))
        )
        moves["z"] = Move(
            [(jnp.where(low, to_next, to_last), along)], jnp.where(low, to_last, to_next)
        )
        return moves

    def edge(copy, buf):
        up = parity == 0
        beside = jnp.where(up, PAIR[1], PAIR[-1])
        along = copy(buf.at[beside], buf.at[EDGE], 9, at_pair(4 * side))
        direct = copy(buf.at[PAIR[0]], buf.at[EDGE], 9, at_pair(3 * side))
        return Move(
            [(jnp.where(up, to_next, to_last), along), (corner, direct)],
            jnp.where(up, to_last | (x == 3), to_next | (x == 0)),
        )

    def legs(copy, buf, source, passing):
        half = passing.shape[0] // 2
        parts = ((pl.ds(0, half), 2, 0, 11), (pl.ds(half, half), -2, 10, 12))
        return [
            [
                copy(source.at[part], passing.at[part], role, along_y(way))
                for part, way, role, _ in parts
            ],
            [
                copy(passing.at[part], buf.at[PAIR[0], part], role, along_y(way))
                for part, way, _, role in parts
            ],
        ]

    k_leg = legs(k_copy, k_buf, k_hbm, k_relay)
    v_leg = legs(v_copy, v_buf, v_buf.at[OWN[0]], v_relay)
    k_own = spread(k_copy, k_buf, OWN, 1, k_hbm)
    v_own = spread(v_copy, v_buf, OWN, 1, v_buf.at[OWN[0]])
    k_other = spread(k_copy, k_buf, PAIR, 5, k_buf.at[PAIR[0]])
    v_other = spread(v_copy, v_buf, PAIR, 5, v_buf.at[PAIR[0]])
    k_edge, v_edge = edge(k_copy, k_buf), edge(v_copy, v_buf)
    q_moves = {mate: q_copy(*mate) for mate in mates}

    pl.semaphore_wait(barrier, answers)

    first_steps = (1, -1, "x")
    for move in k_leg[0]:
        move.start()
    for step in first_steps:
        k_own[step].start()
    q_moves[0, 1].start()
    v_load.wait()
    v_buf[OWN[0]] = v_rows[...].T
    for move in k_leg[0]:
        move.wait_send()
    for move in v_leg[0]:
        move.start()
    for step in first_steps:
        v_own[step].start()
    for mate in ((1, 0), (1, 1)):
        q_moves[mate].start()

    def offset(slot):
        places = {"x": jnp.where(low, 2, -2), "z": jnp.where(low, -2, 2)}
        for base, shift in ((OWN, 0), (PAIR, side)):
            for distance, index in base.items():
                if index == slot:
                    return 2 * places.get(distance, distance) + shift
        return -5 * side

    def turn_queries(ring):
        queries = [
            q_buf[2 * chunk_of(ring) + b, :, g * HEAD_DIM:(g + 1) * HEAD_DIM]
            for b in range(2)
            for g in range(GROUP)
        ]
        q_turned[ring] = jnp.concatenate(queries, axis=0).T

    def score(ring, slot):
        return jnp.dot(k_buf[slot], q_turned[ring], preferred_element_type=jnp.float32)

    def visit(units, fresh=False, finish=None):
        scores = [score(units[0][0], slot) for slot in units[0][1]]
        ones = jnp.ones((16, tokens), jnp.bfloat16)
        for at, (ring, slots) in enumerate(units):
            following = units[at + 1] if at + 1 < len(units) else (ring, ())
            renew = fresh and all(ring != earlier for earlier, _ in units[:at])
            begin, end = first[ring], last[ring]
            inside, best = [], []
            for slot, part in zip(slots, scores):
                place = jnp.asarray(offset(slot), jnp.int32).astype(jnp.float32)
                within = (begin <= place) & (place <= end)
                inside.append(within)
                best.append(jnp.where(within, jnp.max(part, axis=0, keepdims=True), -FAR))
            top = functools.reduce(jnp.maximum, best)
            if renew:
                gained = jnp.zeros(total.shape[1:], jnp.float32)
            else:
                before = peak[ring]
                top = jnp.maximum(before, top)
                gained = total[ring] * jnp.exp2((before - top) * RATE)
            ahead = []
            for i, slot in enumerate(slots):
                if i < len(following[1]):
                    ahead.append(score(following[0], following[1][i]))
                level = jnp.where(inside[i], top, FAR)
                weights = jnp.exp2((scores[i] - level) * RATE).astype(jnp.bfloat16)
                left = jnp.concatenate([v_buf[slot], ones], axis=0)
                gained = gained + jnp.dot(left, weights, preferred_element_type=jnp.float32)
            for slot in following[1][len(slots):]:
                ahead.append(score(following[0], slot))
            if finish is None:
                peak[ring] = top
                total[ring] = gained
            else:
                finish(ring, gained)
            scores = ahead

    for move, onward in zip(k_leg[0], k_leg[1]):
        move.wait_recv()
        onward.start()
    k_own["x"].wait_recv()
    k_own["z"].start()
    for move, onward in zip(v_leg[0], v_leg[1]):
        move.wait_recv()
        onward.start()
    for mate in distant[:2]:
        q_moves[mate].start()
    for move in k_leg[1]:
        move.wait_recv()
    for step in ("x", 1, -1):
        k_other[step].start()
    v_own["x"].wait_recv()
    v_own["z"].start()
    for move in v_leg[1]:
        move.wait_recv()
    for step in ("x", 1, -1):
        v_other[step].start()
    for mate in distant[2:]:
        q_moves[mate].start()
    unused = [(base[d], jnp.logical_not(has(d))) for base in (OWN, PAIR) for d in (1, -1)]
    unused += [(base["z"], jnp.where(low, at_start, at_end)) for base in (OWN, PAIR)]
    unused.append((EDGE, jnp.logical_not(jnp.where(parity == 0, has(-3), has(3)))))
    for slot, empty in unused:
        @pl.when(empty)
        def _(slot=slot):
            k_buf[slot] = jnp.zeros(k_buf.shape[1:], k_buf.dtype)
            v_buf[slot] = jnp.zeros(v_buf.shape[1:], v_buf.dtype)

    for load in span_loads:
        load.wait()
    lane = lax.broadcasted_iota(jnp.int32, (128, 256), 1)
    row = lax.broadcasted_iota(jnp.int32, (128, 256), 0)
    for ring in range(4):
        wanted = chunk_of(ring) * 32 + (lane // 128) * 16 + lane % 16
        chosen = jnp.where(row == wanted, 1.0, 0.0).astype(jnp.bfloat16)
        for ref, held in ((first_ref, first), (last_ref, last)):
            offset_row = (ref[...] - t).astype(jnp.float32)
            offset_row = jnp.broadcast_to(offset_row, (16, 128)).astype(jnp.bfloat16)
            placed = jnp.dot(offset_row, chosen, preferred_element_type=jnp.float32)
            held[ring] = placed[0:1]

    k_load.wait()
    q_load.wait()
    for step in (1, -1):
        k_own[step].wait_recv()
        v_own[step].wait_recv()
    for mate in near:
        q_moves[mate].wait_recv()
    turn_queries(0)
    turn_queries(1)
    visit([(0, (0, 1, 2, 3)), (1, (0, 1, 2, 3))], fresh=True)

    k_own["z"].wait_recv()
    v_own["z"].wait_recv()
    visit([(0, (4, 5)), (1, (4, 5))])

    k_other["x"].wait_recv()
    k_other["z"].start()
    k_other[1].wait_recv()
    k_other[-1].wait_recv()
    k_edge.start()
    for mate in distant[:2]:
        q_moves[mate].wait_recv()
    turn_queries(2)
    visit([(2, (0, 1, 2)), (2, (3, 4, 5))], fresh=True)

    v_other["x"].wait_recv()
    v_other["z"].start()
    v_other[1].wait_recv()
    v_other[-1].wait_recv()
    v_edge.start()
    visit([(ring, (6, 7, 8)) for ring in range(3)])
    for mate in distant[2:]:
        q_moves[mate].wait_recv()
    turn_queries(3)
    visit([(3, (0, 1, 2)), (3, (3, 4, 5)), (3, (6, 7, 8))], fresh=True)

    for move in (k_other["z"], v_other["z"], k_edge, v_edge):
        move.wait_recv()

    own_out = pltpu.make_async_copy(ready.at[h], out_ref.at[:, columns(h)], local_sem.at[3])

    def o_copy(ring, other):
        target = head_of(ring, other)
        index = 2 * ring + other
        return remote(
            ready.at[target], out_ref.at[:, columns(h)], o_send.at[index], o_recv.at[index],
            {"tm": t, "head": target},
        )

    o_moves = {mate: o_copy(*mate) for mate in mates}
    def send(ring, done):
        mean = done[:HEAD_DIM] / done[HEAD_DIM:HEAD_DIM + 1]
        turned = mean.T.astype(jnp.bfloat16)
        for b in range(2):
            for g in range(GROUP):
                begin = (b * GROUP + g) * rows
                ready[2 * chunk_of(ring) + b, :, g * HEAD_DIM:(g + 1) * HEAD_DIM] = turned[
                    begin:begin + rows
                ]
        for mate in mates:
            if mate[0] == ring:
                o_moves[mate].start()
        if ring == 0:
            own_out.start()

    visit([(ring, (9, 10)) for ring in (3, 2, 1, 0)], finish=send)

    for moves in (k_own, v_own, k_other, v_other):
        for move in moves.values():
            move.wait_send()
    for move in (k_edge, v_edge, *k_leg[1], *v_leg[0], *v_leg[1]):
        move.wait_send()
    for move in q_moves.values():
        move.wait_send()
    own_out.wait()
    for move in o_moves.values():
        move.wait_recv()
        move.wait_send()


def shards(groups, queries, vis_keys, vis_values, span_start, span_end):
    rows, width = queries.shape
    tokens = vis_keys.shape[0]
    part = width // KV_HEADS
    dma = pltpu.SemaphoreType.DMA
    spans = [span.reshape(1, -1) for span in (span_start, span_end)]
    operands = [queries, vis_keys, vis_values, *spans]
    flops = 4 * rows * width * tokens * SLOTS
    return pl.pallas_call(
        functools.partial(kernel, groups),
        out_shape=pltpu.VMEM((rows, width), jnp.bfloat16),
        in_specs=[pl.BlockSpec(memory_space=pltpu.HBM)] * 5,
        out_specs=pl.BlockSpec(memory_space=pl.ANY),
        scratch_shapes=[
            pltpu.VMEM(spans[0].shape, jnp.int32),
            pltpu.VMEM(spans[1].shape, jnp.int32),
            pltpu.VMEM((KV_HEADS, rows, part), jnp.bfloat16),
            pltpu.VMEM((4, HEAD_DIM, 256), jnp.bfloat16),
            pltpu.VMEM((SLOTS, tokens, HEAD_DIM), jnp.bfloat16),
            pltpu.VMEM((SLOTS, HEAD_DIM, tokens), jnp.bfloat16),
            pltpu.VMEM((tokens, HEAD_DIM), jnp.bfloat16),
            pltpu.VMEM((HEAD_DIM, tokens), jnp.bfloat16),
            pltpu.VMEM((tokens, HEAD_DIM), jnp.bfloat16),
            pltpu.VMEM((4, HEAD_DIM + 16, 256), jnp.float32),
            pltpu.VMEM((4, 1, 256), jnp.float32),
            pltpu.VMEM((4, 1, 256), jnp.float32),
            pltpu.VMEM((4, 1, 256), jnp.float32),
            pltpu.VMEM((KV_HEADS, rows, part), jnp.bfloat16),
            dma((6,)),
            dma((8,)),
            dma((8,)),
            dma((13,)),
            dma((13,)),
            dma((13,)),
            dma((13,)),
            dma((8,)),
            dma((8,)),
        ],
        cost_estimate=pl.CostEstimate(
            flops=flops, bytes_accessed=8 * rows * width, transcendentals=flops // 512
        ),
        compiler_params=pltpu.CompilerParams(
            collective_id=0, has_side_effects=True, vmem_limit_bytes=40 * 1024 * 1024
        ),
    )(*[pltpu.with_memory_space_constraint(value, pltpu.HBM) for value in operands])


def solution(mesh):
    return jax.shard_map(
        functools.partial(shards, mesh.shape["tm"]),
        mesh=mesh,
        in_specs=(P(("tm", "head"), None), P("tm", "head"), P("tm", "head"), P("tm"), P("tm")),
        out_specs=P(("tm", "head"), None),
        check_vma=False,
    )
```

```python
import functools
import math

import jax
import jax.numpy as jnp
from jax import lax
from jax.experimental import pallas as pl
from jax.experimental.pallas import tpu as pltpu
from jax.sharding import PartitionSpec as P

HEADS = 64
KV_HEADS = 8
HEAD_DIM = 128
MESH = pl.DeviceIdType.MESH
GROUP = HEADS // KV_HEADS
RATE = math.log2(math.e) / math.sqrt(HEAD_DIM)
FAR = 1e30

OWN = {0: 0, -1: 1, 1: 2, "x": 3, "z": 4}
PAIR = {0: 5, -1: 6, 1: 7, "x": 8, "z": 9}
EDGE, SLOTS = 10, 11


class Move:
    def __init__(self, copies, arrives):
        self.copies, self.arrives = copies, arrives

    def start(self):
        for sends, copy in self.copies:
            pl.when(sends)(copy.start)

    def wait_recv(self):
        pl.when(self.arrives)(self.copies[0][1].wait_recv)

    def wait_send(self):
        for sends, copy in self.copies:
            pl.when(sends)(copy.wait_send)


def kernel(
    groups, q_hbm, k_hbm, v_hbm, first_hbm, last_hbm, out_ref, first_ref, last_ref,
    q_buf, q_turned, k_buf, v_buf, k_relay, v_relay, v_rows, total, peak, first, last, ready,
    local_sem, q_send, q_recv, k_send, k_recv, v_send, v_recv, o_send, o_recv,
):
    t = lax.axis_index("tm")
    h = lax.axis_index("head")
    pair, parity = t // 2, t % 2
    side = 1 - 2 * parity
    x, z = pair % 4, pair // 4
    chip, core = h // 2, h % 2
    rows, width = q_buf.shape[1:]
    tokens = k_buf.shape[1]

    opposite_x = {"tm": 8 * z + 2 * ((x + 2) % 4) + parity, "head": h}

    def at_pair(distance):
        return {"tm": (t + groups + 2 * distance) % groups, "head": h}

    def along_y(distance):
        there = (4 * parity + chip + 8 + distance) % 8
        return {"tm": 2 * pair + there // 4, "head": 2 * (there % 4) + core}

    def flip(value):
        return value + 1 - 2 * (value % 2)

    def chunk_of(ring):
        start = chip if ring < 2 else 3 - chip
        return start if ring % 2 == 0 else flip(start)

    def columns(head):
        return pl.ds(pl.multiple_of(head * width, width), width)

    def remote(source, target, send, recv, device):
        return pltpu.make_async_remote_copy(
            source, target, send, recv, device_id=device, device_id_type=MESH
        )

    def head_of(ring, other):
        return 2 * chunk_of(ring) + (core if other == 0 else 1 - core)

    near = [(1, 0), (1, 1), (0, 1)]
    distant = [(2, 0), (2, 1), (3, 0), (3, 1)]
    mates = distant + near

    def q_copy(ring, other):
        target = head_of(ring, other)
        index = 2 * ring + other
        return remote(
            q_hbm.at[:, columns(target)], q_buf.at[h], q_send.at[index], q_recv.at[index],
            {"tm": t, "head": target},
        )

    def k_copy(source, target, role, device):
        return remote(source, target, k_send.at[role], k_recv.at[role], device)

    def v_copy(source, target, role, device):
        return remote(source, target, v_send.at[role], v_recv.at[role], device)

    k_load = pltpu.make_async_copy(k_hbm, k_buf.at[OWN[0]], local_sem.at[0])
    v_load = pltpu.make_async_copy(v_hbm, v_rows, local_sem.at[1])
    q_load = pltpu.make_async_copy(q_hbm.at[:, columns(h)], q_buf.at[h], local_sem.at[2])
    span_loads = [
        pltpu.make_async_copy(first_hbm, first_ref, local_sem.at[4]),
        pltpu.make_async_copy(last_hbm, last_ref, local_sem.at[5]),
    ]
    pairs = groups // 2
    at_start, at_end = z == 0, z == pairs // 4 - 1

    def has(distance):
        return (pair >= -distance) if distance < 0 else (pair < pairs - distance)

    barrier = pltpu.get_barrier_semaphore()
    everywhere = [along_y(2), along_y(-2), opposite_x]
    everywhere += [{"tm": t, "head": head_of(*mate)} for mate in mates]
    for partner in everywhere:
        pl.semaphore_signal(barrier, inc=1, device_id=partner, device_id_type=MESH)
    answers = len(everywhere)
    corner = jnp.where(parity == 0, pair == 0, pair == pairs - 1)
    cornered = jnp.where(parity == 0, pair == 3, pair == pairs - 4)
    others = [(has(distance), at_pair(distance)) for distance in (1, -1, 4, -4)]
    others += [(corner, at_pair(3 * side)), (cornered, at_pair(-3 * side))]
    for present, partner in others:
        answers = answers + jnp.where(present, 1, 0)

        @pl.when(present)
        def _(partner=partner):
            pl.semaphore_signal(barrier, inc=1, device_id=partner, device_id_type=MESH)

    for load in (v_load, k_load, *span_loads, q_load):
        load.start()

    low = x < 2
    to_next, to_last = jnp.logical_not(at_end), jnp.logical_not(at_start)

    def spread(copy, buf, base, role, source):
        moves = {
            e: Move(
                [(has(e), copy(source, buf.at[base[-e]], role + i, at_pair(e)))],
                has(-e),
            )
            for i, e in enumerate((1, -1))
        }
        moves["x"] = copy(source, buf.at[base["x"]], role + 2, opposite_x)
        along = copy(
            buf.at[base["x"]], buf.at[base["z"]], role + 3, at_pair(jnp.where(low, 4, -4))
        )
        moves["z"] = Move(
            [(jnp.where(low, to_next, to_last), along)], jnp.where(low, to_last, to_next)
        )
        return moves

    def edge(copy, buf):
        up = parity == 0
        beside = jnp.where(up, PAIR[1], PAIR[-1])
        along = copy(buf.at[beside], buf.at[EDGE], 9, at_pair(4 * side))
        direct = copy(buf.at[PAIR[0]], buf.at[EDGE], 9, at_pair(3 * side))
        return Move(
            [(jnp.where(up, to_next, to_last), along), (corner, direct)],
            jnp.where(up, to_last | (x == 3), to_next | (x == 0)),
        )

    def legs(copy, buf, source, passing):
        half = passing.shape[0] // 2
        parts = ((pl.ds(0, half), 2, 0, 11), (pl.ds(half, half), -2, 10, 12))
        return [
            [
                copy(source.at[part], passing.at[part], role, along_y(way))
                for part, way, role, _ in parts
            ],
            [
                copy(passing.at[part], buf.at[PAIR[0], part], role, along_y(way))
                for part, way, _, role in parts
            ],
        ]

    k_leg = legs(k_copy, k_buf, k_hbm, k_relay)
    v_leg = legs(v_copy, v_buf, v_buf.at[OWN[0]], v_relay)
    k_own = spread(k_copy, k_buf, OWN, 1, k_hbm)
    v_own = spread(v_copy, v_buf, OWN, 1, v_buf.at[OWN[0]])
    k_other = spread(k_copy, k_buf, PAIR, 5, k_buf.at[PAIR[0]])
    v_other = spread(v_copy, v_buf, PAIR, 5, v_buf.at[PAIR[0]])
    k_edge, v_edge = edge(k_copy, k_buf), edge(v_copy, v_buf)
    q_moves = {mate: q_copy(*mate) for mate in mates}

    pl.semaphore_wait(barrier, answers)

    first_steps = (1, -1, "x")
    for move in k_leg[0]:
        move.start()
    for step in first_steps:
        k_own[step].start()
    q_moves[0, 1].start()
    v_load.wait()
    v_buf[OWN[0]] = v_rows[...].T
    for move in v_leg[0]:
        move.start()
    for step in first_steps:
        v_own[step].start()
    for mate in ((1, 0), (1, 1)):
        q_moves[mate].start()

    def offset(slot):
        places = {"x": jnp.where(low, 2, -2), "z": jnp.where(low, -2, 2)}
        for base, shift in ((OWN, 0), (PAIR, side)):
            for distance, index in base.items():
                if index == slot:
                    return 2 * places.get(distance, distance) + shift
        return -5 * side

    def turn_queries(ring):
        queries = [
            q_buf[2 * chunk_of(ring) + b, :, g * HEAD_DIM:(g + 1) * HEAD_DIM]
            for b in range(2)
            for g in range(GROUP)
        ]
        q_turned[ring] = jnp.concatenate(queries, axis=0).T

    def score(ring, slot):
        return jnp.dot(k_buf[slot], q_turned[ring], preferred_element_type=jnp.float32)

    def visit(units, fresh=False, finish=None):
        scores = [score(units[0][0], slot) for slot in units[0][1]]
        ones = jnp.ones((16, tokens), jnp.bfloat16)
        for at, (ring, slots) in enumerate(units):
            following = units[at + 1] if at + 1 < len(units) else (ring, ())
            renew = fresh and all(ring != earlier for earlier, _ in units[:at])
            begin, end = first[ring], last[ring]
            inside, best = [], []
            for slot, part in zip(slots, scores):
                place = jnp.asarray(offset(slot), jnp.int32).astype(jnp.float32)
                within = (begin <= place) & (place <= end)
                inside.append(within)
                best.append(jnp.where(within, jnp.max(part, axis=0, keepdims=True), -FAR))
            top = functools.reduce(jnp.maximum, best)
            if renew:
                gained = jnp.zeros(total.shape[1:], jnp.float32)
            else:
                before = peak[ring]
                top = jnp.maximum(before, top)
                gained = total[ring] * jnp.exp2((before - top) * RATE)
            ahead = []
            for i, slot in enumerate(slots):
                if i < len(following[1]):
                    ahead.append(score(following[0], following[1][i]))
                level = jnp.where(inside[i], top, FAR)
                weights = jnp.exp2((scores[i] - level) * RATE).astype(jnp.bfloat16)
                left = jnp.concatenate([v_buf[slot], ones], axis=0)
                gained = gained + jnp.dot(left, weights, preferred_element_type=jnp.float32)
            for slot in following[1][len(slots):]:
                ahead.append(score(following[0], slot))
            if finish is None:
                peak[ring] = top
                total[ring] = gained
            else:
                finish(ring, gained)
            scores = ahead

    for move, onward in zip(k_leg[0], k_leg[1]):
        move.wait_recv()
        onward.start()
    k_own["x"].wait_recv()
    k_own["z"].start()
    for move, onward in zip(v_leg[0], v_leg[1]):
        move.wait_recv()
        onward.start()
    for mate in distant[:2]:
        q_moves[mate].start()
    for move in k_leg[1]:
        move.wait_recv()
    for step in ("x", 1, -1):
        k_other[step].start()
    v_own["x"].wait_recv()
    v_own["z"].start()
    for move in v_leg[1]:
        move.wait_recv()
    for step in ("x", 1, -1):
        v_other[step].start()
    for mate in distant[2:]:
        q_moves[mate].start()
    unused = [(base[d], jnp.logical_not(has(d))) for base in (OWN, PAIR) for d in (1, -1)]
    unused += [(base["z"], jnp.where(low, at_start, at_end)) for base in (OWN, PAIR)]
    unused.append((EDGE, jnp.logical_not(jnp.where(parity == 0, has(-3), has(3)))))
    for slot, empty in unused:
        @pl.when(empty)
        def _(slot=slot):
            k_buf[slot] = jnp.zeros(k_buf.shape[1:], k_buf.dtype)
            v_buf[slot] = jnp.zeros(v_buf.shape[1:], v_buf.dtype)

    for load in span_loads:
        load.wait()
    lane = lax.broadcasted_iota(jnp.int32, (128, 256), 1)
    row = lax.broadcasted_iota(jnp.int32, (128, 256), 0)
    for ring in range(4):
        wanted = chunk_of(ring) * 32 + (lane // 128) * 16 + lane % 16
        chosen = jnp.where(row == wanted, 1.0, 0.0).astype(jnp.bfloat16)
        for ref, held in ((first_ref, first), (last_ref, last)):
            offset_row = (ref[...] - t).astype(jnp.float32)
            offset_row = jnp.broadcast_to(offset_row, (16, 128)).astype(jnp.bfloat16)
            placed = jnp.dot(offset_row, chosen, preferred_element_type=jnp.float32)
            held[ring] = placed[0:1]

    k_load.wait()
    q_load.wait()
    for step in (1, -1):
        k_own[step].wait_recv()
        v_own[step].wait_recv()
    for mate in near:
        q_moves[mate].wait_recv()
    turn_queries(0)
    turn_queries(1)
    visit([(0, (0, 1, 2, 3)), (1, (0, 1, 2, 3))], fresh=True)

    k_own["z"].wait_recv()
    v_own["z"].wait_recv()
    visit([(0, (4, 5)), (1, (4, 5))])

    k_other["x"].wait_recv()
    k_other["z"].start()
    k_other[1].wait_recv()
    k_other[-1].wait_recv()
    k_edge.start()
    for mate in distant[:2]:
        q_moves[mate].wait_recv()
    turn_queries(2)
    visit([(2, (0, 1, 2)), (2, (3, 4, 5))], fresh=True)

    v_other["x"].wait_recv()
    v_other["z"].start()
    v_other[1].wait_recv()
    v_other[-1].wait_recv()
    v_edge.start()
    visit([(ring, (6, 7, 8)) for ring in range(3)])
    for mate in distant[2:]:
        q_moves[mate].wait_recv()
    turn_queries(3)
    visit([(3, (0, 1, 2)), (3, (3, 4, 5)), (3, (6, 7, 8))], fresh=True)

    for move in (k_other["z"], v_other["z"], k_edge, v_edge):
        move.wait_recv()

    own_out = pltpu.make_async_copy(ready.at[h], out_ref.at[:, columns(h)], local_sem.at[3])

    def o_copy(ring, other):
        target = head_of(ring, other)
        index = 2 * ring + other
        return remote(
            ready.at[target], out_ref.at[:, columns(h)], o_send.at[index], o_recv.at[index],
            {"tm": t, "head": target},
        )

    o_moves = {mate: o_copy(*mate) for mate in mates}
    def send(ring, done):
        mean = done[:HEAD_DIM] / done[HEAD_DIM:HEAD_DIM + 1]
        turned = mean.T.astype(jnp.bfloat16)
        for b in range(2):
            for g in range(GROUP):
                begin = (b * GROUP + g) * rows
                ready[2 * chunk_of(ring) + b, :, g * HEAD_DIM:(g + 1) * HEAD_DIM] = turned[
                    begin:begin + rows
                ]
        for mate in mates:
            if mate[0] == ring:
                o_moves[mate].start()
        if ring == 0:
            own_out.start()

    visit([(ring, (9, 10)) for ring in (2, 3, 1, 0)], finish=send)

    for moves in (k_own, v_own, k_other, v_other):
        for move in moves.values():
            move.wait_send()
    for move in (k_edge, v_edge, *k_leg[0], *k_leg[1], *v_leg[0], *v_leg[1]):
        move.wait_send()
    for move in q_moves.values():
        move.wait_send()
    own_out.wait()
    for move in o_moves.values():
        move.wait_recv()
        move.wait_send()


def shards(groups, queries, vis_keys, vis_values, span_start, span_end):
    rows, width = queries.shape
    tokens = vis_keys.shape[0]
    part = width // KV_HEADS
    dma = pltpu.SemaphoreType.DMA
    spans = [span.reshape(1, -1) for span in (span_start, span_end)]
    operands = [queries, vis_keys, vis_values, *spans]
    flops = 4 * rows * width * tokens * SLOTS
    return pl.pallas_call(
        functools.partial(kernel, groups),
        out_shape=pltpu.VMEM((rows, width), jnp.bfloat16),
        in_specs=[pl.BlockSpec(memory_space=pltpu.HBM)] * 5,
        out_specs=pl.BlockSpec(memory_space=pl.ANY),
        scratch_shapes=[
            pltpu.VMEM(spans[0].shape, jnp.int32),
            pltpu.VMEM(spans[1].shape, jnp.int32),
            pltpu.VMEM((KV_HEADS, rows, part), jnp.bfloat16),
            pltpu.VMEM((4, HEAD_DIM, 256), jnp.bfloat16),
            pltpu.VMEM((SLOTS, tokens, HEAD_DIM), jnp.bfloat16),
            pltpu.VMEM((SLOTS, HEAD_DIM, tokens), jnp.bfloat16),
            pltpu.VMEM((tokens, HEAD_DIM), jnp.bfloat16),
            pltpu.VMEM((HEAD_DIM, tokens), jnp.bfloat16),
            pltpu.VMEM((tokens, HEAD_DIM), jnp.bfloat16),
            pltpu.VMEM((4, HEAD_DIM + 16, 256), jnp.float32),
            pltpu.VMEM((4, 1, 256), jnp.float32),
            pltpu.VMEM((4, 1, 256), jnp.float32),
            pltpu.VMEM((4, 1, 256), jnp.float32),
            pltpu.VMEM((KV_HEADS, rows, part), jnp.bfloat16),
            dma((6,)),
            dma((8,)),
            dma((8,)),
            dma((13,)),
            dma((13,)),
            dma((13,)),
            dma((13,)),
            dma((8,)),
            dma((8,)),
        ],
        cost_estimate=pl.CostEstimate(
            flops=flops, bytes_accessed=8 * rows * width, transcendentals=flops // 512
        ),
        compiler_params=pltpu.CompilerParams(
            collective_id=0, has_side_effects=True, vmem_limit_bytes=40 * 1024 * 1024
        ),
    )(*[pltpu.with_memory_space_constraint(value, pltpu.HBM) for value in operands])


def solution(mesh):
    return jax.shard_map(
        functools.partial(shards, mesh.shape["tm"]),
        mesh=mesh,
        in_specs=(P(("tm", "head"), None), P("tm", "head"), P("tm", "head"), P("tm"), P("tm")),
        out_specs=P(("tm", "head"), None),
        check_vma=False,
    )
```

```python
import functools
import math

import jax
import jax.numpy as jnp
from jax import lax
from jax.experimental import pallas as pl
from jax.experimental.pallas import tpu as pltpu
from jax.sharding import PartitionSpec as P

HEADS = 64
KV_HEADS = 8
HEAD_DIM = 128
MESH = pl.DeviceIdType.MESH
GROUP = HEADS // KV_HEADS
RATE = math.log2(math.e) / math.sqrt(HEAD_DIM)
FAR = 1e30

OWN = {0: 0, -1: 1, 1: 2, "x": 3, "z": 4}
PAIR = {0: 5, -1: 6, 1: 7, "x": 8, "z": 9}
EDGE, SLOTS = 10, 11


class Move:
    def __init__(self, copies, arrives):
        self.copies, self.arrives = copies, arrives

    def start(self):
        for sends, copy in self.copies:
            pl.when(sends)(copy.start)

    def wait_recv(self):
        pl.when(self.arrives)(self.copies[0][1].wait_recv)

    def wait_send(self):
        for sends, copy in self.copies:
            pl.when(sends)(copy.wait_send)


def kernel(
    groups, q_hbm, k_hbm, v_hbm, first_hbm, last_hbm, out_ref, first_ref, last_ref,
    q_buf, q_turned, k_buf, v_buf, v_rows, total, peak, first, last, ready,
    local_sem, q_send, q_recv, k_send, k_recv, v_send, v_recv, o_send, o_recv,
):
    t = lax.axis_index("tm")
    h = lax.axis_index("head")
    pair, parity = t // 2, t % 2
    side = 1 - 2 * parity
    x, z = pair % 4, pair // 4
    chip, core = h // 2, h % 2
    rows, width = q_buf.shape[1:]
    tokens = k_buf.shape[1]

    opposite_x = {"tm": 8 * z + 2 * ((x + 2) % 4) + parity, "head": h}

    def at_pair(distance):
        return {"tm": (t + groups + 2 * distance) % groups, "head": h}

    def flip(value):
        return value + 1 - 2 * (value % 2)

    def chunk_of(ring):
        start = chip if ring < 2 else (chip + 2) % 4
        return start if ring % 2 == 0 else flip(start)

    def columns(head):
        return pl.ds(pl.multiple_of(head * width, width), width)

    def remote(source, target, send, recv, device):
        return pltpu.make_async_remote_copy(
            source, target, send, recv, device_id=device, device_id_type=MESH
        )

    def head_of(ring, other):
        return 2 * chunk_of(ring) + (core if other == 0 else 1 - core)

    near = [(1, 0), (1, 1), (0, 1)]
    distant = [(2, 0), (2, 1), (3, 0), (3, 1)]
    mates = distant + near

    def q_copy(ring, other):
        target = head_of(ring, other)
        index = 2 * ring + other
        return remote(
            q_hbm.at[:, columns(target)], q_buf.at[h], q_send.at[index], q_recv.at[index],
            {"tm": t, "head": target},
        )

    def k_copy(source, target, role, device):
        return remote(source, target, k_send.at[role], k_recv.at[role], device)

    def v_copy(source, target, role, device):
        return remote(source, target, v_send.at[role], v_recv.at[role], device)

    k_load = pltpu.make_async_copy(k_hbm, k_buf.at[OWN[0]], local_sem.at[0])
    v_load = pltpu.make_async_copy(v_hbm, v_rows, local_sem.at[1])
    q_load = pltpu.make_async_copy(q_hbm.at[:, columns(h)], q_buf.at[h], local_sem.at[2])
    span_loads = [
        pltpu.make_async_copy(first_hbm, first_ref, local_sem.at[4]),
        pltpu.make_async_copy(last_hbm, last_ref, local_sem.at[5]),
    ]
    pairs = groups // 2
    at_start, at_end = z == 0, z == pairs // 4 - 1

    def has(distance):
        return (pair >= -distance) if distance < 0 else (pair < pairs - distance)

    barrier = pltpu.get_barrier_semaphore()
    everywhere = [{"tm": t + side, "head": h}, opposite_x]
    everywhere += [{"tm": t, "head": head_of(*mate)} for mate in mates]
    for partner in everywhere:
        pl.semaphore_signal(barrier, inc=1, device_id=partner, device_id_type=MESH)
    answers = len(everywhere)
    corner = jnp.where(parity == 0, pair == 0, pair == pairs - 1)
    cornered = jnp.where(parity == 0, pair == 3, pair == pairs - 4)
    others = [(has(distance), at_pair(distance)) for distance in (1, -1, 4, -4)]
    others += [(corner, at_pair(3 * side)), (cornered, at_pair(-3 * side))]
    for present, partner in others:
        answers = answers + jnp.where(present, 1, 0)

        @pl.when(present)
        def _(partner=partner):
            pl.semaphore_signal(barrier, inc=1, device_id=partner, device_id_type=MESH)

    for load in (v_load, k_load, *span_loads, q_load):
        load.start()

    low = x < 2
    to_next, to_last = jnp.logical_not(at_end), jnp.logical_not(at_start)

    def spread(copy, buf, base, role, source):
        moves = {
            e: Move(
                [(has(e), copy(source, buf.at[base[-e]], role + i, at_pair(e)))],
                has(-e),
            )
            for i, e in enumerate((1, -1))
        }
        moves["x"] = copy(source, buf.at[base["x"]], role + 2, opposite_x)
        along = copy(
            buf.at[base["x"]], buf.at[base["z"]], role + 3, at_pair(jnp.where(low, 4, -4))
        )
        moves["z"] = Move(
            [(jnp.where(low, to_next, to_last), along)], jnp.where(low, to_last, to_next)
        )
        return moves

    def edge(copy, buf):
        up = parity == 0
        beside = jnp.where(up, PAIR[1], PAIR[-1])
        along = copy(buf.at[beside], buf.at[EDGE], 9, at_pair(4 * side))
        direct = copy(buf.at[PAIR[0]], buf.at[EDGE], 9, at_pair(3 * side))
        return Move(
            [(jnp.where(up, to_next, to_last), along), (corner, direct)],
            jnp.where(up, to_last | (x == 3), to_next | (x == 0)),
        )

    partner = {"tm": t + side, "head": h}
    k_pair = k_copy(k_hbm, k_buf.at[PAIR[0]], 0, partner)
    v_pair = v_copy(v_buf.at[OWN[0]], v_buf.at[PAIR[0]], 0, partner)
    k_own = spread(k_copy, k_buf, OWN, 1, k_hbm)
    v_own = spread(v_copy, v_buf, OWN, 1, v_buf.at[OWN[0]])
    k_other = spread(k_copy, k_buf, PAIR, 5, k_buf.at[PAIR[0]])
    v_other = spread(v_copy, v_buf, PAIR, 5, v_buf.at[PAIR[0]])
    k_edge, v_edge = edge(k_copy, k_buf), edge(v_copy, v_buf)
    q_moves = {mate: q_copy(*mate) for mate in mates}

    pl.semaphore_wait(barrier, answers)

    first_steps = (1, -1, "x")
    k_pair.start()
    for step in first_steps:
        k_own[step].start()
    q_moves[0, 1].start()
    v_load.wait()
    v_buf[OWN[0]] = v_rows[...].T
    v_pair.start()
    for step in first_steps:
        v_own[step].start()
    for mate in ((1, 0), (1, 1)):
        q_moves[mate].start()

    def offset(slot):
        places = {"x": jnp.where(low, 2, -2), "z": jnp.where(low, -2, 2)}
        for base, shift in ((OWN, 0), (PAIR, side)):
            for distance, index in base.items():
                if index == slot:
                    return 2 * places.get(distance, distance) + shift
        return -5 * side

    def turn_queries(ring):
        queries = [
            q_buf[2 * chunk_of(ring) + b, :, g * HEAD_DIM:(g + 1) * HEAD_DIM]
            for b in range(2)
            for g in range(GROUP)
        ]
        q_turned[ring] = jnp.concatenate(queries, axis=0).T

    def score(ring, slot):
        return jnp.dot(k_buf[slot], q_turned[ring], preferred_element_type=jnp.float32)

    def visit(units, fresh=False, finish=None):
        scores = [score(units[0][0], slot) for slot in units[0][1]]
        ones = jnp.ones((16, tokens), jnp.bfloat16)
        for at, (ring, slots) in enumerate(units):
            following = units[at + 1] if at + 1 < len(units) else (ring, ())
            renew = fresh and all(ring != earlier for earlier, _ in units[:at])
            begin, end = first[ring], last[ring]
            inside, best = [], []
            for slot, part in zip(slots, scores):
                place = jnp.asarray(offset(slot), jnp.int32).astype(jnp.float32)
                within = (begin <= place) & (place <= end)
                inside.append(within)
                best.append(jnp.where(within, jnp.max(part, axis=0, keepdims=True), -FAR))
            top = functools.reduce(jnp.maximum, best)
            if renew:
                gained = jnp.zeros(total.shape[1:], jnp.float32)
            else:
                before = peak[ring]
                top = jnp.maximum(before, top)
                gained = total[ring] * jnp.exp2((before - top) * RATE)
            ahead = []
            for i, slot in enumerate(slots):
                if i < len(following[1]):
                    ahead.append(score(following[0], following[1][i]))
                level = jnp.where(inside[i], top, FAR)
                weights = jnp.exp2((scores[i] - level) * RATE).astype(jnp.bfloat16)
                left = jnp.concatenate([v_buf[slot], ones], axis=0)
                gained = gained + jnp.dot(left, weights, preferred_element_type=jnp.float32)
            for slot in following[1][len(slots):]:
                ahead.append(score(following[0], slot))
            if finish is None:
                peak[ring] = top
                total[ring] = gained
            else:
                finish(ring, gained)
            scores = ahead

    k_own["x"].wait_recv()
    k_own["z"].start()
    k_pair.wait_recv()
    for step in ("x", 1, -1):
        k_other[step].start()
    for mate in distant[:2]:
        q_moves[mate].start()
    v_own["x"].wait_recv()
    v_own["z"].start()
    v_pair.wait_recv()
    for step in ("x", 1, -1):
        v_other[step].start()
    for mate in distant[2:]:
        q_moves[mate].start()
    unused = [(base[d], jnp.logical_not(has(d))) for base in (OWN, PAIR) for d in (1, -1)]
    unused += [(base["z"], jnp.where(low, at_start, at_end)) for base in (OWN, PAIR)]
    unused.append((EDGE, jnp.logical_not(jnp.where(parity == 0, has(-3), has(3)))))
    for slot, empty in unused:
        @pl.when(empty)
        def _(slot=slot):
            k_buf[slot] = jnp.zeros(k_buf.shape[1:], k_buf.dtype)
            v_buf[slot] = jnp.zeros(v_buf.shape[1:], v_buf.dtype)

    for load in span_loads:
        load.wait()
    lane = lax.broadcasted_iota(jnp.int32, (128, 256), 1)
    row = lax.broadcasted_iota(jnp.int32, (128, 256), 0)
    for ring in range(4):
        wanted = chunk_of(ring) * 32 + (lane // 128) * 16 + lane % 16
        chosen = jnp.where(row == wanted, 1.0, 0.0).astype(jnp.bfloat16)
        for ref, held in ((first_ref, first), (last_ref, last)):
            offset_row = (ref[...] - t).astype(jnp.float32)
            offset_row = jnp.broadcast_to(offset_row, (16, 128)).astype(jnp.bfloat16)
            placed = jnp.dot(offset_row, chosen, preferred_element_type=jnp.float32)
            held[ring] = placed[0:1]

    k_load.wait()
    q_load.wait()
    for step in (1, -1):
        k_own[step].wait_recv()
        v_own[step].wait_recv()
    for mate in near:
        q_moves[mate].wait_recv()
    turn_queries(0)
    turn_queries(1)
    visit([(0, (0, 1, 2, 3)), (1, (0, 1, 2, 3))], fresh=True)

    k_own["z"].wait_recv()
    v_own["z"].wait_recv()
    visit([(0, (4, 5)), (1, (4, 5))])

    k_other["x"].wait_recv()
    k_other["z"].start()
    k_other[1].wait_recv()
    k_other[-1].wait_recv()
    k_edge.start()
    for mate in distant[:2]:
        q_moves[mate].wait_recv()
    turn_queries(2)
    visit([(2, (0, 1, 2)), (2, (3, 4, 5))], fresh=True)

    v_other["x"].wait_recv()
    v_other["z"].start()
    v_other[1].wait_recv()
    v_other[-1].wait_recv()
    v_edge.start()
    visit([(ring, (6, 7, 8)) for ring in range(3)])
    for mate in distant[2:]:
        q_moves[mate].wait_recv()
    turn_queries(3)
    visit([(3, (0, 1, 2)), (3, (3, 4, 5)), (3, (6, 7, 8))], fresh=True)

    for move in (k_other["z"], v_other["z"], k_edge, v_edge):
        move.wait_recv()

    own_out = pltpu.make_async_copy(ready.at[h], out_ref.at[:, columns(h)], local_sem.at[3])

    def o_copy(ring, other):
        target = head_of(ring, other)
        index = 2 * ring + other
        return remote(
            ready.at[target], out_ref.at[:, columns(h)], o_send.at[index], o_recv.at[index],
            {"tm": t, "head": target},
        )

    o_moves = {mate: o_copy(*mate) for mate in mates}
    def send(ring, done):
        mean = done[:HEAD_DIM] / done[HEAD_DIM:HEAD_DIM + 1]
        turned = mean.T.astype(jnp.bfloat16)
        for b in range(2):
            for g in range(GROUP):
                begin = (b * GROUP + g) * rows
                ready[2 * chunk_of(ring) + b, :, g * HEAD_DIM:(g + 1) * HEAD_DIM] = turned[
                    begin:begin + rows
                ]
        for mate in mates:
            if mate[0] == ring:
                o_moves[mate].start()
        if ring == 0:
            own_out.start()

    visit([(ring, (9, 10)) for ring in (3, 2, 1, 0)], finish=send)

    for moves in (k_own, v_own, k_other, v_other):
        for move in moves.values():
            move.wait_send()
    for move in (k_edge, v_edge, k_pair, v_pair):
        move.wait_send()
    for move in q_moves.values():
        move.wait_send()
    own_out.wait()
    for move in o_moves.values():
        move.wait_recv()
        move.wait_send()


def shards(groups, queries, vis_keys, vis_values, span_start, span_end):
    rows, width = queries.shape
    tokens = vis_keys.shape[0]
    part = width // KV_HEADS
    dma = pltpu.SemaphoreType.DMA
    spans = [span.reshape(1, -1) for span in (span_start, span_end)]
    operands = [queries, vis_keys, vis_values, *spans]
    flops = 4 * rows * width * tokens * SLOTS
    return pl.pallas_call(
        functools.partial(kernel, groups),
        out_shape=pltpu.VMEM((rows, width), jnp.bfloat16),
        in_specs=[pl.BlockSpec(memory_space=pltpu.HBM)] * 5,
        out_specs=pl.BlockSpec(memory_space=pl.ANY),
        scratch_shapes=[
            pltpu.VMEM(spans[0].shape, jnp.int32),
            pltpu.VMEM(spans[1].shape, jnp.int32),
            pltpu.VMEM((KV_HEADS, rows, part), jnp.bfloat16),
            pltpu.VMEM((4, HEAD_DIM, 256), jnp.bfloat16),
            pltpu.VMEM((SLOTS, tokens, HEAD_DIM), jnp.bfloat16),
            pltpu.VMEM((SLOTS, HEAD_DIM, tokens), jnp.bfloat16),
            pltpu.VMEM((tokens, HEAD_DIM), jnp.bfloat16),
            pltpu.VMEM((4, HEAD_DIM + 16, 256), jnp.float32),
            pltpu.VMEM((4, 1, 256), jnp.float32),
            pltpu.VMEM((4, 1, 256), jnp.float32),
            pltpu.VMEM((4, 1, 256), jnp.float32),
            pltpu.VMEM((KV_HEADS, rows, part), jnp.bfloat16),
            dma((6,)),
            dma((8,)),
            dma((8,)),
            dma((10,)),
            dma((10,)),
            dma((10,)),
            dma((10,)),
            dma((8,)),
            dma((8,)),
        ],
        cost_estimate=pl.CostEstimate(
            flops=flops, bytes_accessed=8 * rows * width, transcendentals=flops // 512
        ),
        compiler_params=pltpu.CompilerParams(
            collective_id=0, has_side_effects=True, vmem_limit_bytes=40 * 1024 * 1024
        ),
    )(*[pltpu.with_memory_space_constraint(value, pltpu.HBM) for value in operands])


def solution(mesh):
    return jax.shard_map(
        functools.partial(shards, mesh.shape["tm"]),
        mesh=mesh,
        in_specs=(P(("tm", "head"), None), P("tm", "head"), P("tm", "head"), P("tm"), P("tm")),
        out_specs=P(("tm", "head"), None),
        check_vma=False,
    )
```

```python
import functools
import math

import jax
import jax.numpy as jnp
from jax import lax
from jax.experimental import pallas as pl
from jax.experimental.pallas import tpu as pltpu
from jax.sharding import PartitionSpec as P

HEADS = 64
KV_HEADS = 8
HEAD_DIM = 128
MESH = pl.DeviceIdType.MESH
GROUP = HEADS // KV_HEADS
RATE = math.log2(math.e) / math.sqrt(HEAD_DIM)
FAR = 1e30

OWN = {0: 0, -1: 1, 1: 2, "x": 3, "z": 4}
PAIR = {0: 5, -1: 6, 1: 7, "x": 8, "z": 9}
EDGE, SLOTS = 10, 11


class Move:
    def __init__(self, copies, arrives):
        self.copies, self.arrives = copies, arrives

    def start(self):
        for sends, copy in self.copies:
            pl.when(sends)(copy.start)

    def wait_recv(self):
        pl.when(self.arrives)(self.copies[0][1].wait_recv)

    def wait_send(self):
        for sends, copy in self.copies:
            pl.when(sends)(copy.wait_send)


def kernel(
    groups, q_hbm, k_hbm, v_hbm, first_hbm, last_hbm, out_ref, first_ref, last_ref,
    q_buf, q_turned, k_buf, v_buf, v_rows, total, peak, first, last, ready,
    local_sem, q_send, q_recv, k_send, k_recv, v_send, v_recv, o_send, o_recv,
):
    t = lax.axis_index("tm")
    h = lax.axis_index("head")
    pair, parity = t // 2, t % 2
    side = 1 - 2 * parity
    x, z = pair % 4, pair // 4
    chip, core = h // 2, h % 2
    rows, width = q_buf.shape[1:]
    tokens = k_buf.shape[1]

    opposite_x = {"tm": 8 * z + 2 * ((x + 2) % 4) + parity, "head": h}

    def at_pair(distance):
        return {"tm": (t + groups + 2 * distance) % groups, "head": h}

    def flip(value):
        return value + 1 - 2 * (value % 2)

    def chunk_of(ring):
        start = chip if ring < 2 else (chip + 2) % 4
        return start if ring % 2 == 0 else flip(start)

    def columns(head):
        return pl.ds(pl.multiple_of(head * width, width), width)

    def remote(source, target, send, recv, device):
        return pltpu.make_async_remote_copy(
            source, target, send, recv, device_id=device, device_id_type=MESH
        )

    def head_of(ring, other):
        return 2 * chunk_of(ring) + (core if other == 0 else 1 - core)

    near = [(1, 0), (1, 1), (0, 1)]
    distant = [(2, 0), (2, 1), (3, 0), (3, 1)]
    mates = distant + near

    def q_copy(ring, other):
        target = head_of(ring, other)
        index = 2 * ring + other
        return remote(
            q_hbm.at[:, columns(target)], q_buf.at[h], q_send.at[index], q_recv.at[index],
            {"tm": t, "head": target},
        )

    def k_copy(source, target, role, device):
        return remote(source, target, k_send.at[role], k_recv.at[role], device)

    def v_copy(source, target, role, device):
        return remote(source, target, v_send.at[role], v_recv.at[role], device)

    k_load = pltpu.make_async_copy(k_hbm, k_buf.at[OWN[0]], local_sem.at[0])
    v_load = pltpu.make_async_copy(v_hbm, v_rows, local_sem.at[1])
    q_load = pltpu.make_async_copy(q_hbm.at[:, columns(h)], q_buf.at[h], local_sem.at[2])
    span_loads = [
        pltpu.make_async_copy(first_hbm, first_ref, local_sem.at[4]),
        pltpu.make_async_copy(last_hbm, last_ref, local_sem.at[5]),
    ]
    pairs = groups // 2
    at_start, at_end = z == 0, z == pairs // 4 - 1

    def has(distance):
        return (pair >= -distance) if distance < 0 else (pair < pairs - distance)

    barrier = pltpu.get_barrier_semaphore()
    everywhere = [{"tm": t + side, "head": h}, opposite_x]
    everywhere += [{"tm": t, "head": head_of(*mate)} for mate in mates]
    for partner in everywhere:
        pl.semaphore_signal(barrier, inc=1, device_id=partner, device_id_type=MESH)
    answers = len(everywhere)
    corner = jnp.where(parity == 0, pair == 0, pair == pairs - 1)
    low = x < 2
    to_next, to_last = jnp.logical_not(at_end), jnp.logical_not(at_start)
    beyond = jnp.where(low, to_last, to_next), at_pair(jnp.where(low, -2, 2))
    ahead = jnp.where(parity == 0, has(3), has(-3)), at_pair(3 * side)
    behind = jnp.where(parity == 0, has(-3), has(3)), at_pair(-3 * side)
    others = [(has(distance), at_pair(distance)) for distance in (1, -1, 4, -4)]
    others += [beyond, ahead, behind]
    for present, partner in others:
        answers = answers + jnp.where(present, 1, 0)

        @pl.when(present)
        def _(partner=partner):
            pl.semaphore_signal(barrier, inc=1, device_id=partner, device_id_type=MESH)

    for load in (v_load, k_load, *span_loads, q_load):
        load.start()


    def spread(copy, buf, base, role, source):
        moves = {
            e: Move(
                [(has(e), copy(source, buf.at[base[-e]], role + i, at_pair(e)))],
                has(-e),
            )
            for i, e in enumerate((1, -1))
        }
        moves["x"] = copy(source, buf.at[base["x"]], role + 2, opposite_x)
        along = copy(
            buf.at[base["x"]], buf.at[base["z"]], role + 3, at_pair(jnp.where(low, 4, -4))
        )
        moves["z"] = Move(
            [(jnp.where(low, to_next, to_last), along)], jnp.where(low, to_last, to_next)
        )
        return moves

    def edge(copy, buf):
        up = parity == 0
        beside = jnp.where(up, PAIR[1], PAIR[-1])
        along = copy(buf.at[beside], buf.at[EDGE], 9, at_pair(4 * side))
        direct = copy(buf.at[PAIR[0]], buf.at[EDGE], 9, at_pair(3 * side))
        return Move(
            [(jnp.where(up, to_next, to_last), along), (corner, direct)],
            jnp.where(up, to_last | (x == 3), to_next | (x == 0)),
        )

    partner = {"tm": t + side, "head": h}
    k_pair = k_copy(k_hbm, k_buf.at[PAIR[0]], 0, partner)
    v_pair = v_copy(v_buf.at[OWN[0]], v_buf.at[PAIR[0]], 0, partner)
    k_own = spread(k_copy, k_buf, OWN, 1, k_hbm)
    v_own = spread(v_copy, v_buf, OWN, 1, v_buf.at[OWN[0]])
    k_other = spread(k_copy, k_buf, PAIR, 5, k_buf.at[PAIR[0]])
    v_other = spread(v_copy, v_buf, PAIR, 5, v_buf.at[PAIR[0]])
    k_edge = edge(k_copy, k_buf)
    v_other["z"] = Move(
        [(beyond[0], v_copy(v_buf.at[PAIR[0]], v_buf.at[PAIR["z"]], 8, beyond[1]))],
        v_other["z"].arrives,
    )
    v_edge = Move(
        [(ahead[0], v_copy(v_buf.at[PAIR[0]], v_buf.at[EDGE], 9, ahead[1]))], behind[0]
    )
    q_moves = {mate: q_copy(*mate) for mate in mates}

    pl.semaphore_wait(barrier, answers)

    first_steps = (1, -1, "x")
    k_pair.start()
    for step in first_steps:
        k_own[step].start()
    q_moves[0, 1].start()
    v_load.wait()
    v_buf[OWN[0]] = v_rows[...].T
    v_pair.start()
    for step in first_steps:
        v_own[step].start()
    for mate in ((1, 0), (1, 1)):
        q_moves[mate].start()

    def offset(slot):
        places = {"x": jnp.where(low, 2, -2), "z": jnp.where(low, -2, 2)}
        for base, shift in ((OWN, 0), (PAIR, side)):
            for distance, index in base.items():
                if index == slot:
                    return 2 * places.get(distance, distance) + shift
        return -5 * side

    def turn_queries(ring):
        queries = [
            q_buf[2 * chunk_of(ring) + b, :, g * HEAD_DIM:(g + 1) * HEAD_DIM]
            for b in range(2)
            for g in range(GROUP)
        ]
        q_turned[ring] = jnp.concatenate(queries, axis=0).T

    def score(ring, slot):
        return jnp.dot(k_buf[slot], q_turned[ring], preferred_element_type=jnp.float32)

    def visit(units, fresh=False, finish=None):
        scores = [score(units[0][0], slot) for slot in units[0][1]]
        ones = jnp.ones((16, tokens), jnp.bfloat16)
        for at, (ring, slots) in enumerate(units):
            following = units[at + 1] if at + 1 < len(units) else (ring, ())
            renew = fresh and all(ring != earlier for earlier, _ in units[:at])
            begin, end = first[ring], last[ring]
            inside, best = [], []
            for slot, part in zip(slots, scores):
                place = jnp.asarray(offset(slot), jnp.int32).astype(jnp.float32)
                within = (begin <= place) & (place <= end)
                inside.append(within)
                best.append(jnp.where(within, jnp.max(part, axis=0, keepdims=True), -FAR))
            top = functools.reduce(jnp.maximum, best)
            if renew:
                gained = jnp.zeros(total.shape[1:], jnp.float32)
            else:
                before = peak[ring]
                top = jnp.maximum(before, top)
                gained = total[ring] * jnp.exp2((before - top) * RATE)
            ahead = []
            for i, slot in enumerate(slots):
                if i < len(following[1]):
                    ahead.append(score(following[0], following[1][i]))
                level = jnp.where(inside[i], top, FAR)
                weights = jnp.exp2((scores[i] - level) * RATE).astype(jnp.bfloat16)
                left = jnp.concatenate([v_buf[slot], ones], axis=0)
                gained = gained + jnp.dot(left, weights, preferred_element_type=jnp.float32)
            for slot in following[1][len(slots):]:
                ahead.append(score(following[0], slot))
            if finish is None:
                peak[ring] = top
                total[ring] = gained
            else:
                finish(ring, gained)
            scores = ahead

    k_own["x"].wait_recv()
    k_own["z"].start()
    k_pair.wait_recv()
    for step in ("x", 1, -1):
        k_other[step].start()
    for mate in distant[:2]:
        q_moves[mate].start()
    v_own["x"].wait_recv()
    v_own["z"].start()
    v_pair.wait_recv()
    for step in ("x", "z", 1, -1):
        v_other[step].start()
    v_edge.start()
    for mate in distant[2:]:
        q_moves[mate].start()
    unused = [(base[d], jnp.logical_not(has(d))) for base in (OWN, PAIR) for d in (1, -1)]
    unused += [(base["z"], jnp.where(low, at_start, at_end)) for base in (OWN, PAIR)]
    unused.append((EDGE, jnp.logical_not(jnp.where(parity == 0, has(-3), has(3)))))
    for slot, empty in unused:
        @pl.when(empty)
        def _(slot=slot):
            k_buf[slot] = jnp.zeros(k_buf.shape[1:], k_buf.dtype)
            v_buf[slot] = jnp.zeros(v_buf.shape[1:], v_buf.dtype)

    for load in span_loads:
        load.wait()
    lane = lax.broadcasted_iota(jnp.int32, (128, 256), 1)
    row = lax.broadcasted_iota(jnp.int32, (128, 256), 0)
    for ring in range(4):
        wanted = chunk_of(ring) * 32 + (lane // 128) * 16 + lane % 16
        chosen = jnp.where(row == wanted, 1.0, 0.0).astype(jnp.bfloat16)
        for ref, held in ((first_ref, first), (last_ref, last)):
            offset_row = (ref[...] - t).astype(jnp.float32)
            offset_row = jnp.broadcast_to(offset_row, (16, 128)).astype(jnp.bfloat16)
            placed = jnp.dot(offset_row, chosen, preferred_element_type=jnp.float32)
            held[ring] = placed[0:1]

    k_load.wait()
    q_load.wait()
    for step in (1, -1):
        k_own[step].wait_recv()
        v_own[step].wait_recv()
    for mate in near:
        q_moves[mate].wait_recv()
    turn_queries(0)
    turn_queries(1)
    visit([(0, (0, 1, 2, 3)), (1, (0, 1, 2, 3))], fresh=True)

    k_own["z"].wait_recv()
    v_own["z"].wait_recv()
    visit([(0, (4, 5)), (1, (4, 5))])

    k_other["x"].wait_recv()
    k_other["z"].start()
    k_other[1].wait_recv()
    k_other[-1].wait_recv()
    k_edge.start()
    for mate in distant[:2]:
        q_moves[mate].wait_recv()
    turn_queries(2)
    visit([(2, (0, 1, 2)), (2, (3, 4, 5))], fresh=True)

    for step in ("x", 1, -1):
        v_other[step].wait_recv()
    visit([(ring, (6, 7, 8)) for ring in range(3)])
    for mate in distant[2:]:
        q_moves[mate].wait_recv()
    turn_queries(3)
    visit([(3, (0, 1, 2)), (3, (3, 4, 5)), (3, (6, 7, 8))], fresh=True)

    for move in (k_other["z"], v_other["z"], k_edge, v_edge):
        move.wait_recv()

    own_out = pltpu.make_async_copy(ready.at[h], out_ref.at[:, columns(h)], local_sem.at[3])

    def o_copy(ring, other):
        target = head_of(ring, other)
        index = 2 * ring + other
        return remote(
            ready.at[target], out_ref.at[:, columns(h)], o_send.at[index], o_recv.at[index],
            {"tm": t, "head": target},
        )

    o_moves = {mate: o_copy(*mate) for mate in mates}
    def send(ring, done):
        mean = done[:HEAD_DIM] / done[HEAD_DIM:HEAD_DIM + 1]
        turned = mean.T.astype(jnp.bfloat16)
        for b in range(2):
            for g in range(GROUP):
                begin = (b * GROUP + g) * rows
                ready[2 * chunk_of(ring) + b, :, g * HEAD_DIM:(g + 1) * HEAD_DIM] = turned[
                    begin:begin + rows
                ]
        for mate in mates:
            if mate[0] == ring:
                o_moves[mate].start()
        if ring == 0:
            own_out.start()

    visit([(ring, (9, 10)) for ring in (3, 2, 1, 0)], finish=send)

    for moves in (k_own, v_own, k_other, v_other):
        for move in moves.values():
            move.wait_send()
    for move in (k_edge, v_edge, k_pair, v_pair):
        move.wait_send()
    for move in q_moves.values():
        move.wait_send()
    own_out.wait()
    for move in o_moves.values():
        move.wait_recv()
        move.wait_send()


def shards(groups, queries, vis_keys, vis_values, span_start, span_end):
    rows, width = queries.shape
    tokens = vis_keys.shape[0]
    part = width // KV_HEADS
    dma = pltpu.SemaphoreType.DMA
    spans = [span.reshape(1, -1) for span in (span_start, span_end)]
    operands = [queries, vis_keys, vis_values, *spans]
    flops = 4 * rows * width * tokens * SLOTS
    return pl.pallas_call(
        functools.partial(kernel, groups),
        out_shape=pltpu.VMEM((rows, width), jnp.bfloat16),
        in_specs=[pl.BlockSpec(memory_space=pltpu.HBM)] * 5,
        out_specs=pl.BlockSpec(memory_space=pl.ANY),
        scratch_shapes=[
            pltpu.VMEM(spans[0].shape, jnp.int32),
            pltpu.VMEM(spans[1].shape, jnp.int32),
            pltpu.VMEM((KV_HEADS, rows, part), jnp.bfloat16),
            pltpu.VMEM((4, HEAD_DIM, 256), jnp.bfloat16),
            pltpu.VMEM((SLOTS, tokens, HEAD_DIM), jnp.bfloat16),
            pltpu.VMEM((SLOTS, HEAD_DIM, tokens), jnp.bfloat16),
            pltpu.VMEM((tokens, HEAD_DIM), jnp.bfloat16),
            pltpu.VMEM((4, HEAD_DIM + 16, 256), jnp.float32),
            pltpu.VMEM((4, 1, 256), jnp.float32),
            pltpu.VMEM((4, 1, 256), jnp.float32),
            pltpu.VMEM((4, 1, 256), jnp.float32),
            pltpu.VMEM((KV_HEADS, rows, part), jnp.bfloat16),
            dma((6,)),
            dma((8,)),
            dma((8,)),
            dma((10,)),
            dma((10,)),
            dma((10,)),
            dma((10,)),
            dma((8,)),
            dma((8,)),
        ],
        cost_estimate=pl.CostEstimate(
            flops=flops, bytes_accessed=8 * rows * width, transcendentals=flops // 512
        ),
        compiler_params=pltpu.CompilerParams(
            collective_id=0, has_side_effects=True, vmem_limit_bytes=40 * 1024 * 1024
        ),
    )(*[pltpu.with_memory_space_constraint(value, pltpu.HBM) for value in operands])


def solution(mesh):
    return jax.shard_map(
        functools.partial(shards, mesh.shape["tm"]),
        mesh=mesh,
        in_specs=(P(("tm", "head"), None), P("tm", "head"), P("tm", "head"), P("tm"), P("tm")),
        out_specs=P(("tm", "head"), None),
        check_vma=False,
    )
```

```python
import functools
import math

import jax
import jax.numpy as jnp
from jax import lax
from jax.experimental import pallas as pl
from jax.experimental.pallas import tpu as pltpu
from jax.sharding import PartitionSpec as P

HEADS = 64
KV_HEADS = 8
HEAD_DIM = 128
MESH = pl.DeviceIdType.MESH
GROUP = HEADS // KV_HEADS
RATE = math.log2(math.e) / math.sqrt(HEAD_DIM)
FAR = 1e30

OWN = {0: 0, -1: 1, 1: 2, "x": 3, "z": 4}
PAIR = {0: 5, -1: 6, 1: 7, "x": 8, "z": 9}
EDGE, SLOTS = 10, 11


class Move:
    def __init__(self, copies, arrives):
        self.copies, self.arrives = copies, arrives

    def start(self):
        for sends, copy in self.copies:
            pl.when(sends)(copy.start)

    def wait_recv(self):
        pl.when(self.arrives)(self.copies[0][1].wait_recv)

    def wait_send(self):
        for sends, copy in self.copies:
            pl.when(sends)(copy.wait_send)


def kernel(
    groups, q_hbm, k_hbm, v_hbm, first_hbm, last_hbm, out_ref, first_ref, last_ref,
    q_buf, q_turned, k_buf, v_buf, v_rows, total, peak, first, last, ready,
    local_sem, q_send, q_recv, k_send, k_recv, v_send, v_recv, o_send, o_recv,
):
    t = lax.axis_index("tm")
    h = lax.axis_index("head")
    pair, parity = t // 2, t % 2
    side = 1 - 2 * parity
    x, z = pair % 4, pair // 4
    chip, core = h // 2, h % 2
    rows, width = q_buf.shape[1:]
    tokens = k_buf.shape[1]

    opposite_x = {"tm": 8 * z + 2 * ((x + 2) % 4) + parity, "head": h}

    def at_pair(distance):
        return {"tm": (t + groups + 2 * distance) % groups, "head": h}

    def flip(value):
        return value + 1 - 2 * (value % 2)

    def chunk_of(ring):
        start = chip if ring < 2 else (chip + 2) % 4
        return start if ring % 2 == 0 else flip(start)

    def columns(head):
        return pl.ds(pl.multiple_of(head * width, width), width)

    def remote(source, target, send, recv, device):
        return pltpu.make_async_remote_copy(
            source, target, send, recv, device_id=device, device_id_type=MESH
        )

    def head_of(ring, other):
        return 2 * chunk_of(ring) + (core if other == 0 else 1 - core)

    near = [(1, 0), (1, 1), (0, 1)]
    distant = [(2, 0), (2, 1), (3, 0), (3, 1)]
    mates = distant + near

    def q_copy(ring, other):
        target = head_of(ring, other)
        index = 2 * ring + other
        return remote(
            q_hbm.at[:, columns(target)], q_buf.at[h], q_send.at[index], q_recv.at[index],
            {"tm": t, "head": target},
        )

    def k_copy(source, target, role, device):
        return remote(source, target, k_send.at[role], k_recv.at[role], device)

    def v_copy(source, target, role, device):
        return remote(source, target, v_send.at[role], v_recv.at[role], device)

    k_load = pltpu.make_async_copy(k_hbm, k_buf.at[OWN[0]], local_sem.at[0])
    v_load = pltpu.make_async_copy(v_hbm, v_rows, local_sem.at[1])
    q_load = pltpu.make_async_copy(q_hbm.at[:, columns(h)], q_buf.at[h], local_sem.at[2])
    span_loads = [
        pltpu.make_async_copy(first_hbm, first_ref, local_sem.at[4]),
        pltpu.make_async_copy(last_hbm, last_ref, local_sem.at[5]),
    ]
    pairs = groups // 2
    at_start, at_end = z == 0, z == pairs // 4 - 1

    def has(distance):
        return (pair >= -distance) if distance < 0 else (pair < pairs - distance)

    barrier = pltpu.get_barrier_semaphore()
    everywhere = [{"tm": t + side, "head": h}, opposite_x]
    everywhere += [{"tm": t, "head": head_of(*mate)} for mate in mates]
    for partner in everywhere:
        pl.semaphore_signal(barrier, inc=1, device_id=partner, device_id_type=MESH)
    answers = len(everywhere)
    corner = jnp.where(parity == 0, pair == 0, pair == pairs - 1)
    low = x < 2
    to_next, to_last = jnp.logical_not(at_end), jnp.logical_not(at_start)
    beyond = jnp.where(low, to_last, to_next), at_pair(jnp.where(low, -2, 2))
    ahead = jnp.where(parity == 0, has(3), has(-3)), at_pair(3 * side)
    behind = jnp.where(parity == 0, has(-3), has(3)), at_pair(-3 * side)
    others = [(has(distance), at_pair(distance)) for distance in (1, -1, 4, -4)]
    others += [beyond, ahead, behind]
    for present, partner in others:
        answers = answers + jnp.where(present, 1, 0)

        @pl.when(present)
        def _(partner=partner):
            pl.semaphore_signal(barrier, inc=1, device_id=partner, device_id_type=MESH)

    for load in (v_load, k_load, *span_loads, q_load):
        load.start()

    def spread(copy, buf, base, role, source, relayed=True):
        moves = {
            e: Move(
                [(has(e), copy(source, buf.at[base[-e]], role + i, at_pair(e)))],
                has(-e),
            )
            for i, e in enumerate((1, -1))
        }
        moves["x"] = copy(source, buf.at[base["x"]], role + 2, opposite_x)
        if relayed:
            leaves, target, held = jnp.where(low, to_next, to_last), jnp.where(low, 4, -4), "x"
        else:
            leaves, target, held = beyond[0], jnp.where(low, -2, 2), 0
        along = copy(buf.at[base[held]], buf.at[base["z"]], role + 3, at_pair(target))
        moves["z"] = Move([(leaves, along)], beyond[0])
        return moves

    def edge(copy, buf):
        up = parity == 0
        beside = jnp.where(up, PAIR[1], PAIR[-1])
        along = copy(buf.at[beside], buf.at[EDGE], 9, at_pair(4 * side))
        direct = copy(buf.at[PAIR[0]], buf.at[EDGE], 9, at_pair(3 * side))
        return Move(
            [(jnp.where(up, to_next, to_last), along), (corner, direct)],
            jnp.where(up, to_last | (x == 3), to_next | (x == 0)),
        )

    partner = {"tm": t + side, "head": h}
    k_pair = k_copy(k_hbm, k_buf.at[PAIR[0]], 0, partner)
    v_pair = v_copy(v_buf.at[OWN[0]], v_buf.at[PAIR[0]], 0, partner)
    k_own = spread(k_copy, k_buf, OWN, 1, k_hbm)
    v_own = spread(v_copy, v_buf, OWN, 1, v_buf.at[OWN[0]])
    k_other = spread(k_copy, k_buf, PAIR, 5, k_buf.at[PAIR[0]])
    v_other = spread(v_copy, v_buf, PAIR, 5, v_buf.at[PAIR[0]], relayed=False)
    k_edge = edge(k_copy, k_buf)
    v_edge = Move(
        [(ahead[0], v_copy(v_buf.at[PAIR[0]], v_buf.at[EDGE], 9, ahead[1]))], behind[0]
    )
    q_moves = {mate: q_copy(*mate) for mate in mates}

    pl.semaphore_wait(barrier, answers)

    first_steps = (1, -1, "x")
    k_pair.start()
    for step in first_steps:
        k_own[step].start()
    q_moves[0, 1].start()
    v_load.wait()
    v_buf[OWN[0]] = v_rows[...].T
    v_pair.start()
    for step in first_steps:
        v_own[step].start()
    for mate in ((1, 0), (1, 1)):
        q_moves[mate].start()

    def offset(slot):
        places = {"x": jnp.where(low, 2, -2), "z": jnp.where(low, -2, 2)}
        for base, shift in ((OWN, 0), (PAIR, side)):
            for distance, index in base.items():
                if index == slot:
                    return 2 * places.get(distance, distance) + shift
        return -5 * side

    def turn_queries(ring):
        queries = [
            q_buf[2 * chunk_of(ring) + b, :, g * HEAD_DIM:(g + 1) * HEAD_DIM]
            for b in range(2)
            for g in range(GROUP)
        ]
        q_turned[ring] = jnp.concatenate(queries, axis=0).T

    def score(ring, slot):
        return jnp.dot(k_buf[slot], q_turned[ring], preferred_element_type=jnp.float32)

    def visit(units, fresh=False, finish=None):
        scores = [score(units[0][0], slot) for slot in units[0][1]]
        ones = jnp.ones((16, tokens), jnp.bfloat16)
        for at, (ring, slots) in enumerate(units):
            following = units[at + 1] if at + 1 < len(units) else (ring, ())
            renew = fresh and all(ring != earlier for earlier, _ in units[:at])
            begin, end = first[ring], last[ring]
            inside, best = [], []
            for slot, part in zip(slots, scores):
                place = jnp.asarray(offset(slot), jnp.int32).astype(jnp.float32)
                within = (begin <= place) & (place <= end)
                inside.append(within)
                best.append(jnp.where(within, jnp.max(part, axis=0, keepdims=True), -FAR))
            top = functools.reduce(jnp.maximum, best)
            if renew:
                gained = jnp.zeros(total.shape[1:], jnp.float32)
            else:
                before = peak[ring]
                top = jnp.maximum(before, top)
                gained = total[ring] * jnp.exp2((before - top) * RATE)
            ahead = []
            for i, slot in enumerate(slots):
                if i < len(following[1]):
                    ahead.append(score(following[0], following[1][i]))
                level = jnp.where(inside[i], top, FAR)
                weights = jnp.exp2((scores[i] - level) * RATE).astype(jnp.bfloat16)
                left = jnp.concatenate([v_buf[slot], ones], axis=0)
                gained = gained + jnp.dot(left, weights, preferred_element_type=jnp.float32)
            for slot in following[1][len(slots):]:
                ahead.append(score(following[0], slot))
            if finish is None:
                peak[ring] = top
                total[ring] = gained
            else:
                finish(ring, gained)
            scores = ahead

    k_own["x"].wait_recv()
    k_own["z"].start()
    k_pair.wait_recv()
    for step in ("x", 1, -1):
        k_other[step].start()
    for mate in distant[:2]:
        q_moves[mate].start()
    v_own["x"].wait_recv()
    v_own["z"].start()
    v_pair.wait_recv()
    for step in ("x", "z", 1, -1):
        v_other[step].start()
    v_edge.start()
    for mate in distant[2:]:
        q_moves[mate].start()
    unused = [(base[d], jnp.logical_not(has(d))) for base in (OWN, PAIR) for d in (1, -1)]
    unused += [(base["z"], jnp.where(low, at_start, at_end)) for base in (OWN, PAIR)]
    unused.append((EDGE, jnp.logical_not(jnp.where(parity == 0, has(-3), has(3)))))
    for slot, empty in unused:
        @pl.when(empty)
        def _(slot=slot):
            k_buf[slot] = jnp.zeros(k_buf.shape[1:], k_buf.dtype)
            v_buf[slot] = jnp.zeros(v_buf.shape[1:], v_buf.dtype)

    for load in span_loads:
        load.wait()
    lane = lax.broadcasted_iota(jnp.int32, (128, 256), 1)
    row = lax.broadcasted_iota(jnp.int32, (128, 256), 0)
    for ring in range(4):
        wanted = chunk_of(ring) * 32 + (lane // 128) * 16 + lane % 16
        chosen = jnp.where(row == wanted, 1.0, 0.0).astype(jnp.bfloat16)
        for ref, held in ((first_ref, first), (last_ref, last)):
            offset_row = (ref[...] - t).astype(jnp.float32)
            offset_row = jnp.broadcast_to(offset_row, (16, 128)).astype(jnp.bfloat16)
            placed = jnp.dot(offset_row, chosen, preferred_element_type=jnp.float32)
            held[ring] = placed[0:1]

    k_load.wait()
    q_load.wait()
    for step in (1, -1):
        k_own[step].wait_recv()
        v_own[step].wait_recv()
    for mate in near:
        q_moves[mate].wait_recv()
    turn_queries(0)
    turn_queries(1)
    visit([(0, (0, 1, 2, 3)), (1, (0, 1, 2, 3))], fresh=True)

    k_own["z"].wait_recv()
    v_own["z"].wait_recv()
    visit([(0, (4, 5)), (1, (4, 5))])

    k_other["x"].wait_recv()
    k_other["z"].start()
    k_other[1].wait_recv()
    k_other[-1].wait_recv()
    k_edge.start()
    for mate in distant[:2]:
        q_moves[mate].wait_recv()
    turn_queries(2)
    visit([(2, (0, 1, 2)), (2, (3, 4, 5))], fresh=True)

    for mate in distant[2:]:
        q_moves[mate].wait_recv()
    turn_queries(3)
    visit([(3, (0, 1, 2)), (3, (3, 4, 5))], fresh=True)

    for step in ("x", 1, -1):
        v_other[step].wait_recv()
    visit([(ring, (6, 7, 8)) for ring in range(4)])

    for move in (k_other["z"], v_other["z"], k_edge, v_edge):
        move.wait_recv()

    own_out = pltpu.make_async_copy(ready.at[h], out_ref.at[:, columns(h)], local_sem.at[3])

    def o_copy(ring, other):
        target = head_of(ring, other)
        index = 2 * ring + other
        return remote(
            ready.at[target], out_ref.at[:, columns(h)], o_send.at[index], o_recv.at[index],
            {"tm": t, "head": target},
        )

    o_moves = {mate: o_copy(*mate) for mate in mates}
    def send(ring, done):
        mean = done[:HEAD_DIM] / done[HEAD_DIM:HEAD_DIM + 1]
        turned = mean.T.astype(jnp.bfloat16)
        for b in range(2):
            for g in range(GROUP):
                begin = (b * GROUP + g) * rows
                ready[2 * chunk_of(ring) + b, :, g * HEAD_DIM:(g + 1) * HEAD_DIM] = turned[
                    begin:begin + rows
                ]
        for mate in mates:
            if mate[0] == ring:
                o_moves[mate].start()
        if ring == 0:
            own_out.start()

    visit([(ring, (9, 10)) for ring in (3, 2, 1, 0)], finish=send)

    for moves in (k_own, v_own, k_other, v_other):
        for move in moves.values():
            move.wait_send()
    for move in (k_edge, v_edge, k_pair, v_pair):
        move.wait_send()
    for move in q_moves.values():
        move.wait_send()
    own_out.wait()
    for move in o_moves.values():
        move.wait_recv()
        move.wait_send()


def shards(groups, queries, vis_keys, vis_values, span_start, span_end):
    rows, width = queries.shape
    tokens = vis_keys.shape[0]
    part = width // KV_HEADS
    dma = pltpu.SemaphoreType.DMA
    spans = [span.reshape(1, -1) for span in (span_start, span_end)]
    operands = [queries, vis_keys, vis_values, *spans]
    flops = 4 * rows * width * tokens * SLOTS
    return pl.pallas_call(
        functools.partial(kernel, groups),
        out_shape=pltpu.VMEM((rows, width), jnp.bfloat16),
        in_specs=[pl.BlockSpec(memory_space=pltpu.HBM)] * 5,
        out_specs=pl.BlockSpec(memory_space=pl.ANY),
        scratch_shapes=[
            pltpu.VMEM(spans[0].shape, jnp.int32),
            pltpu.VMEM(spans[1].shape, jnp.int32),
            pltpu.VMEM((KV_HEADS, rows, part), jnp.bfloat16),
            pltpu.VMEM((4, HEAD_DIM, 256), jnp.bfloat16),
            pltpu.VMEM((SLOTS, tokens, HEAD_DIM), jnp.bfloat16),
            pltpu.VMEM((SLOTS, HEAD_DIM, tokens), jnp.bfloat16),
            pltpu.VMEM((tokens, HEAD_DIM), jnp.bfloat16),
            pltpu.VMEM((4, HEAD_DIM + 16, 256), jnp.float32),
            pltpu.VMEM((4, 1, 256), jnp.float32),
            pltpu.VMEM((4, 1, 256), jnp.float32),
            pltpu.VMEM((4, 1, 256), jnp.float32),
            pltpu.VMEM((KV_HEADS, rows, part), jnp.bfloat16),
            dma((6,)),
            dma((8,)),
            dma((8,)),
            dma((10,)),
            dma((10,)),
            dma((10,)),
            dma((10,)),
            dma((8,)),
            dma((8,)),
        ],
        cost_estimate=pl.CostEstimate(
            flops=flops, bytes_accessed=8 * rows * width, transcendentals=flops // 512
        ),
        compiler_params=pltpu.CompilerParams(
            collective_id=0, has_side_effects=True, vmem_limit_bytes=40 * 1024 * 1024
        ),
    )(*[pltpu.with_memory_space_constraint(value, pltpu.HBM) for value in operands])


def solution(mesh):
    return jax.shard_map(
        functools.partial(shards, mesh.shape["tm"]),
        mesh=mesh,
        in_specs=(P(("tm", "head"), None), P("tm", "head"), P("tm", "head"), P("tm"), P("tm")),
        out_specs=P(("tm", "head"), None),
        check_vma=False,
    )
```

```python
import functools
import math

import jax
import jax.numpy as jnp
from jax import lax
from jax.experimental import pallas as pl
from jax.experimental.pallas import tpu as pltpu
from jax.sharding import PartitionSpec as P

HEADS = 64
KV_HEADS = 8
HEAD_DIM = 128
MESH = pl.DeviceIdType.MESH
GROUP = HEADS // KV_HEADS
RATE = math.log2(math.e) / math.sqrt(HEAD_DIM)
FAR = 1e30

OWN = {0: 0, -1: 1, 1: 2, "x": 3, "z": 4}
PAIR = {0: 5, -1: 6, 1: 7, "x": 8, "z": 9}
EDGE, SLOTS = 10, 11


class Move:
    def __init__(self, copies, arrives):
        self.copies, self.arrives = copies, arrives

    def start(self):
        for sends, copy in self.copies:
            pl.when(sends)(copy.start)

    def wait_recv(self):
        pl.when(self.arrives)(self.copies[0][1].wait_recv)

    def wait_send(self):
        for sends, copy in self.copies:
            pl.when(sends)(copy.wait_send)


def kernel(
    groups, q_hbm, k_hbm, v_hbm, first_hbm, last_hbm, out_ref, first_ref, last_ref,
    q_buf, q_turned, k_buf, v_buf, v_rows, total, peak, first, last, ready,
    local_sem, q_send, q_recv, k_send, k_recv, v_send, v_recv, o_send, o_recv,
):
    t = lax.axis_index("tm")
    h = lax.axis_index("head")
    pair, parity = t // 2, t % 2
    side = 1 - 2 * parity
    x, z = pair % 4, pair // 4
    chip, core = h // 2, h % 2
    rows, width = q_buf.shape[1:]
    tokens = k_buf.shape[1]

    opposite_x = {"tm": 8 * z + 2 * ((x + 2) % 4) + parity, "head": h}

    def at_pair(distance):
        return {"tm": (t + groups + 2 * distance) % groups, "head": h}

    def flip(value):
        return value + 1 - 2 * (value % 2)

    def chunk_of(ring):
        start = chip if ring < 2 else 3 - chip
        return start if ring % 2 == 0 else flip(start)

    def columns(head):
        return pl.ds(pl.multiple_of(head * width, width), width)

    def remote(source, target, send, recv, device):
        return pltpu.make_async_remote_copy(
            source, target, send, recv, device_id=device, device_id_type=MESH
        )

    def head_of(ring, other):
        return 2 * chunk_of(ring) + (core if other == 0 else 1 - core)

    near = [(1, 0), (1, 1), (0, 1)]
    distant = [(2, 0), (2, 1), (3, 0), (3, 1)]
    mates = distant + near

    def q_copy(ring, other):
        target = head_of(ring, other)
        index = 2 * ring + other
        return remote(
            q_hbm.at[:, columns(target)], q_buf.at[h], q_send.at[index], q_recv.at[index],
            {"tm": t, "head": target},
        )

    def k_copy(source, target, role, device):
        return remote(source, target, k_send.at[role], k_recv.at[role], device)

    def v_copy(source, target, role, device):
        return remote(source, target, v_send.at[role], v_recv.at[role], device)

    k_load = pltpu.make_async_copy(k_hbm, k_buf.at[OWN[0]], local_sem.at[0])
    v_load = pltpu.make_async_copy(v_hbm, v_rows, local_sem.at[1])
    q_load = pltpu.make_async_copy(q_hbm.at[:, columns(h)], q_buf.at[h], local_sem.at[2])
    span_loads = [
        pltpu.make_async_copy(first_hbm, first_ref, local_sem.at[4]),
        pltpu.make_async_copy(last_hbm, last_ref, local_sem.at[5]),
    ]
    pairs = groups // 2
    at_start, at_end = z == 0, z == pairs // 4 - 1

    def has(distance):
        return (pair >= -distance) if distance < 0 else (pair < pairs - distance)

    barrier = pltpu.get_barrier_semaphore()
    everywhere = [{"tm": t + side, "head": h}, opposite_x]
    everywhere += [{"tm": t, "head": head_of(*mate)} for mate in mates]
    for partner in everywhere:
        pl.semaphore_signal(barrier, inc=1, device_id=partner, device_id_type=MESH)
    answers = len(everywhere)
    corner = jnp.where(parity == 0, pair == 0, pair == pairs - 1)
    low = x < 2
    to_next, to_last = jnp.logical_not(at_end), jnp.logical_not(at_start)
    beyond = jnp.where(low, to_last, to_next), at_pair(jnp.where(low, -2, 2))
    ahead = jnp.where(parity == 0, has(3), has(-3)), at_pair(3 * side)
    behind = jnp.where(parity == 0, has(-3), has(3)), at_pair(-3 * side)
    others = [(has(distance), at_pair(distance)) for distance in (1, -1, 4, -4)]
    others += [beyond, ahead, behind]
    for present, partner in others:
        answers = answers + jnp.where(present, 1, 0)

        @pl.when(present)
        def _(partner=partner):
            pl.semaphore_signal(barrier, inc=1, device_id=partner, device_id_type=MESH)

    for load in (v_load, k_load, *span_loads, q_load):
        load.start()

    def spread(copy, buf, base, role, source, relayed=True):
        moves = {
            e: Move(
                [(has(e), copy(source, buf.at[base[-e]], role + i, at_pair(e)))],
                has(-e),
            )
            for i, e in enumerate((1, -1))
        }
        moves["x"] = copy(source, buf.at[base["x"]], role + 2, opposite_x)
        if relayed:
            leaves, target, held = jnp.where(low, to_next, to_last), jnp.where(low, 4, -4), "x"
        else:
            leaves, target, held = beyond[0], jnp.where(low, -2, 2), 0
        along = copy(buf.at[base[held]], buf.at[base["z"]], role + 3, at_pair(target))
        moves["z"] = Move([(leaves, along)], beyond[0])
        return moves

    def edge(copy, buf):
        up = parity == 0
        beside = jnp.where(up, PAIR[1], PAIR[-1])
        along = copy(buf.at[beside], buf.at[EDGE], 9, at_pair(4 * side))
        direct = copy(buf.at[PAIR[0]], buf.at[EDGE], 9, at_pair(3 * side))
        return Move(
            [(jnp.where(up, to_next, to_last), along), (corner, direct)],
            jnp.where(up, to_last | (x == 3), to_next | (x == 0)),
        )

    partner = {"tm": t + side, "head": h}
    k_pair = k_copy(k_hbm, k_buf.at[PAIR[0]], 0, partner)
    v_pair = v_copy(v_buf.at[OWN[0]], v_buf.at[PAIR[0]], 0, partner)
    k_own = spread(k_copy, k_buf, OWN, 1, k_hbm)
    v_own = spread(v_copy, v_buf, OWN, 1, v_buf.at[OWN[0]])
    k_other = spread(k_copy, k_buf, PAIR, 5, k_buf.at[PAIR[0]])
    v_other = spread(v_copy, v_buf, PAIR, 5, v_buf.at[PAIR[0]], relayed=False)
    k_edge = edge(k_copy, k_buf)
    v_edge = Move(
        [(ahead[0], v_copy(v_buf.at[PAIR[0]], v_buf.at[EDGE], 9, ahead[1]))], behind[0]
    )
    q_moves = {mate: q_copy(*mate) for mate in mates}

    pl.semaphore_wait(barrier, answers)

    first_steps = (1, -1, "x")
    k_pair.start()
    for step in first_steps:
        k_own[step].start()
    q_moves[0, 1].start()
    v_load.wait()
    v_buf[OWN[0]] = v_rows[...].T
    v_pair.start()
    for step in first_steps:
        v_own[step].start()
    for mate in ((1, 0), (1, 1)):
        q_moves[mate].start()

    def offset(slot):
        places = {"x": jnp.where(low, 2, -2), "z": jnp.where(low, -2, 2)}
        for base, shift in ((OWN, 0), (PAIR, side)):
            for distance, index in base.items():
                if index == slot:
                    return 2 * places.get(distance, distance) + shift
        return -5 * side

    def turn_queries(ring):
        queries = [
            q_buf[2 * chunk_of(ring) + b, :, g * HEAD_DIM:(g + 1) * HEAD_DIM]
            for b in range(2)
            for g in range(GROUP)
        ]
        q_turned[ring] = jnp.concatenate(queries, axis=0).T

    def score(ring, slot):
        return jnp.dot(k_buf[slot], q_turned[ring], preferred_element_type=jnp.float32)

    def visit(units, fresh=False, finish=None):
        scores = [score(units[0][0], slot) for slot in units[0][1]]
        ones = jnp.ones((16, tokens), jnp.bfloat16)
        for at, (ring, slots) in enumerate(units):
            following = units[at + 1] if at + 1 < len(units) else (ring, ())
            renew = fresh and all(ring != earlier for earlier, _ in units[:at])
            begin, end = first[ring], last[ring]
            inside, best = [], []
            for slot, part in zip(slots, scores):
                place = jnp.asarray(offset(slot), jnp.int32).astype(jnp.float32)
                within = (begin <= place) & (place <= end)
                inside.append(within)
                best.append(jnp.where(within, jnp.max(part, axis=0, keepdims=True), -FAR))
            top = functools.reduce(jnp.maximum, best)
            if renew:
                gained = jnp.zeros(total.shape[1:], jnp.float32)
            else:
                before = peak[ring]
                top = jnp.maximum(before, top)
                gained = total[ring] * jnp.exp2((before - top) * RATE)
            ahead = []
            for i, slot in enumerate(slots):
                if i < len(following[1]):
                    ahead.append(score(following[0], following[1][i]))
                level = jnp.where(inside[i], top, FAR)
                weights = jnp.exp2((scores[i] - level) * RATE).astype(jnp.bfloat16)
                left = jnp.concatenate([v_buf[slot], ones], axis=0)
                gained = gained + jnp.dot(left, weights, preferred_element_type=jnp.float32)
            for slot in following[1][len(slots):]:
                ahead.append(score(following[0], slot))
            if finish is None:
                peak[ring] = top
                total[ring] = gained
            else:
                finish(ring, gained)
            scores = ahead

    k_own["x"].wait_recv()
    k_own["z"].start()
    k_pair.wait_recv()
    for step in ("x", 1, -1):
        k_other[step].start()
    for mate in distant[:2]:
        q_moves[mate].start()
    v_own["x"].wait_recv()
    v_own["z"].start()
    v_pair.wait_recv()
    for step in ("x", "z", 1, -1):
        v_other[step].start()
    v_edge.start()
    for mate in distant[2:]:
        q_moves[mate].start()
    unused = [(base[d], jnp.logical_not(has(d))) for base in (OWN, PAIR) for d in (1, -1)]
    unused += [(base["z"], jnp.where(low, at_start, at_end)) for base in (OWN, PAIR)]
    unused.append((EDGE, jnp.logical_not(jnp.where(parity == 0, has(-3), has(3)))))
    for slot, empty in unused:
        @pl.when(empty)
        def _(slot=slot):
            k_buf[slot] = jnp.zeros(k_buf.shape[1:], k_buf.dtype)
            v_buf[slot] = jnp.zeros(v_buf.shape[1:], v_buf.dtype)

    for load in span_loads:
        load.wait()
    lane = lax.broadcasted_iota(jnp.int32, (128, 256), 1)
    row = lax.broadcasted_iota(jnp.int32, (128, 256), 0)
    for ring in range(4):
        wanted = chunk_of(ring) * 32 + (lane // 128) * 16 + lane % 16
        chosen = jnp.where(row == wanted, 1.0, 0.0).astype(jnp.bfloat16)
        for ref, held in ((first_ref, first), (last_ref, last)):
            offset_row = (ref[...] - t).astype(jnp.float32)
            offset_row = jnp.broadcast_to(offset_row, (16, 128)).astype(jnp.bfloat16)
            placed = jnp.dot(offset_row, chosen, preferred_element_type=jnp.float32)
            held[ring] = placed[0:1]

    k_load.wait()
    q_load.wait()
    for step in (1, -1):
        k_own[step].wait_recv()
        v_own[step].wait_recv()
    for mate in near:
        q_moves[mate].wait_recv()
    turn_queries(0)
    turn_queries(1)
    visit([(0, (0, 1, 2, 3)), (1, (0, 1, 2, 3))], fresh=True)

    k_own["z"].wait_recv()
    v_own["z"].wait_recv()
    visit([(0, (4, 5)), (1, (4, 5))])

    k_other["x"].wait_recv()
    k_other["z"].start()
    k_other[1].wait_recv()
    k_other[-1].wait_recv()
    k_edge.start()
    for mate in distant[:2]:
        q_moves[mate].wait_recv()
    turn_queries(2)
    visit([(2, (0, 1, 2)), (2, (3, 4, 5))], fresh=True)

    for mate in distant[2:]:
        q_moves[mate].wait_recv()
    turn_queries(3)
    visit([(3, (0, 1, 2)), (3, (3, 4, 5))], fresh=True)

    for step in ("x", 1, -1):
        v_other[step].wait_recv()
    visit([(ring, (6, 7, 8)) for ring in range(4)])

    for move in (k_other["z"], v_other["z"], k_edge, v_edge):
        move.wait_recv()

    own_out = pltpu.make_async_copy(ready.at[h], out_ref.at[:, columns(h)], local_sem.at[3])

    def o_copy(ring, other):
        target = head_of(ring, other)
        index = 2 * ring + other
        return remote(
            ready.at[target], out_ref.at[:, columns(h)], o_send.at[index], o_recv.at[index],
            {"tm": t, "head": target},
        )

    o_moves = {mate: o_copy(*mate) for mate in mates}

    def send(ring, done):
        mean = done[:HEAD_DIM] * (1.0 / done[HEAD_DIM:HEAD_DIM + 1])
        turned = mean.T.astype(jnp.bfloat16)
        for b in range(2):
            for g in range(GROUP):
                begin = (b * GROUP + g) * rows
                ready[2 * chunk_of(ring) + b, :, g * HEAD_DIM:(g + 1) * HEAD_DIM] = turned[
                    begin:begin + rows
                ]
        for mate in mates:
            if mate[0] == ring:
                o_moves[mate].start()
        if ring == 0:
            own_out.start()

    visit([(ring, (9, 10)) for ring in (2, 3, 1, 0)], finish=send)

    for moves in (k_own, v_own, k_other, v_other):
        for move in moves.values():
            move.wait_send()
    for move in (k_edge, v_edge, k_pair, v_pair):
        move.wait_send()
    for move in q_moves.values():
        move.wait_send()
    own_out.wait()
    for move in o_moves.values():
        move.wait_recv()
        move.wait_send()


def shards(groups, queries, vis_keys, vis_values, span_start, span_end):
    rows, width = queries.shape
    tokens = vis_keys.shape[0]
    part = width // KV_HEADS
    dma = pltpu.SemaphoreType.DMA
    spans = [span.reshape(1, -1) for span in (span_start, span_end)]
    operands = [queries, vis_keys, vis_values, *spans]
    flops = 4 * rows * width * tokens * SLOTS
    return pl.pallas_call(
        functools.partial(kernel, groups),
        out_shape=pltpu.VMEM((rows, width), jnp.bfloat16),
        in_specs=[pl.BlockSpec(memory_space=pltpu.HBM)] * 5,
        out_specs=pl.BlockSpec(memory_space=pl.ANY),
        scratch_shapes=[
            pltpu.VMEM(spans[0].shape, jnp.int32),
            pltpu.VMEM(spans[1].shape, jnp.int32),
            pltpu.VMEM((KV_HEADS, rows, part), jnp.bfloat16),
            pltpu.VMEM((4, HEAD_DIM, 256), jnp.bfloat16),
            pltpu.VMEM((SLOTS, tokens, HEAD_DIM), jnp.bfloat16),
            pltpu.VMEM((SLOTS, HEAD_DIM, tokens), jnp.bfloat16),
            pltpu.VMEM((tokens, HEAD_DIM), jnp.bfloat16),
            pltpu.VMEM((4, HEAD_DIM + 16, 256), jnp.float32),
            pltpu.VMEM((4, 1, 256), jnp.float32),
            pltpu.VMEM((4, 1, 256), jnp.float32),
            pltpu.VMEM((4, 1, 256), jnp.float32),
            pltpu.VMEM((KV_HEADS, rows, part), jnp.bfloat16),
            dma((6,)),
            dma((8,)),
            dma((8,)),
            dma((10,)),
            dma((10,)),
            dma((10,)),
            dma((10,)),
            dma((8,)),
            dma((8,)),
        ],
        cost_estimate=pl.CostEstimate(
            flops=flops, bytes_accessed=8 * rows * width, transcendentals=flops // 512
        ),
        compiler_params=pltpu.CompilerParams(
            collective_id=0, has_side_effects=True, vmem_limit_bytes=40 * 1024 * 1024
        ),
    )(*[pltpu.with_memory_space_constraint(value, pltpu.HBM) for value in operands])


def solution(mesh):
    return jax.shard_map(
        functools.partial(shards, mesh.shape["tm"]),
        mesh=mesh,
        in_specs=(P(("tm", "head"), None), P("tm", "head"), P("tm", "head"), P("tm"), P("tm")),
        out_specs=P(("tm", "head"), None),
        check_vma=False,
    )
```
